256 devices in a mesh: lon: 64 (over x, z, core), lat: 4 (over y).
Axes of the slice: x: 4, y: 4, z: 8, core: 2. Of those that a mesh axis runs over, the one named last changes fastest.
Arguments:
- guidance: float32 [256, 32768], P('lat', 'lon'), may hold values from -36 to 36, as said below
- cond_lon: float32 [256, 32768], P('lat', 'lon'), may hold values from 0.2 to 5
- cond_lat: float32 [256, 32768], P('lat', 'lon'), may hold values from 0.2 to 5
Outputs:
- solution: float32 [256, 32768], P('lat', 'lon')
- residual: float32 [256, 32768], P('lat', 'lon')
The draws below stay inside these ranges and needn't reach their ends.
Inputs may be any that keep to these rules, and one draw needn't show every extreme that they name: `guidance`: each entry is a product of a random value, a factor of its row and a factor of its column.
All inputs are finite; a program needn't handle non-finite values.
Results may differ from the reference program's by a relative error of at most 0.0003.
Values sent between devices are 32-bit elements; how exact they have to be, the bound alone decides.
A program may use at most 128 MiB of HBM per device.

```python
import math
import jax
import jax.numpy as jnp

SMOOTH = 2
LEVELS = 6
COARSE_SWEEPS = 8
NY = 256
NX = 32768


def draw_guidance(key, part):
    key = jax.random.fold_in(key, 11)
    first, second, third = jax.random.split(key, 3)
    row_scale = jnp.exp(jax.random.uniform(first, (NY, 1), jnp.float32, math.log(0.3), math.log(3.0)))
    col_scale = jnp.exp(jax.random.uniform(second, (1, NX), jnp.float32, math.log(0.3), math.log(3.0)))
    noise = jnp.clip(jax.random.normal(third, (NY, NX), jnp.float32), -4.0, 4.0)
    return (noise * row_scale * col_scale).astype(jnp.float32)


def steps_of(rng, dims, cuts, smallest, high):
    def one(position, parts):
        heights = jax.random.uniform(jax.random.fold_in(jax.random.fold_in(rng, 6), position), (parts,), jnp.float32, smallest / len(cuts), high / len(cuts))
        return jnp.repeat(jnp.exp(heights), dims[position] // parts).reshape((-1,) + (1,) * (len(dims) - position - 1))

    level = one(*cuts[0])
    for cut in cuts[1:]:
        level = level * one(*cut)
    return level


def setup_inputs(seed: int = 0) -> dict:
    arg_keys = jax.random.split(jax.random.key(seed), 4)
    guidance = draw_guidance(jax.random.fold_in(arg_keys[3], 71), 0)
    cond_lon = jnp.clip(jnp.exp(math.log(5.0) - 3.218876 * jax.random.uniform(arg_keys[1], (NY, NX), jnp.float32) ** steps_of(arg_keys[1], (NY, NX), ((0, 4), (1, 64)), -0.2, 0.2)), 0.2, 5.0)
    cond_lat = jnp.clip(jnp.exp(math.log(5.0) - 3.218876 * jax.random.uniform(arg_keys[2], (NY, NX), jnp.float32) ** steps_of(arg_keys[2], (NY, NX), ((0, 4), (1, 64)), -0.2, 0.2)), 0.2, 5.0)
    return {"guidance": guidance, "cond_lon": cond_lon, "cond_lat": cond_lat}


OMEGA = 0.8


def grid_coeffs(east_cond, south_cond):
    west_cond = jnp.roll(east_cond, 1, axis=1)
    north_cond = jnp.concatenate([jnp.zeros_like(south_cond[:1]), south_cond[:-1]], axis=0)
    diagonal = ((east_cond + west_cond) + south_cond) + north_cond
    return west_cond, north_cond, diagonal


def grid_apply(field, east_cond, south_cond, west_cond, north_cond, diagonal):
    east = jnp.roll(field, -1, axis=1)
    west = jnp.roll(field, 1, axis=1)
    south = jnp.concatenate([field[1:], jnp.zeros_like(field[:1])], axis=0)
    north = jnp.concatenate([jnp.zeros_like(field[:1]), field[:-1]], axis=0)
    return (((diagonal * field - east_cond * east) - west_cond * west) - south_cond * south) - north_cond * north


def sweep(field, source, applied, diagonal):
    return field + OMEGA * ((source - applied) / diagonal)


def restrict(values):
    height, breadth = values.shape
    return values.reshape(height // 2, 2, breadth // 2, 2).sum(axis=(1, 3))


def coarsen(east_cond, south_cond):
    return east_cond[0::2, 1::2] + east_cond[1::2, 1::2], south_cond[1::2, 0::2] + south_cond[1::2, 1::2]


def prolong(values):
    return jnp.repeat(jnp.repeat(values, 2, axis=0), 2, axis=1)


def grid_cycle(level_index, source, east_cond, south_cond):
    west_cond, north_cond, diagonal = grid_coeffs(east_cond, south_cond)
    field = jnp.zeros_like(source)
    if level_index == LEVELS:
        for sweep_index in range(COARSE_SWEEPS):
            field = sweep(field, source, grid_apply(field, east_cond, south_cond, west_cond, north_cond, diagonal), diagonal)
        leftover = source - grid_apply(field, east_cond, south_cond, west_cond, north_cond, diagonal)
        return field + jnp.sum(leftover) / jnp.sum(south_cond[-1])
    for sweep_index in range(SMOOTH):
        field = sweep(field, source, grid_apply(field, east_cond, south_cond, west_cond, north_cond, diagonal), diagonal)
    remainder = source - grid_apply(field, east_cond, south_cond, west_cond, north_cond, diagonal)
    coarse_east, coarse_south = coarsen(east_cond, south_cond)
    field = field + prolong(grid_cycle(level_index + 1, restrict(remainder), coarse_east, coarse_south))
    for sweep_index in range(SMOOTH):
        field = sweep(field, source, grid_apply(field, east_cond, south_cond, west_cond, north_cond, diagonal), diagonal)
    return field


def reference(guidance, cond_lon, cond_lat):
    precond = grid_cycle(0, guidance, cond_lon, cond_lat)
    west_cond, north_cond, diagonal = grid_coeffs(cond_lon, cond_lat)
    applied = grid_apply(precond, cond_lon, cond_lat, west_cond, north_cond, diagonal)
    step_size = jnp.sum(guidance * precond) / jnp.sum(precond * applied)
    return step_size * precond, guidance - step_size * applied
```

```python
import jax
import jax.numpy as jnp
from jax import lax
from jax.experimental import pallas as pl
from jax.experimental.pallas import tpu as pltpu
from jax.sharding import PartitionSpec as P

OMEGA = 0.8
COARSE_SWEEPS = 8
NLAT, NLON, BLOCK = 4, 64, 16
ROWS, COLS = 64, 512
H = 16
R0N = ROWS + 2 * H
WIDE = COLS + 128
MESH = pl.DeviceIdType.MESH
F32 = jnp.float32

HALO = ((0, 1), (0, -1), (1, 0), (-1, 0), (1, 1), (1, -1), (-1, 1), (-1, -1))
SPREAD_LAT = (1, 2, 3)
SPREAD_LON = (1, -1, 2, -2)


def lanes(shape):
    return lax.broadcasted_iota(jnp.int32, shape, len(shape) - 1)


def rows_of(shape):
    return lax.broadcasted_iota(jnp.int32, shape, 0)


def roll_l(x, by):
    n = x.shape[1]
    return pltpu.roll(x, by % n, 1)


def up_one(x, after):
    n = x.shape[0]
    t = pltpu.roll(x, n - 1, 0)
    a = pltpu.roll(after, 7, 0)
    tail = jnp.where(rows_of(a.shape) == 7, a, t[n - 8:])
    return tail if n == 8 else jnp.concatenate([t[:n - 8], tail], axis=0)


def down_one(x, carry):
    n = x.shape[0]
    t = pltpu.roll(x, 1, 0)
    head = jnp.where(rows_of(carry.shape) == 0, carry, t[:8])
    out = head if n == 8 else jnp.concatenate([head, t[8:]], axis=0)
    return out, t[:8]


def apply_chunk(v, after, east, south, s, carry):
    fe = east * (v - roll_l(v, -s))
    fs = south * (v - up_one(v, after))
    fn, carry = down_one(fs, carry)
    return ((fe - roll_l(fe, s)) + fs) - fn, carry


def zero8():
    return jnp.zeros((8, WIDE), F32)


def loop(k0, k1, body, carry):
    if k1 - k0 == 1:
        return body(k0, carry)
    return lax.fori_loop(k0, k1, body, carry)


def at(k, ch, n=None):
    n = ch if n is None else n
    if isinstance(k, int):
        return pl.ds(k * ch, n)
    return pl.ds(pl.multiple_of(k * ch, 8), n)


def ld(ref, rows, blocks=range(5)):
    return jnp.concatenate([ref[j, rows, :] for j in blocks], axis=1)


def st(ref, rows, x):
    for j in range(x.shape[1] // 128):
        ref[j, rows, :] = x[:, 128 * j:128 * (j + 1)]


def coeffs(east, south, w, s, n, ch, keep=None, source=None, v=None):
    def body(k, carry):
        e, so = ld(east, at(k, ch)), ld(south, at(k, ch))
        north, carry = down_one(so, carry)
        wk = OMEGA / (((e + roll_l(e, s)) + so) + north)
        if keep is not None:
            r = rows_of(wk.shape) + k * ch
            wk = jnp.where((r >= keep[0]) & (r < keep[1]), wk, 0.0)
        st(w, at(k, ch), wk)
        if v is not None:
            st(v, at(k, ch), wk * ld(source, at(k, ch)))
        return carry

    loop(0, n // ch, body, zero8())


def first_sweep(v, w, source, n, ch):
    def body(k, carry):
        st(v, at(k, ch), ld(w, at(k, ch)) * ld(source, at(k, ch)))
        return carry

    loop(0, n // ch, body, 0)


def sweep(v, source, east, south, w, s, k0, k1, ch):
    def body(k, carry):
        vk = ld(v, at(k, ch))
        after = ld(v, at(k + 1, ch, 8))
        av, carry = apply_chunk(vk, after, ld(east, at(k, ch)), ld(south, at(k, ch)), s, carry)
        wk = ld(w, at(k, ch))
        if source is None:
            st(v, at(k, ch), vk - wk * av)
        else:
            st(v, at(k, ch), vk + wk * (ld(source, at(k, ch)) - av))
        return carry

    loop(k0, k1, body, zero8())


def remainder(r, v, source, east, south, s, n, ch):
    def body(k, carry):
        vk = ld(v, at(k, ch))
        after = ld(v, at(k + 1, ch, 8))
        av, carry = apply_chunk(vk, after, ld(east, at(k, ch)), ld(south, at(k, ch)), s, carry)
        st(r, at(k, ch), ld(source, at(k, ch)) - av)
        return carry

    loop(0, n // ch, body, zero8())


def pair(ref, a, n, odd):
    return ld(ref, pl.ds(2 * a + odd, n, stride=2))


def restrict(r, coarse, n, s):
    for a in range(0, n, 8):
        x = pair(r, a, 8, 0) + pair(r, a, 8, 1)
        st(coarse, pl.ds(a, 8), x + roll_l(x, -s))


def coarsen(east, south, ceast, csouth, n, s):
    for a in range(0, n, 8):
        x = pair(east, a, 8, 0) + pair(east, a, 8, 1)
        st(ceast, pl.ds(a, 8), roll_l(x, -s))
        y = pair(south, a, 8, 1)
        st(csouth, pl.ds(a, 8), y + roll_l(y, -s))


def prolong(coarse, v, n, s, add):
    for a in range(0, n, 8):
        e = ld(coarse, pl.ds(a, 8))
        spread_rows(v, a, jnp.where((lanes(e.shape) & s) == 0, e, roll_l(e, s)), add)


def spread_rows(v, a, e, add):
    for odd in (0, 1):
        where = pl.ds(2 * a + odd, 8, stride=2)
        if add:
            st(v, where, ld(v, where) + e)
        else:
            st(v, where, e)


def pick(x, index):
    return jnp.take_along_axis(x, index, axis=1, mode="promise_in_bounds")


def compact(x, offset):
    l = lanes((8, 128))
    index = (l % 32) * 4 + offset
    out = pick(x[:, 384:512], index)
    for j in (2, 1, 0):
        out = jnp.where(l < 32 * (j + 1), pick(x[:, 128 * j:128 * (j + 1)], index), out)
    return out


def expand(x, base):
    l = lanes((8, 128))
    q = l // 4
    own = x[2, pl.ds(base, 8), :]
    parts = [pick(own, q + 32 * j) for j in range(4)]
    east = pick(x[3, pl.ds(base, 8), :], q)
    west = pick(x[1, pl.ds(base, 8), :], q + 96)
    return jnp.concatenate(parts + [jnp.where(l < 64, east, west)], axis=1)


def kernel(
    b_in, e_in, s_in, sol, res,
    g, pk, re_, rw_, w0, v0, q0, r0, a0, ag,
    e1, s1, f1, w1, v1, q1, r1,
    c, w2, v2, q2, r2, x2, xq2,
    e3, s3, f3, w3, v3, q3, r3,
    e4, s4, f4, w4, v4, q4, r4,
    e5, s5, f5, w5, v5, q5, r5,
    t1, got1, t2, got2,
    in_sem, a_send, a_recv, cs_send, cs_recv, fs_send, fs_recv, c1_send, c1_recv, c2_send, c2_recv,
):
    lat, lon = lax.axis_index("lat"), lax.axis_index("lon")

    def device(dlon, dlat):
        return {"lon": lax.rem(lon + dlon + NLON, NLON), "lat": lax.rem(lat + dlat + NLAT, NLAT)}

    block = (lon // BLOCK) * BLOCK
    inner = lax.rem(lon, BLOCK)

    def mate1(d):
        return {"lon": block + lax.rem(inner + d, BLOCK), "lat": lat}

    def mate2(d):
        return device(BLOCK * (d // 4), d % 4)

    loads = [
        pltpu.make_async_copy(x.at[:, pl.ds(128 * j, 128)], g.at[i, j, pl.ds(H, ROWS)], in_sem.at[i, j])
        for i, x in enumerate((b_in, e_in, s_in))
        for j in range(4)
    ]
    for copy in loads:
        copy.start()

    barrier = pltpu.get_barrier_semaphore()
    greeted = [device(*d) for d in HALO] + [device(0, 2), device(2, 0), device(-2, 0)]
    greeted += [mate1(d) for d in range(1, BLOCK)] + [mate2(d) for d in range(4, 16)]
    for other in greeted:
        pl.semaphore_signal(barrier, inc=1, device_id=other, device_id_type=MESH)

    for v, n in ((v0, R0N), (q0, R0N), (v1, R0N // 2), (q1, R0N // 2), (v2, 64), (q2, 64), (v3, 32), (q3, 32), (v4, 16), (q4, 16), (v5, 8), (q5, 8)):
        st(v, pl.ds(n, 8), zero8())
    for x in (x2, xq2):
        st(x, pl.ds(0, 8), zero8())
        st(x, pl.ds(64, 8), zero8())
    for x in (r5, e5, s5):
        st(x, pl.ds(8, 8), zero8())

    for copy in loads:
        copy.wait()

    l8 = lanes((8, 128))
    for k in range(ROWS // 8):
        rows = slice(H + 8 * k, H + 8 * k + 8)
        first = [g[i, 0, rows] for i in range(3)]
        last = [g[i, 3, rows] for i in range(3)]
        x = jnp.where(l8 < 16, first[0], jnp.where(l8 < 32, roll_l(first[1], 16), roll_l(first[2], 32)))
        y = jnp.where(l8 >= 112, last[0], jnp.where(l8 >= 96, roll_l(last[1], -16), roll_l(last[2], -32)))
        pk[8 * k:8 * k + 8] = jnp.where(l8 < 64, x, y)

    own_rows = pl.ds(pl.multiple_of(lat * 16, 16), 16)

    for a in range(0, 16, 8):
        x = ld(g.at[1], pl.ds(H + 4 * a, 8, stride=4), range(4))
        for j in (1, 2, 3):
            x = x + ld(g.at[1], pl.ds(H + 4 * a + j, 8, stride=4), range(4))
        y = ld(g.at[2], pl.ds(H + 4 * a + 3, 8, stride=4), range(4))
        y = y + roll_l(y, -1)
        y = y + roll_l(y, -2)
        rows = pl.ds(pl.multiple_of(lat * 16 + a, 8), 8)
        c[1, 2, rows, :] = compact(x, 3)
        c[2, 2, rows, :] = compact(y, 0)

    pl.semaphore_wait(barrier, len(greeted))

    def send(src, dst, s_sem, r_sem, k, to):
        copy = pltpu.make_async_remote_copy(
            src_ref=src, dst_ref=dst, send_sem=s_sem.at[k], recv_sem=r_sem.at[k], device_id=to, device_id_type=MESH
        )
        copy.start()
        return copy

    halos = []
    for k, (dlon, dlat) in enumerate(HALO):
        rows_from = {0: (0, ROWS), 1: (ROWS - H, H), -1: (0, H)}[dlat]
        rows_to = {0: H, 1: 0, -1: H + ROWS}[dlat]
        if dlon == 0:
            src = g.at[:, pl.ds(0, 4), pl.ds(H + rows_from[0], rows_from[1])]
            dst = g.at[:, pl.ds(0, 4), pl.ds(rows_to, rows_from[1])]
        else:
            src = pk.at[pl.ds(*rows_from)]
            dst = (rw_ if dlon == 1 else re_).at[pl.ds(rows_to, rows_from[1])]
        halos.append(send(src, dst, a_send, a_recv, k, device(dlon, dlat)))

    def spread_lat(index, s_sem, r_sem):
        part = c.at[index, 2, own_rows]
        return [send(part, part, s_sem, r_sem, k, device(0, d)) for k, d in enumerate(SPREAD_LAT)]

    def spread_lon(index, s_sem, r_sem):
        return [
            send(
                c.at[index, 2], c.at[index, 2 - d],
                s_sem, r_sem, 3 + k, device(d, 0),
            )
            for k, d in enumerate(SPREAD_LON)
        ]

    def receive_lat(copies, index):
        for copy in copies:
            copy.wait_recv()

    conds = spread_lat(pl.ds(1, 2), cs_send, cs_recv)

    for copy in halos:
        copy.wait_recv()
    receive_lat(conds, 1)
    conds_lon = spread_lon(pl.ds(1, 2), cs_send, cs_recv)

    has_north = jnp.where(lat > 0, 1.0, 0.0).astype(F32)
    used = (l8 < 16) | (l8 >= 112)
    for k in range(R0N // 8):
        rows = slice(8 * k, 8 * k + 8)
        x = jnp.where(l8 < 64, re_[rows], rw_[rows])
        for i, other in ((0, 0.0), (1, 1.0), (2, 1.0)):
            y = x if i == 0 else jnp.where(l8 < 64, roll_l(x, -16 * i), roll_l(x, 16 * i))
            g[i, 4, rows, :] = jnp.where(used, y, other)
    g[2, :, 0:H] = g[2, :, 0:H] * has_north

    def bounds(top, own):
        return jnp.where(lat > 0, 0, top), jnp.where(lat < NLAT - 1, 2 * top + own, top + own)

    f0, e0, s0 = g.at[0], g.at[1], g.at[2]
    coeffs(e0, s0, w0, 1, R0N, 16, bounds(H, ROWS), f0, v0)
    sweep(v0, f0, e0, s0, w0, 1, 0, R0N // 16, 16)
    remainder(r0, v0, f0, e0, s0, 1, R0N, 16)
    restrict(r0, f1, R0N // 2, 1)
    coarsen(e0, s0, e1, s1, R0N // 2, 1)
    coeffs(e1, s1, w1, 2, R0N // 2, 16, bounds(H // 2, ROWS // 2), f1, v1)
    sweep(v1, f1, e1, s1, w1, 2, 0, 3, 16)
    remainder(r1, v1, f1, e1, s1, 2, R0N // 2, 16)
    for a in range(0, 16, 8):
        x = ld(r1, pl.ds(8 + 2 * a, 8, stride=2), range(4)) + ld(r1, pl.ds(9 + 2 * a, 8, stride=2), range(4))
        c[0, 2, pl.ds(pl.multiple_of(lat * 16 + a, 8), 8), :] = compact(x + roll_l(x, -2), 0)
    fields = spread_lat(0, fs_send, fs_recv)

    f2, e2, s2 = c.at[0], c.at[1], c.at[2]
    for copy in conds_lon:
        copy.wait_recv()
    coeffs(e2, s2, w2, 1, 64, 16)
    coarsen(e2, s2, e3, s3, 32, 1)
    coeffs(e3, s3, w3, 2, 32, 16)
    coarsen(e3, s3, e4, s4, 16, 2)
    coeffs(e4, s4, w4, 4, 16, 16)
    coarsen(e4, s4, e5, s5, 8, 4)
    coeffs(e5, s5, w5, 8, 8, 8)

    for copy in fields:
        copy.wait_recv()
    fields_lon = spread_lon(0, fs_send, fs_recv)

    st(q5, pl.ds(0, 8), jnp.ones((8, WIDE), F32))
    for _ in range(2):
        sweep(q5, None, e5, s5, w5, 8, 0, 1, 8)
    prolong(q5, q4, 8, 4, False)
    for _ in range(2):
        sweep(q4, None, e4, s4, w4, 4, 0, 1, 16)
    prolong(q4, q3, 16, 2, False)
    for _ in range(2):
        sweep(q3, None, e3, s3, w3, 2, 0, 2, 16)
    prolong(q3, q2, 32, 1, False)
    for _ in range(2):
        sweep(q2, None, e2, s2, w2, 1, 0, 4, 16)

    def to_level1(v, x, fine, add):
        for a in range(0, 64, 8):
            for j in (1, 2, 3):
                x[j, 4 + a:12 + a, :] = v[j, a:a + 8, :]
        for i in range(3):
            spread_rows(fine, 8 * i, expand(x, pl.multiple_of(lat * 16 + 8 * i, 8)), add)

    def finish(v, q, source1, source0, fine):
        for _ in range(2):
            sweep(v, source1, e1, s1, w1, 2, 0, 3, 16)
        prolong(v, fine, R0N // 2, 1, source0 is not None)
        for _ in range(2):
            sweep(fine, source0, e0, s0, w0, 1, 0, R0N // 16, 16)

    def applied(v, out, sums):
        def body(k, carry):
            vk = ld(v, at(k, 8))
            av, edge = apply_chunk(vk, ld(v, at(k + 1, 8)), ld(e0, at(k, 8)), ld(s0, at(k, 8)), 1, carry[0])
            vk, av = vk[:, :COLS], av[:, :COLS]
            rows = at(k - 2, 8)
            out[rows] = av
            more = sums(rows, ld(f0, at(k, 8), range(4)), vk, av)
            return (edge,) + tuple(x + y for x, y in zip(carry[1:], more))

        _, edge = apply_chunk(*[ld(x, pl.ds(*r)) for x, r in ((v, (8, 8)), (v, (16, 8)), (e0, (8, 8)), (s0, (8, 8)))], 1, zero8())
        first = (edge,) + tuple(jnp.zeros((8, COLS), F32) for _ in range(2 if v is q0 else 3))
        return lax.fori_loop(2, 10, body, first)[1:]

    to_level1(q2, xq2, q1, False)
    finish(q1, None, None, None, q0)
    sums_q = applied(q0, ag, lambda rows, b, v, av: (b * v, v * av))

    for copy in fields_lon:
        copy.wait_recv()

    first_sweep(v2, w2, f2, 64, 16)
    sweep(v2, f2, e2, s2, w2, 1, 0, 4, 16)
    remainder(r2, v2, f2, e2, s2, 1, 64, 16)
    restrict(r2, f3, 32, 1)
    first_sweep(v3, w3, f3, 32, 16)
    sweep(v3, f3, e3, s3, w3, 2, 0, 2, 16)
    remainder(r3, v3, f3, e3, s3, 2, 32, 16)
    restrict(r3, f4, 16, 2)
    first_sweep(v4, w4, f4, 16, 16)
    sweep(v4, f4, e4, s4, w4, 4, 0, 1, 16)
    remainder(r4, v4, f4, e4, s4, 4, 16, 16)
    restrict(r4, f5, 8, 4)
    first_sweep(v5, w5, f5, 8, 8)
    sweep(v5, f5, e5, s5, w5, 8, 0, 1, 8)
    remainder(r5, v5, f5, e5, s5, 8, 8, 8)

    x = pair(r5, 0, 8, 0) + pair(r5, 0, 8, 1)
    f6 = x + roll_l(x, -8)
    x = pair(e5, 0, 8, 0) + pair(e5, 0, 8, 1)
    e6 = roll_l(x, -8)
    x = pair(s5, 0, 8, 1)
    s6 = x + roll_l(x, -8)
    row6, lane6 = rows_of((8, WIDE)), lanes((8, WIDE))
    north, _ = down_one(s6, zero8())
    w6 = jnp.where(row6 < 4, OMEGA / (((e6 + roll_l(e6, 16)) + s6) + north), 0.0)
    field = w6 * f6
    for _ in range(COARSE_SWEEPS - 1):
        av, _ = apply_chunk(field, zero8(), e6, s6, 16, zero8())
        field = field + w6 * (f6 - av)
    av, _ = apply_chunk(field, zero8(), e6, s6, 16, zero8())
    left = f6 - av
    mine = ((lane6 & 15) == 0) & (lane6 >= 256) & (lane6 < 384)
    left = jnp.where(mine & (row6 == lat), left, 0.0)[:, 256:384]
    last = jnp.where(mine & (row6 == 3) & (lat == 3), s6, 0.0)[:, 256:384]

    e = jnp.where((lane6 & 8) == 0, field, roll_l(field, 8))
    for odd in (0, 1):
        st(r5, pl.ds(odd, 8, stride=2), e)
    st(v5, pl.ds(0, 8), ld(v5, pl.ds(0, 8)) + ld(r5, pl.ds(0, 8)))
    for _ in range(2):
        sweep(v5, f5, e5, s5, w5, 8, 0, 1, 8)
    prolong(v5, v4, 8, 4, True)
    for _ in range(2):
        sweep(v4, f4, e4, s4, w4, 4, 0, 1, 16)
    prolong(v4, v3, 16, 2, True)
    for _ in range(2):
        sweep(v3, f3, e3, s3, w3, 2, 0, 2, 16)
    prolong(v3, v2, 32, 1, True)
    for _ in range(2):
        sweep(v2, f2, e2, s2, w2, 1, 0, 4, 16)
    to_level1(v2, x2, v1, True)
    finish(v1, None, f1, f0, v0)
    sums_v = applied(v0, a0, lambda rows, b, v, av: (b * v, v * av, v * ag[rows]))

    def fold(x):
        x = (x[:, 0:128] + x[:, 128:256]) + (x[:, 256:384] + x[:, 384:512])
        return x

    seven = [left, last, fold(sums_v[0]), fold(sums_q[0]), fold(sums_v[1]), fold(sums_v[2]), fold(sums_q[1])]
    row = rows_of((8, 128))
    total = jnp.zeros((8, 128), F32)
    for i, x in enumerate(seven):
        total = jnp.where(row == i, jnp.sum(x, axis=0, keepdims=True), total)
    t1[...] = total
    firsts = [send(t1, got1.at[d - 1], c1_send, c1_recv, d - 1, mate1(d)) for d in range(1, 16)]
    for copy in firsts:
        copy.wait_recv()
    for d in range(15):
        total = total + got1[d]
    t2[...] = total
    seconds = [send(t2, got2.at[d - 1], c2_send, c2_recv, d - 1, mate2(d)) for d in range(1, 16)]
    for copy in seconds:
        copy.wait_recv()
    for d in range(15):
        total = total + got2[d]
    for by in (64, 32, 16, 8, 4, 2, 1):
        total = total + pltpu.roll(total, by, 1)
    n_left, n_last, bv, bq, vav, vaq, qaq = [total[i:i + 1] for i in range(7)]
    const = n_left / n_last
    step = (bv + const * bq) / ((vav + (2.0 * const) * vaq) + (const * const) * qaq)
    const = jnp.concatenate([const] * 4, axis=1)
    step = jnp.concatenate([step] * 4, axis=1)
    def final(k, carry):
        rows, there = at(k, 16), pl.ds(pl.multiple_of(H + k * 16, 16), 16)
        sol[rows] = step * (ld(v0, there, range(4)) + const * ld(q0, there, range(4)))
        res[rows] = ld(f0, there, range(4)) - step * (a0[rows] + const * ag[rows])
        return carry

    lax.fori_loop(0, 4, final, 0)
    for copy in halos + conds + conds_lon + fields + fields_lon + firsts + seconds:
        copy.wait_send()


def body(guidance, cond_lon, cond_lat):
    def vm(*shape):
        return pltpu.VMEM(shape, F32)

    def wide(n):
        return vm(5, n, 128)

    def level(n, extra=0):
        return [wide(n + extra), wide(n + extra), wide(n), wide(n), wide(n + 8), wide(n + 8), wide(n + extra)]

    dma = pltpu.SemaphoreType.DMA
    scratch = [vm(3, 5, R0N, 128), vm(ROWS, 128), vm(R0N, 128), vm(R0N, 128)]
    scratch += [wide(R0N), wide(R0N + 8), wide(R0N + 8), wide(R0N), vm(ROWS, COLS), vm(ROWS, COLS)]
    scratch += level(R0N // 2)
    scratch += [vm(3, 5, 64, 128), wide(64), wide(72), wide(72), wide(64), wide(72), wide(72)]
    scratch += level(32) + level(16) + level(8, 8)
    scratch += [vm(8, 128), vm(15, 8, 128), vm(8, 128), vm(15, 8, 128)]
    scratch += [dma((3, 4)), dma((8,)), dma((8,)), dma((7,)), dma((7,)), dma((7,)), dma((7,))] + [dma((15,))] * 4
    return pl.pallas_call(
        kernel,
        out_shape=(jax.ShapeDtypeStruct((ROWS, COLS), F32),) * 2,
        in_specs=[pl.BlockSpec(memory_space=pl.ANY)] * 3,
        out_specs=(pl.BlockSpec(memory_space=pltpu.VMEM),) * 2,
        scratch_shapes=scratch,
        compiler_params=pltpu.CompilerParams(
            collective_id=0, has_side_effects=True, vmem_limit_bytes=40 * 1024 * 1024
        ),
        cost_estimate=pl.CostEstimate(flops=10_000_000, bytes_accessed=655360, transcendentals=0),
    )(guidance, cond_lon, cond_lat)


def solution(mesh):
    spec = P("lat", "lon")
    return jax.shard_map(body, mesh=mesh, in_specs=(spec,) * 3, out_specs=(spec,) * 2, check_vma=False)
```

```python
import jax
import jax.numpy as jnp
from jax import lax
from jax.experimental import pallas as pl
from jax.experimental.pallas import tpu as pltpu
from jax.sharding import PartitionSpec as P

OMEGA = 0.8
COARSE_SWEEPS = 8
NLAT, NLON, BLOCK = 4, 64, 16
ROWS, COLS = 64, 512
H = 16
PAD = 8
PAD2 = 16
N0 = ROWS + 2 * H
WIDE = COLS + 128
ALL = range(5)
MID = range(1, 4)
MESH = pl.DeviceIdType.MESH
F32 = jnp.float32

HALO = ((0, 1), (0, -1), (1, 0), (-1, 0), (1, 1), (1, -1), (-1, 1), (-1, -1))
SPREAD_LAT = (1, 2, 3)
SPREAD_LON = (1, -1, 2, -2)


def lanes(shape):
    return lax.broadcasted_iota(jnp.int32, shape, len(shape) - 1)


def rows_of(shape):
    return lax.broadcasted_iota(jnp.int32, shape, 0)


def roll_l(x, by):
    return pltpu.roll(x, by % x.shape[1], 1)


def ld(ref, start, n, blocks=ALL, stride=None):
    rows = pl.ds(start, n) if stride is None else pl.ds(start, n, stride=stride)
    return jnp.concatenate([ref[j, rows, :] for j in blocks], axis=1)


def st(ref, start, x, blocks=ALL, stride=None):
    n = x.shape[0]
    rows = pl.ds(start, n) if stride is None else pl.ds(start, n, stride=stride)
    for i, j in enumerate(blocks):
        ref[j, rows, :] = x[:, 128 * i:128 * (i + 1)]


def loop(r0, count, ch, body):
    if count == ch:
        body(r0)
    else:

        def step(k, carry):
            body(pl.multiple_of(r0 + k * ch, 8))
            return carry

        lax.fori_loop(0, count // ch, step, 0)


class Level:
    def __init__(self, s, pad, n, f, e, so, west, ae, aw, as_, an, w, wf, v, v2, q, r=None):
        self.s, self.pad, self.n = s, pad, n
        self.f, self.e, self.so, self.west = f, e, so, west
        self.ae, self.aw, self.as_, self.an, self.w, self.wf = ae, aw, as_, an, w, wf
        self.v, self.v2, self.q, self.r = v, v2, q, v2 if r is None else r


def coeffs(l, ch, keep=None, source=False):
    def body(r):
        p = l.pad + r
        e, so, no = ld(l.e, p, ch), ld(l.so, p, ch), ld(l.so, p - 1, ch)
        we = roll_l(e, l.s)
        wk = OMEGA / (((e + we) + so) + no)
        if keep is not None:
            row = rows_of(wk.shape) + r
            wk = jnp.where((row >= keep[0]) & (row < keep[1]), wk, 0.0)
        st(l.west, p, we)
        st(l.ae, p, wk * e)
        st(l.aw, p, wk * we)
        st(l.as_, p, wk * so)
        st(l.an, p, wk * no)
        if source:
            st(l.wf, p, wk * ld(l.f, p, ch))
        else:
            st(l.w, p, wk)

    loop(0, l.n, ch, body)


def sweep(l, src, dst, source, r0, count, ch, blocks=ALL):
    def body(r):
        p = l.pad + r
        v = ld(src, p, ch, blocks)
        x = ld(l.ae, p, ch, blocks) * roll_l(v, -l.s) + ld(l.aw, p, ch, blocks) * roll_l(v, l.s)
        y = ld(l.as_, p, ch, blocks) * ld(src, p + 1, ch, blocks) + ld(l.an, p, ch, blocks) * ld(src, p - 1, ch, blocks)
        z = (1.0 - OMEGA) * v
        if source:
            z = z + ld(l.wf, p, ch, blocks)
        st(dst, p, (y + z) + x, blocks)

    loop(r0, count, ch, body)


def operator(l, v, p, ch):
    x = ld(v, p, ch)
    lon = ld(l.e, p, ch) * (x - roll_l(x, -l.s)) + ld(l.west, p, ch) * (x - roll_l(x, l.s))
    lat = ld(l.so, p, ch) * (x - ld(v, p + 1, ch)) + ld(l.so, p - 1, ch) * (x - ld(v, p - 1, ch))
    return x, lat + lon


def remainder(l, ch):
    def body(r):
        p = l.pad + r
        st(l.r, p, ld(l.f, p, ch) - operator(l, l.v, p, ch)[1])

    loop(0, l.n, ch, body)


def pair(ref, start, n, odd, blocks=ALL):
    return ld(ref, start + odd, n, blocks, 2)


def restrict(l, c):
    ch = min(16, c.n)

    def body(a):
        x = pair(l.r, l.pad + 2 * a, ch, 0) + pair(l.r, l.pad + 2 * a, ch, 1)
        x = x + roll_l(x, -l.s)
        st(c.f, c.pad + a, x)
        st(c.wf, c.pad + a, x * ld(c.w, c.pad + a, ch))

    for a in range(0, c.n, ch):
        body(a)


def coarsen(l, c):
    ch = min(16, c.n)
    for a in range(0, c.n, ch):
        x = pair(l.e, l.pad + 2 * a, ch, 0) + pair(l.e, l.pad + 2 * a, ch, 1)
        st(c.e, c.pad + a, roll_l(x, -l.s))
        y = pair(l.so, l.pad + 2 * a, ch, 1)
        st(c.so, c.pad + a, y + roll_l(y, -l.s))


def spread_rows(v, start, e, add, blocks=ALL):
    for odd in (0, 1):
        x = e
        if add:
            x = x + ld(v, start + odd, e.shape[0], blocks, 2)
        st(v, start + odd, x, blocks, 2)


def prolong(c, l, src, dst, a0, n, add, blocks=ALL):
    for a in range(0, n, 8):
        e = ld(src, c.pad + a0 + a, 8, blocks)
        e = jnp.where((lanes(e.shape) & l.s) == 0, e, roll_l(e, l.s))
        spread_rows(dst, l.pad + 2 * (a0 + a), e, add, blocks)


def pick(x, index):
    return jnp.take_along_axis(x, index, axis=1, mode="promise_in_bounds")


def compact(x, offset):
    l = lanes((8, 128))
    index = (l % 32) * 4 + offset
    out = pick(x[:, 384:512], index)
    for j in (2, 1, 0):
        out = jnp.where(l < 32 * (j + 1), pick(x[:, 128 * j:128 * (j + 1)], index), out)
    return out


def expand(x, base):
    l = lanes((8, 128))
    q = l // 4
    own = x[2, pl.ds(base, 8), :]
    parts = [pick(own, q + 32 * j) for j in range(4)]
    east = pick(x[3, pl.ds(base, 8), :], q)
    west = pick(x[1, pl.ds(base, 8), :], q + 96)
    return jnp.concatenate(parts + [jnp.where(l < 64, east, west)], axis=1)


def kernel(
    b_in, e_in, s_in, out_v, out_q, out_a,
    g, pk, re_, rw_, a0, ag, c, t1, got1, t2, got2,
    *rest,
):
    fine0, fine1, fine2, fine3, fine4, fine5 = rest[:9], rest[9:22], rest[22:32], rest[32:45], rest[45:58], rest[58:72]
    in_sem, a_send, a_recv, cs_send, cs_recv, fs_send, fs_recv, c1_send, c1_recv, c2_send, c2_recv = rest[72:]

    l0 = Level(1, PAD, N0, g.at[0], g.at[1], g.at[2], *fine0[:5], None, *fine0[5:])
    l1 = Level(2, PAD, N0 // 2, *fine1)
    l2 = Level(1, PAD2, 64, c.at[0], c.at[1], c.at[2], *fine2)
    l3 = Level(2, PAD, 32, *fine3)
    l4 = Level(4, PAD, 16, *fine4)
    l5 = Level(8, PAD, 8, *fine5)
    lat, lon = lax.axis_index("lat"), lax.axis_index("lon")

    def device(dlon, dlat):
        return {"lon": lax.rem(lon + dlon + NLON, NLON), "lat": lax.rem(lat + dlat + NLAT, NLAT)}

    block = (lon // BLOCK) * BLOCK
    inner = lax.rem(lon, BLOCK)

    def mate1(d):
        return {"lon": block + lax.rem(inner + d, BLOCK), "lat": lat}

    def mate2(d):
        return device(BLOCK * (d // 4), d % 4)

    top = PAD + H
    loads = [
        pltpu.make_async_copy(x.at[:, pl.ds(128 * j, 128)], g.at[i, j, pl.ds(top, ROWS)], in_sem.at[i, j])
        for i, x in enumerate((b_in, e_in, s_in))
        for j in range(4)
    ]
    for copy in loads:
        copy.start()

    barrier = pltpu.get_barrier_semaphore()
    greeted = [device(*d) for d in HALO] + [device(0, 2), device(2, 0), device(-2, 0)]
    greeted += [mate1(d) for d in range(1, BLOCK)] + [mate2(d) for d in range(4, 16)]
    for other in greeted:
        pl.semaphore_signal(barrier, inc=1, device_id=other, device_id_type=MESH)

    def clear(ref, l):
        zero = jnp.zeros((l.pad, WIDE), F32)
        st(ref, 0, zero)
        st(ref, l.pad + l.n, zero)

    for l in (l0, l1):
        for ref in (l.wf, l.v, l.v2, l.q):
            clear(ref, l)
    for l in (l2, l3, l4, l5):
        for ref in (l.wf, l.v, l.v2, l.q, l.so):
            clear(ref, l)
    for ref in (l2.ae, l2.aw, l2.as_, l2.an):
        clear(ref, l2)
    for ref in (l5.e, l5.r):
        clear(ref, l5)

    for copy in loads:
        copy.wait()

    l8 = lanes((8, 128))
    for k in range(ROWS // 8):
        rows = slice(top + 8 * k, top + 8 * k + 8)
        first = [g[i, 0, rows] for i in range(3)]
        last = [g[i, 3, rows] for i in range(3)]
        x = jnp.where(l8 < 16, first[0], jnp.where(l8 < 32, roll_l(first[1], 16), roll_l(first[2], 32)))
        y = jnp.where(l8 >= 112, last[0], jnp.where(l8 >= 96, roll_l(last[1], -16), roll_l(last[2], -32)))
        pk[8 * k:8 * k + 8] = jnp.where(l8 < 64, x, y)

    own_rows = pl.ds(pl.multiple_of(PAD2 + lat * 16, 16), 16)

    for a in range(0, 16, 8):
        x = ld(g.at[1], top + 4 * a, 8, range(4), 4)
        for j in (1, 2, 3):
            x = x + ld(g.at[1], top + 4 * a + j, 8, range(4), 4)
        y = ld(g.at[2], top + 4 * a + 3, 8, range(4), 4)
        y = y + roll_l(y, -1)
        y = y + roll_l(y, -2)
        rows = pl.ds(pl.multiple_of(PAD2 + lat * 16 + a, 8), 8)
        c[1, 2, rows, :] = compact(x, 3)
        c[2, 2, rows, :] = compact(y, 0)

    pl.semaphore_wait(barrier, len(greeted))

    def send(src, dst, s_sem, r_sem, k, to):
        copy = pltpu.make_async_remote_copy(
            src_ref=src, dst_ref=dst, send_sem=s_sem.at[k], recv_sem=r_sem.at[k], device_id=to, device_id_type=MESH
        )
        copy.start()
        return copy

    halos = []
    for k, (dlon, dlat) in enumerate(HALO):
        first_row, count = {0: (0, ROWS), 1: (ROWS - H, H), -1: (0, H)}[dlat]
        to = {0: H, 1: 0, -1: H + ROWS}[dlat]
        if dlon == 0:
            src = g.at[:, pl.ds(0, 4), pl.ds(top + first_row, count)]
            dst = g.at[:, pl.ds(0, 4), pl.ds(PAD + to, count)]
        else:
            src = pk.at[pl.ds(first_row, count)]
            dst = (rw_ if dlon == 1 else re_).at[pl.ds(to, count)]
        halos.append(send(src, dst, a_send, a_recv, k, device(dlon, dlat)))

    def spread_lat(index, s_sem, r_sem):
        part = c.at[index, 2, own_rows]
        return [send(part, part, s_sem, r_sem, k, device(0, d)) for k, d in enumerate(SPREAD_LAT)]

    def spread_lon(index, s_sem, r_sem):
        rows = pl.ds(PAD2, 64)
        return [
            send(c.at[index, 2, rows], c.at[index, 2 - d, rows], s_sem, r_sem, 3 + k, device(d, 0))
            for k, d in enumerate(SPREAD_LON)
        ]

    conds = spread_lat(pl.ds(1, 2), cs_send, cs_recv)

    for copy in halos:
        copy.wait_recv()
    for copy in conds:
        copy.wait_recv()
    conds_lon = spread_lon(pl.ds(1, 2), cs_send, cs_recv)

    has_north = jnp.where(lat > 0, 1.0, 0.0).astype(F32)
    used = (l8 < 16) | (l8 >= 112)
    for k in range(N0 // 8):
        x = jnp.where(l8 < 64, re_[8 * k:8 * k + 8], rw_[8 * k:8 * k + 8])
        for i, other in ((0, 0.0), (1, 1.0), (2, 1.0)):
            y = x if i == 0 else jnp.where(l8 < 64, roll_l(x, -16 * i), roll_l(x, 16 * i))
            g[i, 4, PAD + 8 * k:PAD + 8 * k + 8, :] = jnp.where(used, y, other)
    g[2, :, PAD:PAD + H] = g[2, :, PAD:PAD + H] * has_north

    def bounds(halo, own):
        return jnp.where(lat > 0, 0, halo), jnp.where(lat < NLAT - 1, 2 * halo + own, halo + own)

    coeffs(l0, 32, bounds(H, ROWS), True)
    sweep(l0, l0.wf, l0.v, True, 0, N0, 32)
    coarsen(l0, l1)
    remainder(l0, 32)
    coeffs(l1, 24, bounds(H // 2, ROWS // 2))
    restrict(l0, l1)
    sweep(l1, l1.wf, l1.v, True, 0, 48, 48)
    remainder(l1, 48)
    for a in range(0, 16, 8):
        x = ld(l1.r, PAD + 8 + 2 * a, 8, range(4), 2) + ld(l1.r, PAD + 9 + 2 * a, 8, range(4), 2)
        rows = pl.ds(pl.multiple_of(PAD2 + lat * 16 + a, 8), 8)
        c[0, 2, rows, :] = compact(x + roll_l(x, -2), 0)
    fields = spread_lat(0, fs_send, fs_recv)

    for copy in conds_lon:
        copy.wait_recv()
    coeffs(l2, 32)
    coarsen(l2, l3)
    coeffs(l3, 32)
    coarsen(l3, l4)
    coeffs(l4, 16)
    coarsen(l4, l5)
    coeffs(l5, 8)

    for copy in fields:
        copy.wait_recv()
    fields_lon = spread_lon(0, fs_send, fs_recv)

    def twice(l, v, source, r0, count, ch, blocks=ALL):
        sweep(l, v, l.v2, source, r0, count, ch, blocks)
        sweep(l, l.v2, v, source, r0, count, ch, blocks)

    def rise(name, source):
        u = [getattr(l, name) for l in (l0, l1, l2, l3, l4, l5)]
        twice(l5, u[5], source, 0, 8, 8, MID)
        prolong(l5, l4, u[5], u[4], 0, 8, source, MID)
        twice(l4, u[4], source, 0, 16, 16, MID)
        prolong(l4, l3, u[4], u[3], 0, 16, source, MID)
        twice(l3, u[3], source, 0, 32, 32, MID)
        near = lat * 8 - 4
        prolong(l3, l2, u[3], u[2], near, 16, source, MID)
        near = pl.multiple_of(lat * 16 - 8, 8)
        twice(l2, u[2], source, near, 32, 32, MID)
        for i in range(3):
            e = expand(u[2], PAD2 + lat * 16 - 4 + 8 * i)
            spread_rows(u[1], PAD + 16 * i, e, source)
        twice(l1, u[1], source, 0, 48, 48)
        prolong(l1, l0, u[1], u[0], 0, 48, source)
        twice(l0, u[0], source, 8, 80, 40)

    def applied(v, out, sums, n):
        def body(k, carry):
            r = pl.multiple_of(k * 16, 16)
            x, av = operator(l0, v, top + r, 16)
            x, av = x[:, :COLS], av[:, :COLS]
            out[pl.ds(r, 16)] = av
            more = sums(pl.ds(r, 16), ld(l0.f, top + r, 16, range(4)), x, av)
            return tuple(y + (z[:8] + z[8:]) for y, z in zip(carry, more))

        return lax.fori_loop(0, ROWS // 16, body, (jnp.zeros((8, COLS), F32),) * n)

    st(l5.q, PAD, jnp.ones((8, WIDE), F32))
    rise("q", False)
    sums_q = applied(l0.q, ag, lambda rows, b, v, av: (b * v, v * av), 2)

    for copy in fields_lon:
        copy.wait_recv()

    def first(r):
        st(l2.wf, PAD2 + r, ld(l2.w, PAD2 + r, 32) * ld(l2.f, PAD2 + r, 32))

    loop(0, 64, 32, first)
    sweep(l2, l2.wf, l2.v, True, 0, 64, 32)
    remainder(l2, 32)
    for l, coarse in ((l2, l3), (l3, l4), (l4, l5)):
        restrict(l, coarse)
        sweep(coarse, coarse.wf, coarse.v, True, 0, coarse.n, coarse.n)
        remainder(coarse, coarse.n)

    x = pair(l5.r, PAD, 8, 0) + pair(l5.r, PAD, 8, 1)
    f6 = x + roll_l(x, -8)
    x = pair(l5.e, PAD, 8, 0) + pair(l5.e, PAD, 8, 1)
    e6 = roll_l(x, -8)
    x = pair(l5.so, PAD, 8, 1)
    s6 = x + roll_l(x, -8)
    row6, lane6 = rows_of((8, WIDE)), lanes((8, WIDE))
    west6 = roll_l(e6, 16)
    north6 = jnp.where(row6 == 0, 0.0, pltpu.roll(s6, 1, 0))
    w6 = jnp.where(row6 < 4, OMEGA / (((e6 + west6) + s6) + north6), 0.0)
    ae6, aw6, as6, an6, wf6 = w6 * e6, w6 * west6, w6 * s6, w6 * north6, w6 * f6
    field = wf6
    for _ in range(COARSE_SWEEPS - 1):
        x = ae6 * roll_l(field, -16) + aw6 * roll_l(field, 16)
        y = as6 * pltpu.roll(field, 7, 0) + an6 * pltpu.roll(field, 1, 0)
        field = (((1.0 - OMEGA) * field + wf6) + y) + x
    lon6 = e6 * (field - roll_l(field, -16)) + west6 * (field - roll_l(field, 16))
    lat6 = s6 * (field - pltpu.roll(field, 7, 0)) + north6 * (field - pltpu.roll(field, 1, 0))
    left = f6 - (lon6 + lat6)
    mine = ((lane6 & 15) == 0) & (lane6 >= 256) & (lane6 < 384)
    left = jnp.where(mine & (row6 == lat), left, 0.0)[:, 256:384]
    last = jnp.where(mine & (row6 == 3) & (lat == 3), s6, 0.0)[:, 256:384]

    e = jnp.where((lane6 & 8) == 0, field, roll_l(field, 8))
    for odd in (0, 1):
        st(l5.r, odd, e, ALL, 2)
    st(l5.v, PAD, ld(l5.v, PAD, 8) + ld(l5.r, 0, 8))
    rise("v", True)
    sums_v = applied(l0.v, a0, lambda rows, b, v, av: (b * v, v * av, v * ag[rows]), 3)

    def fold(x):
        return (x[:, 0:128] + x[:, 128:256]) + (x[:, 256:384] + x[:, 384:512])

    seven = [left, last, fold(sums_v[0]), fold(sums_q[0]), fold(sums_v[1]), fold(sums_v[2]), fold(sums_q[1])]
    row = rows_of((8, 128))
    total = jnp.zeros((8, 128), F32)
    for i, x in enumerate(seven):
        total = jnp.where(row == i, jnp.sum(x, axis=0, keepdims=True), total)
    t1[...] = total
    firsts = [send(t1, got1.at[d - 1], c1_send, c1_recv, d - 1, mate1(d)) for d in range(1, 16)]
    for copy in firsts:
        copy.wait_recv()

    def gathered(total, got):
        parts = [total] + [got[d] for d in range(15)]
        while len(parts) > 1:
            parts = [x + y for x, y in zip(parts[::2], parts[1::2])]
        return parts[0]

    total = gathered(total, got1)
    t2[...] = total
    seconds = [send(t2, got2.at[d - 1], c2_send, c2_recv, d - 1, mate2(d)) for d in range(1, 16)]
    for copy in seconds:
        copy.wait_recv()
    total = gathered(total, got2)
    for by in (64, 32, 16, 8, 4, 2, 1):
        total = total + pltpu.roll(total, by, 1)
    n_left, n_last, bv, bq, vav, vaq, qaq = [total[i:i + 1] for i in range(7)]
    const = n_left / n_last
    step = (bv + const * bq) / ((vav + (2.0 * const) * vaq) + (const * const) * qaq)
    both = jnp.concatenate([step * const] * 4, axis=1)
    step = jnp.concatenate([step] * 4, axis=1)

    def final(k, carry):
        r = pl.multiple_of(k * 16, 16)
        rows = pl.ds(r, 16)
        out_v[rows] = step * ld(l0.v, top + r, 16, range(4))
        out_q[rows] = both * ld(l0.q, top + r, 16, range(4))
        out_a[rows] = step * a0[rows] + both * ag[rows]
        return carry

    lax.fori_loop(0, 4, final, 0)
    for copy in halos + conds + conds_lon + fields + fields_lon + firsts + seconds:
        copy.wait_send()


def body(guidance, cond_lon, cond_lat):
    def vm(*shape):
        return pltpu.VMEM(shape, F32)

    def wide(n, count):
        return [vm(5, n, 128)] * count

    dma = pltpu.SemaphoreType.DMA
    scratch = [vm(3, 5, N0 + 2 * PAD, 128), vm(ROWS, 128), vm(N0, 128), vm(N0, 128), vm(ROWS, COLS), vm(ROWS, COLS)]
    scratch += [vm(3, 5, 64 + 2 * PAD2, 128), vm(8, 128), vm(15, 8, 128), vm(8, 128), vm(15, 8, 128)]
    scratch += wide(N0 + 2 * PAD, 9) + wide(N0 // 2 + 2 * PAD, 13) + wide(64 + 2 * PAD2, 10)
    scratch += wide(32 + 2 * PAD, 13) + wide(16 + 2 * PAD, 13) + wide(8 + 2 * PAD, 14)
    scratch += [dma((3, 4)), dma((8,)), dma((8,)), dma((7,)), dma((7,)), dma((7,)), dma((7,))] + [dma((15,))] * 4
    v, q, a = pl.pallas_call(
        kernel,
        out_shape=(jax.ShapeDtypeStruct((ROWS, COLS), F32),) * 3,
        in_specs=[pl.BlockSpec(memory_space=pltpu.HBM)] * 3,
        out_specs=(pl.BlockSpec(memory_space=pltpu.VMEM),) * 3,
        scratch_shapes=scratch,
        compiler_params=pltpu.CompilerParams(
            collective_id=0, has_side_effects=True, vmem_limit_bytes=40 * 1024 * 1024
        ),
        cost_estimate=pl.CostEstimate(flops=10_000_000, bytes_accessed=655360, transcendentals=0),
    )(guidance, cond_lon, cond_lat)
    return v + q, guidance - a


def solution(mesh):
    spec = P("lat", "lon")
    return jax.shard_map(body, mesh=mesh, in_specs=(spec,) * 3, out_specs=(spec,) * 2, check_vma=False)
```

```python
import jax
import jax.numpy as jnp
from jax import lax
from jax.experimental import pallas as pl
from jax.experimental.pallas import tpu as pltpu
from jax.sharding import PartitionSpec as P

OMEGA = 0.8
COARSE_SWEEPS = 8
NLAT, NLON, BLOCK = 4, 64, 16
ROWS, COLS = 64, 512
H = 16
PAD = 8
PAD2 = 16
N0 = ROWS + 2 * H
WIDE = COLS + 128
ALL = range(5)
MID = range(1, 4)
MESH = pl.DeviceIdType.MESH
F32 = jnp.float32

HALO = ((0, 1), (0, -1), (1, 0), (-1, 0), (1, 1), (1, -1), (-1, 1), (-1, -1))
SPREAD_LAT = (1, 2, 3)
SPREAD_LON = (1, -1, 2, -2)


def lanes(shape):
    return lax.broadcasted_iota(jnp.int32, shape, len(shape) - 1)


def rows_of(shape):
    return lax.broadcasted_iota(jnp.int32, shape, 0)


def roll_l(x, by):
    return pltpu.roll(x, by % x.shape[1], 1)


def ld(ref, start, n, blocks=ALL, stride=None):
    rows = pl.ds(start, n) if stride is None else pl.ds(start, n, stride=stride)
    return jnp.concatenate([ref[j, rows, :] for j in blocks], axis=1)


def st(ref, start, x, blocks=ALL, stride=None):
    n = x.shape[0]
    rows = pl.ds(start, n) if stride is None else pl.ds(start, n, stride=stride)
    for i, j in enumerate(blocks):
        ref[j, rows, :] = x[:, 128 * i:128 * (i + 1)]


def loop(r0, count, ch, body):
    if count == ch:
        body(r0)
    else:

        def step(k, carry):
            body(pl.multiple_of(r0 + k * ch, 8))
            return carry

        lax.fori_loop(0, count // ch, step, 0)


class Level:
    def __init__(self, s, pad, n, f, e, so, west, ae, aw, as_, an, w, wf, v, v2, q, r=None):
        self.s, self.pad, self.n = s, pad, n
        self.f, self.e, self.so, self.west = f, e, so, west
        self.ae, self.aw, self.as_, self.an, self.w, self.wf = ae, aw, as_, an, w, wf
        self.v, self.v2, self.q, self.r = v, v2, q, v2 if r is None else r


def coeffs(l, ch, keep=None, source=False):
    def body(r):
        p = l.pad + r
        e, so, no = ld(l.e, p, ch), ld(l.so, p, ch), ld(l.so, p - 1, ch)
        we = roll_l(e, l.s)
        wk = OMEGA / (((e + we) + so) + no)
        if keep is not None:
            row = rows_of(wk.shape) + r
            wk = jnp.where((row >= keep[0]) & (row < keep[1]), wk, 0.0)
        st(l.west, p, we)
        st(l.ae, p, wk * e)
        st(l.aw, p, wk * we)
        st(l.as_, p, wk * so)
        st(l.an, p, wk * no)
        if source:
            st(l.wf, p, wk * ld(l.f, p, ch))
        else:
            st(l.w, p, wk)

    loop(0, l.n, ch, body)


def sweep(l, src, dst, source, r0, count, ch, blocks=ALL):
    def body(r):
        p = l.pad + r
        v = ld(src, p, ch, blocks)
        x = ld(l.ae, p, ch, blocks) * roll_l(v, -l.s) + ld(l.aw, p, ch, blocks) * roll_l(v, l.s)
        y = ld(l.as_, p, ch, blocks) * ld(src, p + 1, ch, blocks) + ld(l.an, p, ch, blocks) * ld(src, p - 1, ch, blocks)
        z = (1.0 - OMEGA) * v
        if source:
            z = z + ld(l.wf, p, ch, blocks)
        st(dst, p, (y + z) + x, blocks)

    loop(r0, count, ch, body)


def operator(l, v, p, ch):
    x = ld(v, p, ch)
    lon = ld(l.e, p, ch) * (x - roll_l(x, -l.s)) + ld(l.west, p, ch) * (x - roll_l(x, l.s))
    lat = ld(l.so, p, ch) * (x - ld(v, p + 1, ch)) + ld(l.so, p - 1, ch) * (x - ld(v, p - 1, ch))
    return x, lat + lon


def remainder(l, ch):
    def body(r):
        p = l.pad + r
        st(l.r, p, ld(l.f, p, ch) - operator(l, l.v, p, ch)[1])

    loop(0, l.n, ch, body)


def pair(ref, start, n, odd, blocks=ALL):
    return ld(ref, start + odd, n, blocks, 2)


def restrict(l, c):
    ch = min(16, c.n)

    def body(a):
        x = pair(l.r, l.pad + 2 * a, ch, 0) + pair(l.r, l.pad + 2 * a, ch, 1)
        x = x + roll_l(x, -l.s)
        st(c.f, c.pad + a, x)
        st(c.wf, c.pad + a, x * ld(c.w, c.pad + a, ch))

    for a in range(0, c.n, ch):
        body(a)


def coarsen(l, c):
    ch = min(16, c.n)
    for a in range(0, c.n, ch):
        x = pair(l.e, l.pad + 2 * a, ch, 0) + pair(l.e, l.pad + 2 * a, ch, 1)
        st(c.e, c.pad + a, roll_l(x, -l.s))
        y = pair(l.so, l.pad + 2 * a, ch, 1)
        st(c.so, c.pad + a, y + roll_l(y, -l.s))


def spread_rows(v, start, e, add, blocks=ALL):
    for odd in (0, 1):
        x = e
        if add:
            x = x + ld(v, start + odd, e.shape[0], blocks, 2)
        st(v, start + odd, x, blocks, 2)


def prolong(c, l, src, dst, a0, n, add, blocks=ALL):
    for a in range(0, n, 8):
        e = ld(src, c.pad + a0 + a, 8, blocks)
        e = jnp.where((lanes(e.shape) & l.s) == 0, e, roll_l(e, l.s))
        spread_rows(dst, l.pad + 2 * (a0 + a), e, add, blocks)


def pick(x, index):
    return jnp.take_along_axis(x, index, axis=1, mode="promise_in_bounds")


def compact(x, offset):
    l = lanes((8, 128))
    index = (l % 32) * 4 + offset
    out = pick(x[:, 384:512], index)
    for j in (2, 1, 0):
        out = jnp.where(l < 32 * (j + 1), pick(x[:, 128 * j:128 * (j + 1)], index), out)
    return out


def expand(x, base):
    l = lanes((8, 128))
    q = l // 4
    own = x[2, pl.ds(base, 8), :]
    parts = [pick(own, q + 32 * j) for j in range(4)]
    east = pick(x[3, pl.ds(base, 8), :], q)
    west = pick(x[1, pl.ds(base, 8), :], q + 96)
    return jnp.concatenate(parts + [jnp.where(l < 64, east, west)], axis=1)


def kernel(
    b_in, e_in, s_in, sol, res,
    g, pk, re_, rw_, a0, ag, c, t1, got1, t2, got2,
    *rest,
):
    fine0, fine1, fine2, fine3, fine4, fine5 = rest[:9], rest[9:22], rest[22:32], rest[32:45], rest[45:58], rest[58:72]
    in_sem, a_send, a_recv, cs_send, cs_recv, fs_send, fs_recv, c1_send, c1_recv, c2_send, c2_recv = rest[72:]

    l0 = Level(1, PAD, N0, g.at[0], g.at[1], g.at[2], *fine0[:5], None, *fine0[5:])
    l1 = Level(2, PAD, N0 // 2, *fine1)
    l2 = Level(1, PAD2, 64, c.at[0], c.at[1], c.at[2], *fine2)
    l3 = Level(2, PAD, 32, *fine3)
    l4 = Level(4, PAD, 16, *fine4)
    l5 = Level(8, PAD, 8, *fine5)
    lat, lon = lax.axis_index("lat"), lax.axis_index("lon")

    def device(dlon, dlat):
        return {"lon": lax.rem(lon + dlon + NLON, NLON), "lat": lax.rem(lat + dlat + NLAT, NLAT)}

    block = (lon // BLOCK) * BLOCK
    inner = lax.rem(lon, BLOCK)

    def mate1(d):
        return {"lon": block + lax.rem(inner + d, BLOCK), "lat": lat}

    def mate2(d):
        return device(BLOCK * (d // 4), d % 4)

    top = PAD + H
    loads = [
        pltpu.make_async_copy(x.at[:, pl.ds(128 * j, 128)], g.at[i, j, pl.ds(top, ROWS)], in_sem.at[i, j])
        for i, x in enumerate((b_in, e_in, s_in))
        for j in range(4)
    ]
    barrier = pltpu.get_barrier_semaphore()
    greeted = [device(*d) for d in HALO] + [device(0, 2), device(2, 0), device(-2, 0)]
    greeted += [mate1(d) for d in range(1, BLOCK)] + [mate2(d) for d in range(4, 16)]
    for k, other in enumerate(greeted):
        pl.semaphore_signal(barrier, inc=1, device_id=other, device_id_type=MESH)
        if k == len(HALO) - 1:
            for copy in loads:
                copy.start()

    def clear(ref, l):
        zero = jnp.zeros((l.pad, WIDE), F32)
        st(ref, 0, zero)
        st(ref, l.pad + l.n, zero)

    for l in (l0, l1):
        for ref in (l.wf, l.v, l.v2, l.q):
            clear(ref, l)
    for l in (l2, l3, l4, l5):
        for ref in (l.wf, l.v, l.v2, l.q, l.so):
            clear(ref, l)
    for ref in (l2.ae, l2.aw, l2.as_, l2.an):
        clear(ref, l2)
    for ref in (l5.e, l5.r):
        clear(ref, l5)

    for copy in loads:
        copy.wait()

    l8 = lanes((8, 128))
    for k in range(ROWS // 8):
        rows = slice(top + 8 * k, top + 8 * k + 8)
        first = [g[i, 0, rows] for i in range(3)]
        last = [g[i, 3, rows] for i in range(3)]
        x = jnp.where(l8 < 16, first[0], jnp.where(l8 < 32, roll_l(first[1], 16), roll_l(first[2], 32)))
        y = jnp.where(l8 >= 112, last[0], jnp.where(l8 >= 96, roll_l(last[1], -16), roll_l(last[2], -32)))
        pk[8 * k:8 * k + 8] = jnp.where(l8 < 64, x, y)

    own_rows = pl.ds(pl.multiple_of(PAD2 + lat * 16, 16), 16)

    for a in range(0, 16, 8):
        x = ld(g.at[1], top + 4 * a, 8, range(4), 4)
        for j in (1, 2, 3):
            x = x + ld(g.at[1], top + 4 * a + j, 8, range(4), 4)
        y = ld(g.at[2], top + 4 * a + 3, 8, range(4), 4)
        y = y + roll_l(y, -1)
        y = y + roll_l(y, -2)
        rows = pl.ds(pl.multiple_of(PAD2 + lat * 16 + a, 8), 8)
        c[1, 2, rows, :] = compact(x, 3)
        c[2, 2, rows, :] = compact(y, 0)

    pl.semaphore_wait(barrier, len(greeted))

    def send(src, dst, s_sem, r_sem, k, to):
        copy = pltpu.make_async_remote_copy(
            src_ref=src, dst_ref=dst, send_sem=s_sem.at[k], recv_sem=r_sem.at[k], device_id=to, device_id_type=MESH
        )
        copy.start()
        return copy

    halos = []
    for k, (dlon, dlat) in enumerate(HALO):
        first_row, count = {0: (0, ROWS), 1: (ROWS - H, H), -1: (0, H)}[dlat]
        to = {0: H, 1: 0, -1: H + ROWS}[dlat]
        if dlon == 0:
            src = g.at[:, pl.ds(0, 4), pl.ds(top + first_row, count)]
            dst = g.at[:, pl.ds(0, 4), pl.ds(PAD + to, count)]
        else:
            src = pk.at[pl.ds(first_row, count)]
            dst = (rw_ if dlon == 1 else re_).at[pl.ds(to, count)]
        halos.append(send(src, dst, a_send, a_recv, k, device(dlon, dlat)))

    def spread_lat(index, s_sem, r_sem):
        part = c.at[index, 2, own_rows]
        return [send(part, part, s_sem, r_sem, k, device(0, d)) for k, d in enumerate(SPREAD_LAT)]

    def spread_lon(index, s_sem, r_sem):
        rows = pl.ds(PAD2, 64)
        return [
            send(c.at[index, 2, rows], c.at[index, 2 - d, rows], s_sem, r_sem, 3 + k, device(d, 0))
            for k, d in enumerate(SPREAD_LON)
        ]

    conds = spread_lat(pl.ds(1, 2), cs_send, cs_recv)

    for copy in halos:
        copy.wait_recv()
    for copy in conds:
        copy.wait_recv()
    conds_lon = spread_lon(pl.ds(1, 2), cs_send, cs_recv)

    has_north = jnp.where(lat > 0, 1.0, 0.0).astype(F32)
    used = (l8 < 16) | (l8 >= 112)
    for k in range(N0 // 8):
        x = jnp.where(l8 < 64, re_[8 * k:8 * k + 8], rw_[8 * k:8 * k + 8])
        for i, other in ((0, 0.0), (1, 1.0), (2, 1.0)):
            y = x if i == 0 else jnp.where(l8 < 64, roll_l(x, -16 * i), roll_l(x, 16 * i))
            g[i, 4, PAD + 8 * k:PAD + 8 * k + 8, :] = jnp.where(used, y, other)
    g[2, :, PAD:PAD + H] = g[2, :, PAD:PAD + H] * has_north

    def bounds(halo, own):
        return jnp.where(lat > 0, 0, halo), jnp.where(lat < NLAT - 1, 2 * halo + own, halo + own)

    coeffs(l0, 32, bounds(H, ROWS), True)
    sweep(l0, l0.wf, l0.v, True, 0, N0, 32)
    coarsen(l0, l1)
    remainder(l0, 32)
    coeffs(l1, 24, bounds(H // 2, ROWS // 2))
    restrict(l0, l1)
    sweep(l1, l1.wf, l1.v, True, 0, 48, 48)
    remainder(l1, 48)
    for a in range(0, 16, 8):
        x = ld(l1.r, PAD + 8 + 2 * a, 8, range(4), 2) + ld(l1.r, PAD + 9 + 2 * a, 8, range(4), 2)
        rows = pl.ds(pl.multiple_of(PAD2 + lat * 16 + a, 8), 8)
        c[0, 2, rows, :] = compact(x + roll_l(x, -2), 0)
    fields = spread_lat(0, fs_send, fs_recv)

    for copy in conds_lon:
        copy.wait_recv()
    coeffs(l2, 32)
    coarsen(l2, l3)
    coeffs(l3, 32)
    coarsen(l3, l4)
    coeffs(l4, 16)
    coarsen(l4, l5)
    coeffs(l5, 8)


    def twice(l, v, source, r0, count, ch, blocks=ALL):
        sweep(l, v, l.v2, source, r0, count, ch, blocks)
        sweep(l, l.v2, v, source, r0, count, ch, blocks)

    def rise_coarse(name, source):
        u = [getattr(l, name) for l in (l0, l1, l2, l3, l4, l5)]
        twice(l5, u[5], source, 0, 8, 8, MID)
        prolong(l5, l4, u[5], u[4], 0, 8, source, MID)
        twice(l4, u[4], source, 0, 16, 16, MID)
        prolong(l4, l3, u[4], u[3], 0, 16, source, MID)
        twice(l3, u[3], source, 0, 32, 32, MID)
        near = lat * 8 - 4
        prolong(l3, l2, u[3], u[2], near, 16, source, MID)
        near = pl.multiple_of(lat * 16 - 8, 8)
        twice(l2, u[2], source, near, 32, 32, MID)

    def rise_fine(name, source):
        u = [getattr(l, name) for l in (l0, l1, l2)]
        for i in range(3):
            e = expand(u[2], PAD2 + lat * 16 - 4 + 8 * i)
            spread_rows(u[1], PAD + 16 * i, e, source)
        twice(l1, u[1], source, 0, 48, 48)
        prolong(l1, l0, u[1], u[0], 0, 48, source)
        twice(l0, u[0], source, 8, 80, 40)

    def applied(v, out, sums, n):
        def body(k, carry):
            r = pl.multiple_of(k * 16, 16)
            x, av = operator(l0, v, top + r, 16)
            x, av = x[:, :COLS], av[:, :COLS]
            out[pl.ds(r, 16)] = av
            more = sums(pl.ds(r, 16), ld(l0.f, top + r, 16, range(4)), x, av)
            return tuple(y + (z[:8] + z[8:]) for y, z in zip(carry, more))

        return lax.fori_loop(0, ROWS // 16, body, (jnp.zeros((8, COLS), F32),) * n)

    st(l5.q, PAD, jnp.ones((8, WIDE), F32))
    rise_coarse("q", False)
    for copy in halos + conds:
        copy.wait_send()
    for copy in fields:
        copy.wait_recv()
    fields_lon = spread_lon(0, fs_send, fs_recv)
    rise_fine("q", False)
    for copy in fields + conds_lon:
        copy.wait_send()
    sums_q = applied(l0.q, ag, lambda rows, b, v, av: (b * v, v * av), 2)

    for copy in fields_lon:
        copy.wait_recv()

    def first(r):
        st(l2.wf, PAD2 + r, ld(l2.w, PAD2 + r, 32) * ld(l2.f, PAD2 + r, 32))

    loop(0, 64, 32, first)
    sweep(l2, l2.wf, l2.v, True, 0, 64, 32)
    remainder(l2, 32)
    for l, coarse in ((l2, l3), (l3, l4), (l4, l5)):
        restrict(l, coarse)
        sweep(coarse, coarse.wf, coarse.v, True, 0, coarse.n, coarse.n)
        remainder(coarse, coarse.n)

    x = pair(l5.r, PAD, 8, 0) + pair(l5.r, PAD, 8, 1)
    f6 = x + roll_l(x, -8)
    x = pair(l5.e, PAD, 8, 0) + pair(l5.e, PAD, 8, 1)
    e6 = roll_l(x, -8)
    x = pair(l5.so, PAD, 8, 1)
    s6 = x + roll_l(x, -8)
    row6, lane6 = rows_of((8, WIDE)), lanes((8, WIDE))
    west6 = roll_l(e6, 16)
    north6 = jnp.where(row6 == 0, 0.0, pltpu.roll(s6, 1, 0))
    w6 = jnp.where(row6 < 4, OMEGA / (((e6 + west6) + s6) + north6), 0.0)
    ae6, aw6, as6, an6, wf6 = w6 * e6, w6 * west6, w6 * s6, w6 * north6, w6 * f6
    field = wf6
    for _ in range(COARSE_SWEEPS - 1):
        x = ae6 * roll_l(field, -16) + aw6 * roll_l(field, 16)
        y = as6 * pltpu.roll(field, 7, 0) + an6 * pltpu.roll(field, 1, 0)
        field = (((1.0 - OMEGA) * field + wf6) + y) + x
    lon6 = e6 * (field - roll_l(field, -16)) + west6 * (field - roll_l(field, 16))
    lat6 = s6 * (field - pltpu.roll(field, 7, 0)) + north6 * (field - pltpu.roll(field, 1, 0))
    left = f6 - (lon6 + lat6)
    mine = ((lane6 & 15) == 0) & (lane6 >= 256) & (lane6 < 384)
    left = jnp.where(mine & (row6 == lat), left, 0.0)[:, 256:384]
    last = jnp.where(mine & (row6 == 3) & (lat == 3), s6, 0.0)[:, 256:384]

    e = jnp.where((lane6 & 8) == 0, field, roll_l(field, 8))
    for odd in (0, 1):
        st(l5.r, odd, e, ALL, 2)
    st(l5.v, PAD, ld(l5.v, PAD, 8) + ld(l5.r, 0, 8))
    rise_coarse("v", True)
    rise_fine("v", True)
    sums_v = applied(l0.v, a0, lambda rows, b, v, av: (b * v, v * av, v * ag[rows]), 3)

    def wait_all(got, sem):
        pltpu.make_async_copy(got, got, sem.at[0]).wait()

    def fold(x):
        return (x[:, 0:128] + x[:, 128:256]) + (x[:, 256:384] + x[:, 384:512])

    seven = [left, last, fold(sums_v[0]), fold(sums_q[0]), fold(sums_v[1]), fold(sums_v[2]), fold(sums_q[1])]
    row = rows_of((8, 128))
    total = jnp.zeros((8, 128), F32)
    for i, x in enumerate(seven):
        total = jnp.where(row == i, jnp.sum(x, axis=0, keepdims=True), total)
    t1[...] = total
    for d in range(1, 16):
        send(t1, got1.at[d - 1], c1_send, c1_recv, 0, mate1(d))
    for copy in fields_lon:
        copy.wait_send()
    wait_all(got1, c1_recv)

    def gathered(total, got):
        parts = [total] + [got[d] for d in range(15)]
        while len(parts) > 1:
            parts = [x + y for x, y in zip(parts[::2], parts[1::2])]
        return parts[0]

    total = gathered(total, got1)
    t2[...] = total
    for d in range(1, 16):
        send(t2, got2.at[d - 1], c2_send, c2_recv, 0, mate2(d))
    wait_all(got1, c1_send)
    wait_all(got2, c2_recv)
    total = gathered(total, got2)
    for by in (64, 32, 16, 8, 4, 2, 1):
        total = total + pltpu.roll(total, by, 1)
    n_left, n_last, bv, bq, vav, vaq, qaq = [total[i:i + 1] for i in range(7)]
    const = n_left / n_last
    step = (bv + const * bq) / ((vav + (2.0 * const) * vaq) + (const * const) * qaq)
    both = jnp.concatenate([step * const] * 4, axis=1)
    step = jnp.concatenate([step] * 4, axis=1)

    def final(k, carry):
        r = pl.multiple_of(k * 16, 16)
        rows = pl.ds(r, 16)
        sol[rows] = step * ld(l0.v, top + r, 16, range(4)) + both * ld(l0.q, top + r, 16, range(4))
        res[rows] = ld(l0.f, top + r, 16, range(4)) - (step * a0[rows] + both * ag[rows])
        return carry

    lax.fori_loop(0, 4, final, 0)
    wait_all(got2, c2_send)


def body(guidance, cond_lon, cond_lat):
    def vm(*shape):
        return pltpu.VMEM(shape, F32)

    def wide(n, count):
        return [vm(5, n, 128)] * count

    dma = pltpu.SemaphoreType.DMA
    scratch = [vm(3, 5, N0 + 2 * PAD, 128), vm(ROWS, 128), vm(N0, 128), vm(N0, 128), vm(ROWS, COLS), vm(ROWS, COLS)]
    scratch += [vm(3, 5, 64 + 2 * PAD2, 128), vm(8, 128), vm(15, 8, 128), vm(8, 128), vm(15, 8, 128)]
    scratch += wide(N0 + 2 * PAD, 9) + wide(N0 // 2 + 2 * PAD, 13) + wide(64 + 2 * PAD2, 10)
    scratch += wide(32 + 2 * PAD, 13) + wide(16 + 2 * PAD, 13) + wide(8 + 2 * PAD, 14)
    scratch += [dma((3, 4)), dma((8,)), dma((8,)), dma((7,)), dma((7,)), dma((7,)), dma((7,))] + [dma((1,))] * 4
    return pl.pallas_call(
        kernel,
        out_shape=(jax.ShapeDtypeStruct((ROWS, COLS), F32),) * 2,
        in_specs=[pl.BlockSpec(memory_space=pltpu.HBM)] * 3,
        out_specs=(pl.BlockSpec(memory_space=pltpu.VMEM),) * 2,
        scratch_shapes=scratch,
        compiler_params=pltpu.CompilerParams(
            collective_id=0, has_side_effects=True, vmem_limit_bytes=63 * 1024 * 1024
        ),
        cost_estimate=pl.CostEstimate(flops=10_000_000, bytes_accessed=655360, transcendentals=0),
    )(guidance, cond_lon, cond_lat)


def solution(mesh):
    spec = P("lat", "lon")
    return jax.shard_map(body, mesh=mesh, in_specs=(spec,) * 3, out_specs=(spec,) * 2, check_vma=False)
```

```python
import jax
import jax.numpy as jnp
from jax import lax
from jax.experimental import pallas as pl
from jax.experimental.pallas import tpu as pltpu
from jax.sharding import PartitionSpec as P

OMEGA = 0.8
COARSE_SWEEPS = 8
NLAT, NLON, BLOCK = 4, 64, 16
ROWS, COLS = 64, 512
H = 16
PAD = 8
PAD2 = 16
N0 = ROWS + 2 * H
WIDE = COLS + 128
ALL = range(5)
MID = range(1, 4)
MESH = pl.DeviceIdType.MESH
F32 = jnp.float32

HALO = ((0, 1), (0, -1), (1, 0), (-1, 0), (1, 1), (1, -1), (-1, 1), (-1, -1))
SPREAD_LAT = (1, 2, 3)
SPREAD_LON = (1, -1, 2, -2)


def lanes(shape):
    return lax.broadcasted_iota(jnp.int32, shape, len(shape) - 1)


def rows_of(shape):
    return lax.broadcasted_iota(jnp.int32, shape, 0)


def roll_l(x, by):
    return pltpu.roll(x, by % x.shape[1], 1)


def ld(ref, start, n, blocks=ALL, stride=None):
    rows = pl.ds(start, n) if stride is None else pl.ds(start, n, stride=stride)
    return jnp.concatenate([ref[j, rows, :] for j in blocks], axis=1)


def st(ref, start, x, blocks=ALL, stride=None):
    n = x.shape[0]
    rows = pl.ds(start, n) if stride is None else pl.ds(start, n, stride=stride)
    for i, j in enumerate(blocks):
        ref[j, rows, :] = x[:, 128 * i:128 * (i + 1)]


def loop(r0, count, ch, body):
    if count == ch:
        body(r0)
    else:

        def step(k, carry):
            body(pl.multiple_of(r0 + k * ch, 8))
            return carry

        lax.fori_loop(0, count // ch, step, 0)


class Level:
    def __init__(self, s, pad, n, f, e, so, west, ae, aw, as_, an, w, wf, v, v2, q, r=None):
        self.s, self.pad, self.n = s, pad, n
        self.f, self.e, self.so, self.west = f, e, so, west
        self.ae, self.aw, self.as_, self.an, self.w, self.wf = ae, aw, as_, an, w, wf
        self.v, self.v2, self.q, self.r = v, v2, q, v2 if r is None else r


def coeffs(l, ch, keep=None, source=False):
    def body(r):
        p = l.pad + r
        e, so, no = ld(l.e, p, ch), ld(l.so, p, ch), ld(l.so, p - 1, ch)
        we = roll_l(e, l.s)
        wk = OMEGA / (((e + we) + so) + no)
        if keep is not None:
            row = rows_of(wk.shape) + r
            wk = jnp.where((row >= keep[0]) & (row < keep[1]), wk, 0.0)
        st(l.west, p, we)
        st(l.ae, p, wk * e)
        st(l.aw, p, wk * we)
        st(l.as_, p, wk * so)
        st(l.an, p, wk * no)
        if source:
            st(l.wf, p, wk * ld(l.f, p, ch))
        else:
            st(l.w, p, wk)

    loop(0, l.n, ch, body)


def sweep(l, src, dst, source, r0, count, ch, blocks=ALL):
    def body(r):
        p = l.pad + r
        v = ld(src, p, ch, blocks)
        x = ld(l.ae, p, ch, blocks) * roll_l(v, -l.s) + ld(l.aw, p, ch, blocks) * roll_l(v, l.s)
        y = ld(l.as_, p, ch, blocks) * ld(src, p + 1, ch, blocks) + ld(l.an, p, ch, blocks) * ld(src, p - 1, ch, blocks)
        z = (1.0 - OMEGA) * v
        if source:
            z = z + ld(l.wf, p, ch, blocks)
        st(dst, p, (y + z) + x, blocks)

    loop(r0, count, ch, body)


def operator(l, v, p, ch):
    x = ld(v, p, ch)
    lon = ld(l.e, p, ch) * (x - roll_l(x, -l.s)) + ld(l.west, p, ch) * (x - roll_l(x, l.s))
    lat = ld(l.so, p, ch) * (x - ld(v, p + 1, ch)) + ld(l.so, p - 1, ch) * (x - ld(v, p - 1, ch))
    return x, lat + lon


def remainder(l, ch):
    def body(r):
        p = l.pad + r
        st(l.r, p, ld(l.f, p, ch) - operator(l, l.v, p, ch)[1])

    loop(0, l.n, ch, body)


def pair(ref, start, n, odd, blocks=ALL):
    return ld(ref, start + odd, n, blocks, 2)


def restrict(l, c):
    ch = min(16, c.n)

    def body(a):
        x = pair(l.r, l.pad + 2 * a, ch, 0) + pair(l.r, l.pad + 2 * a, ch, 1)
        x = x + roll_l(x, -l.s)
        st(c.f, c.pad + a, x)
        st(c.wf, c.pad + a, x * ld(c.w, c.pad + a, ch))

    loop(0, c.n, ch, body)


def coarsen(l, c):
    ch = min(16, c.n)

    def body(a):
        x = pair(l.e, l.pad + 2 * a, ch, 0) + pair(l.e, l.pad + 2 * a, ch, 1)
        st(c.e, c.pad + a, roll_l(x, -l.s))
        y = pair(l.so, l.pad + 2 * a, ch, 1)
        st(c.so, c.pad + a, y + roll_l(y, -l.s))

    loop(0, c.n, ch, body)


def spread_rows(v, start, e, add, blocks=ALL):
    for odd in (0, 1):
        x = e
        if add:
            x = x + ld(v, start + odd, e.shape[0], blocks, 2)
        st(v, start + odd, x, blocks, 2)


def prolong(c, l, src, dst, a0, n, add, blocks=ALL):
    def body(a):
        e = ld(src, c.pad + a0 + a, 8, blocks)
        e = jnp.where((lanes(e.shape) & l.s) == 0, e, roll_l(e, l.s))
        spread_rows(dst, l.pad + 2 * (a0 + a), e, add, blocks)

    loop(0, n, 8, body)


def pick(x, index):
    return jnp.take_along_axis(x, index, axis=1, mode="promise_in_bounds")


def compact(x, offset):
    l = lanes((8, 128))
    index = (l % 32) * 4 + offset
    out = pick(x[:, 384:512], index)
    for j in (2, 1, 0):
        out = jnp.where(l < 32 * (j + 1), pick(x[:, 128 * j:128 * (j + 1)], index), out)
    return out


def expand(x, base):
    l = lanes((8, 128))
    q = l // 4
    own = x[2, pl.ds(base, 8), :]
    parts = [pick(own, q + 32 * j) for j in range(4)]
    east = pick(x[3, pl.ds(base, 8), :], q)
    west = pick(x[1, pl.ds(base, 8), :], q + 96)
    return jnp.concatenate(parts + [jnp.where(l < 64, east, west)], axis=1)


def kernel(
    b_in, e_in, s_in, sol, res,
    g, pk, re_, rw_, a0, ag, c, t1, got1, t2, got2,
    *rest,
):
    fine0, fine1, fine2, fine3, fine4, fine5 = rest[:9], rest[9:22], rest[22:32], rest[32:45], rest[45:58], rest[58:72]
    in_sem, a_send, a_recv, cs_send, cs_recv, fs_send, fs_recv, c1_send, c1_recv, c2_send, c2_recv = rest[72:]

    l0 = Level(1, PAD, N0, g.at[0], g.at[1], g.at[2], *fine0[:5], None, *fine0[5:])
    l1 = Level(2, PAD, N0 // 2, *fine1)
    l2 = Level(1, PAD2, 64, c.at[0], c.at[1], c.at[2], *fine2)
    l3 = Level(2, PAD, 32, *fine3)
    l4 = Level(4, PAD, 16, *fine4)
    l5 = Level(8, PAD, 8, *fine5)
    lat, lon = lax.axis_index("lat"), lax.axis_index("lon")

    def device(dlon, dlat):
        return {"lon": lax.rem(lon + dlon + NLON, NLON), "lat": lax.rem(lat + dlat + NLAT, NLAT)}

    block = (lon // BLOCK) * BLOCK
    inner = lax.rem(lon, BLOCK)

    def mate1(d):
        return {"lon": block + lax.rem(inner + d, BLOCK), "lat": lat}

    def mate2(d):
        return device(BLOCK * (d // 4), d % 4)

    top = PAD + H
    loads = [
        pltpu.make_async_copy(x.at[:, pl.ds(128 * j, 128)], g.at[i, j, pl.ds(top, ROWS)], in_sem.at[i, j])
        for i, x in enumerate((b_in, e_in, s_in))
        for j in range(4)
    ]
    barrier = pltpu.get_barrier_semaphore()
    greeted = [device(*d) for d in HALO] + [device(0, 2), device(2, 0), device(-2, 0)]
    greeted += [mate1(d) for d in range(1, BLOCK)] + [mate2(d) for d in range(4, 16)]
    for k, other in enumerate(greeted):
        pl.semaphore_signal(barrier, inc=1, device_id=other, device_id_type=MESH)
        if k == len(HALO) - 1:
            for copy in loads:
                copy.start()

    def clear(ref, l):
        zero = jnp.zeros((l.pad, WIDE), F32)
        st(ref, 0, zero)
        st(ref, l.pad + l.n, zero)

    for l in (l0, l1):
        for ref in (l.wf, l.v, l.v2, l.q):
            clear(ref, l)
    for l in (l2, l3, l4, l5):
        for ref in (l.wf, l.v, l.v2, l.q, l.so):
            clear(ref, l)
    for ref in (l2.ae, l2.aw, l2.as_, l2.an):
        clear(ref, l2)
    for ref in (l5.e, l5.r):
        clear(ref, l5)

    for copy in loads:
        copy.wait()

    l8 = lanes((8, 128))
    def pack(a):
        rows = pl.ds(pl.multiple_of(top + a, 8), 8)
        first = [g[i, 0, rows] for i in range(3)]
        last = [g[i, 3, rows] for i in range(3)]
        x = jnp.where(l8 < 16, first[0], jnp.where(l8 < 32, roll_l(first[1], 16), roll_l(first[2], 32)))
        y = jnp.where(l8 >= 112, last[0], jnp.where(l8 >= 96, roll_l(last[1], -16), roll_l(last[2], -32)))
        pk[pl.ds(a, 8)] = jnp.where(l8 < 64, x, y)

    loop(0, ROWS, 8, pack)

    own_rows = pl.ds(pl.multiple_of(PAD2 + lat * 16, 16), 16)

    for a in range(0, 16, 8):
        x = ld(g.at[1], top + 4 * a, 8, range(4), 4)
        for j in (1, 2, 3):
            x = x + ld(g.at[1], top + 4 * a + j, 8, range(4), 4)
        y = ld(g.at[2], top + 4 * a + 3, 8, range(4), 4)
        y = y + roll_l(y, -1)
        y = y + roll_l(y, -2)
        rows = pl.ds(pl.multiple_of(PAD2 + lat * 16 + a, 8), 8)
        c[1, 2, rows, :] = compact(x, 3)
        c[2, 2, rows, :] = compact(y, 0)

    pl.semaphore_wait(barrier, len(greeted))

    def send(src, dst, s_sem, r_sem, k, to):
        copy = pltpu.make_async_remote_copy(
            src_ref=src, dst_ref=dst, send_sem=s_sem.at[k], recv_sem=r_sem.at[k], device_id=to, device_id_type=MESH
        )
        copy.start()
        return copy

    halos = []
    for k, (dlon, dlat) in enumerate(HALO):
        first_row, count = {0: (0, ROWS), 1: (ROWS - H, H), -1: (0, H)}[dlat]
        to = {0: H, 1: 0, -1: H + ROWS}[dlat]
        if dlon == 0:
            src = g.at[:, pl.ds(0, 4), pl.ds(top + first_row, count)]
            dst = g.at[:, pl.ds(0, 4), pl.ds(PAD + to, count)]
        else:
            src = pk.at[pl.ds(first_row, count)]
            dst = (rw_ if dlon == 1 else re_).at[pl.ds(to, count)]
        halos.append(send(src, dst, a_send, a_recv, k, device(dlon, dlat)))

    def spread_lat(index, s_sem, r_sem):
        part = c.at[index, 2, own_rows]
        return [send(part, part, s_sem, r_sem, k, device(0, d)) for k, d in enumerate(SPREAD_LAT)]

    def spread_lon(index, s_sem, r_sem):
        rows = pl.ds(PAD2, 64)
        return [
            send(c.at[index, 2, rows], c.at[index, 2 - d, rows], s_sem, r_sem, 3 + k, device(d, 0))
            for k, d in enumerate(SPREAD_LON)
        ]

    conds = spread_lat(pl.ds(1, 2), cs_send, cs_recv)

    for copy in halos:
        copy.wait_recv()
    for copy in conds:
        copy.wait_recv()
    conds_lon = spread_lon(pl.ds(1, 2), cs_send, cs_recv)

    has_north = jnp.where(lat > 0, 1.0, 0.0).astype(F32)
    used = (l8 < 16) | (l8 >= 112)

    def unpack(a):
        x = jnp.where(l8 < 64, re_[pl.ds(a, 8)], rw_[pl.ds(a, 8)])
        for i, other in ((0, 0.0), (1, 1.0), (2, 1.0)):
            y = x if i == 0 else jnp.where(l8 < 64, roll_l(x, -16 * i), roll_l(x, 16 * i))
            g[i, 4, pl.ds(pl.multiple_of(PAD + a, 8), 8), :] = jnp.where(used, y, other)

    loop(0, N0, 8, unpack)
    g[2, :, PAD:PAD + H] = g[2, :, PAD:PAD + H] * has_north

    def bounds(halo, own):
        return jnp.where(lat > 0, 0, halo), jnp.where(lat < NLAT - 1, 2 * halo + own, halo + own)

    coeffs(l0, 16, bounds(H, ROWS), True)
    sweep(l0, l0.wf, l0.v, True, 0, N0, 16)
    coarsen(l0, l1)
    remainder(l0, 16)
    coeffs(l1, 16, bounds(H // 2, ROWS // 2))
    restrict(l0, l1)
    sweep(l1, l1.wf, l1.v, True, 0, 48, 16)
    remainder(l1, 16)
    for a in range(0, 16, 8):
        x = ld(l1.r, PAD + 8 + 2 * a, 8, range(4), 2) + ld(l1.r, PAD + 9 + 2 * a, 8, range(4), 2)
        rows = pl.ds(pl.multiple_of(PAD2 + lat * 16 + a, 8), 8)
        c[0, 2, rows, :] = compact(x + roll_l(x, -2), 0)
    fields = spread_lat(0, fs_send, fs_recv)

    for copy in conds_lon:
        copy.wait_recv()
    coeffs(l2, 16)
    coarsen(l2, l3)
    coeffs(l3, 16)
    coarsen(l3, l4)
    coeffs(l4, 16)
    coarsen(l4, l5)
    coeffs(l5, 8)


    def twice(l, v, source, r0, count, ch, blocks=ALL):
        sweep(l, v, l.v2, source, r0, count, ch, blocks)
        sweep(l, l.v2, v, source, r0, count, ch, blocks)

    def rise_coarse(name, source):
        u = [getattr(l, name) for l in (l0, l1, l2, l3, l4, l5)]
        twice(l5, u[5], source, 0, 8, 8, MID)
        prolong(l5, l4, u[5], u[4], 0, 8, source, MID)
        twice(l4, u[4], source, 0, 16, 16, MID)
        prolong(l4, l3, u[4], u[3], 0, 16, source, MID)
        twice(l3, u[3], source, 0, 32, 16, MID)
        near = lat * 8 - 4
        prolong(l3, l2, u[3], u[2], near, 16, source, MID)
        near = pl.multiple_of(lat * 16 - 8, 8)
        twice(l2, u[2], source, near, 32, 16, MID)

    def rise_fine(name, source):
        u = [getattr(l, name) for l in (l0, l1, l2)]
        for i in range(3):
            e = expand(u[2], PAD2 + lat * 16 - 4 + 8 * i)
            spread_rows(u[1], PAD + 16 * i, e, source)
        twice(l1, u[1], source, 0, 48, 16)
        prolong(l1, l0, u[1], u[0], 0, 48, source)
        twice(l0, u[0], source, 8, 80, 16)

    def applied(v, out, sums, n):
        def body(k, carry):
            r = pl.multiple_of(k * 16, 16)
            x, av = operator(l0, v, top + r, 16)
            x, av = x[:, :COLS], av[:, :COLS]
            out[pl.ds(r, 16)] = av
            more = sums(pl.ds(r, 16), ld(l0.f, top + r, 16, range(4)), x, av)
            return tuple(y + (z[:8] + z[8:]) for y, z in zip(carry, more))

        return lax.fori_loop(0, ROWS // 16, body, (jnp.zeros((8, COLS), F32),) * n)

    st(l5.q, PAD, jnp.ones((8, WIDE), F32))
    rise_coarse("q", False)
    for copy in halos + conds:
        copy.wait_send()
    for copy in fields:
        copy.wait_recv()
    fields_lon = spread_lon(0, fs_send, fs_recv)
    rise_fine("q", False)
    for copy in fields + conds_lon:
        copy.wait_send()
    sums_q = applied(l0.q, ag, lambda rows, b, v, av: (b * v, v * av), 2)

    for copy in fields_lon:
        copy.wait_recv()

    def first(r):
        st(l2.wf, PAD2 + r, ld(l2.w, PAD2 + r, 16) * ld(l2.f, PAD2 + r, 16))

    loop(0, 64, 16, first)
    sweep(l2, l2.wf, l2.v, True, 0, 64, 16)
    remainder(l2, 16)
    for l, coarse in ((l2, l3), (l3, l4), (l4, l5)):
        restrict(l, coarse)
        sweep(coarse, coarse.wf, coarse.v, True, 0, coarse.n, min(16, coarse.n))
        remainder(coarse, min(16, coarse.n))

    x = pair(l5.r, PAD, 8, 0) + pair(l5.r, PAD, 8, 1)
    f6 = x + roll_l(x, -8)
    x = pair(l5.e, PAD, 8, 0) + pair(l5.e, PAD, 8, 1)
    e6 = roll_l(x, -8)
    x = pair(l5.so, PAD, 8, 1)
    s6 = x + roll_l(x, -8)
    row6, lane6 = rows_of((8, WIDE)), lanes((8, WIDE))
    west6 = roll_l(e6, 16)
    north6 = jnp.where(row6 == 0, 0.0, pltpu.roll(s6, 1, 0))
    w6 = jnp.where(row6 < 4, OMEGA / (((e6 + west6) + s6) + north6), 0.0)
    ae6, aw6, as6, an6, wf6 = w6 * e6, w6 * west6, w6 * s6, w6 * north6, w6 * f6
    field = wf6
    for _ in range(COARSE_SWEEPS - 1):
        x = ae6 * roll_l(field, -16) + aw6 * roll_l(field, 16)
        y = as6 * pltpu.roll(field, 7, 0) + an6 * pltpu.roll(field, 1, 0)
        field = (((1.0 - OMEGA) * field + wf6) + y) + x
    lon6 = e6 * (field - roll_l(field, -16)) + west6 * (field - roll_l(field, 16))
    lat6 = s6 * (field - pltpu.roll(field, 7, 0)) + north6 * (field - pltpu.roll(field, 1, 0))
    left = f6 - (lon6 + lat6)
    mine = ((lane6 & 15) == 0) & (lane6 >= 256) & (lane6 < 384)
    left = jnp.where(mine & (row6 == lat), left, 0.0)[:, 256:384]
    last = jnp.where(mine & (row6 == 3) & (lat == 3), s6, 0.0)[:, 256:384]

    e = jnp.where((lane6 & 8) == 0, field, roll_l(field, 8))
    for odd in (0, 1):
        st(l5.r, odd, e, ALL, 2)
    st(l5.v, PAD, ld(l5.v, PAD, 8) + ld(l5.r, 0, 8))
    rise_coarse("v", True)
    rise_fine("v", True)
    sums_v = applied(l0.v, a0, lambda rows, b, v, av: (b * v, v * av, v * ag[rows]), 3)

    def wait_all(got, sem):
        pltpu.make_async_copy(got, got, sem.at[0]).wait()

    def fold(x):
        return (x[:, 0:128] + x[:, 128:256]) + (x[:, 256:384] + x[:, 384:512])

    seven = [left, last, fold(sums_v[0]), fold(sums_q[0]), fold(sums_v[1]), fold(sums_v[2]), fold(sums_q[1])]
    row = rows_of((8, 128))
    total = jnp.zeros((8, 128), F32)
    for i, x in enumerate(seven):
        total = jnp.where(row == i, jnp.sum(x, axis=0, keepdims=True), total)
    t1[...] = total
    for d in range(1, 16):
        send(t1, got1.at[d - 1], c1_send, c1_recv, 0, mate1(d))
    for copy in fields_lon:
        copy.wait_send()
    wait_all(got1, c1_recv)

    def gathered(total, got):
        parts = [total] + [got[d] for d in range(15)]
        while len(parts) > 1:
            parts = [x + y for x, y in zip(parts[::2], parts[1::2])]
        return parts[0]

    total = gathered(total, got1)
    t2[...] = total
    for d in range(1, 16):
        send(t2, got2.at[d - 1], c2_send, c2_recv, 0, mate2(d))
    wait_all(got1, c1_send)
    wait_all(got2, c2_recv)
    total = gathered(total, got2)
    for by in (64, 32, 16, 8, 4, 2, 1):
        total = total + pltpu.roll(total, by, 1)
    n_left, n_last, bv, bq, vav, vaq, qaq = [total[i:i + 1] for i in range(7)]
    const = n_left / n_last
    step = (bv + const * bq) / ((vav + (2.0 * const) * vaq) + (const * const) * qaq)
    both = jnp.concatenate([step * const] * 4, axis=1)
    step = jnp.concatenate([step] * 4, axis=1)

    def final(k, carry):
        r = pl.multiple_of(k * 16, 16)
        rows = pl.ds(r, 16)
        sol[rows] = step * ld(l0.v, top + r, 16, range(4)) + both * ld(l0.q, top + r, 16, range(4))
        res[rows] = ld(l0.f, top + r, 16, range(4)) - (step * a0[rows] + both * ag[rows])
        return carry

    lax.fori_loop(0, 4, final, 0)
    wait_all(got2, c2_send)


def body(guidance, cond_lon, cond_lat):
    def vm(*shape):
        return pltpu.VMEM(shape, F32)

    def wide(n, count):
        return [vm(5, n, 128)] * count

    dma = pltpu.SemaphoreType.DMA
    scratch = [vm(3, 5, N0 + 2 * PAD, 128), vm(ROWS, 128), vm(N0, 128), vm(N0, 128), vm(ROWS, COLS), vm(ROWS, COLS)]
    scratch += [vm(3, 5, 64 + 2 * PAD2, 128), vm(8, 128), vm(15, 8, 128), vm(8, 128), vm(15, 8, 128)]
    scratch += wide(N0 + 2 * PAD, 9) + wide(N0 // 2 + 2 * PAD, 13) + wide(64 + 2 * PAD2, 10)
    scratch += wide(32 + 2 * PAD, 13) + wide(16 + 2 * PAD, 13) + wide(8 + 2 * PAD, 14)
    scratch += [dma((3, 4)), dma((8,)), dma((8,)), dma((7,)), dma((7,)), dma((7,)), dma((7,))] + [dma((1,))] * 4
    return pl.pallas_call(
        kernel,
        out_shape=(jax.ShapeDtypeStruct((ROWS, COLS), F32),) * 2,
        in_specs=[pl.BlockSpec(memory_space=pltpu.HBM)] * 3,
        out_specs=(pl.BlockSpec(memory_space=pltpu.VMEM),) * 2,
        scratch_shapes=scratch,
        compiler_params=pltpu.CompilerParams(
            collective_id=0, has_side_effects=True, vmem_limit_bytes=63 * 1024 * 1024
        ),
        cost_estimate=pl.CostEstimate(flops=10_000_000, bytes_accessed=655360, transcendentals=0),
    )(guidance, cond_lon, cond_lat)


def solution(mesh):
    spec = P("lat", "lon")
    return jax.shard_map(body, mesh=mesh, in_specs=(spec,) * 3, out_specs=(spec,) * 2, check_vma=False)
```

```python
import jax
import jax.numpy as jnp
from jax import lax
from jax.experimental import pallas as pl
from jax.experimental.pallas import tpu as pltpu
from jax.sharding import PartitionSpec as P

OMEGA = 0.8
COARSE_SWEEPS = 8
NLAT, NLON, BLOCK = 4, 64, 16
ROWS, COLS = 64, 512
H = 16
PAD = 8
PAD2 = 16
N0 = ROWS + 2 * H
WIDE = COLS + 128
ALL = range(5)
MID = range(1, 4)
MESH = pl.DeviceIdType.MESH
F32 = jnp.float32

HALO = ((0, 1), (0, -1), (1, 0), (-1, 0), (1, 1), (1, -1), (-1, 1), (-1, -1))
SPREAD_LAT = (1, 2, 3)
SPREAD_LON = (1, -1, 2, -2)


def lanes(shape):
    return lax.broadcasted_iota(jnp.int32, shape, len(shape) - 1)


def rows_of(shape):
    return lax.broadcasted_iota(jnp.int32, shape, 0)


def roll_l(x, by):
    return pltpu.roll(x, by % x.shape[1], 1)


def ld(ref, start, n, blocks=ALL, stride=None):
    rows = pl.ds(start, n) if stride is None else pl.ds(start, n, stride=stride)
    return jnp.concatenate([ref[j, rows, :] for j in blocks], axis=1)


def st(ref, start, x, blocks=ALL, stride=None):
    n = x.shape[0]
    rows = pl.ds(start, n) if stride is None else pl.ds(start, n, stride=stride)
    for i, j in enumerate(blocks):
        ref[j, rows, :] = x[:, 128 * i:128 * (i + 1)]


def loop(r0, count, ch, body):
    for k in range(count // ch):
        body(r0 + k * ch)


class Level:
    def __init__(self, s, pad, n, f, e, so, west, ae, aw, as_, an, w, wf, v, v2, q, r=None):
        self.s, self.pad, self.n = s, pad, n
        self.f, self.e, self.so, self.west = f, e, so, west
        self.ae, self.aw, self.as_, self.an, self.w, self.wf = ae, aw, as_, an, w, wf
        self.v, self.v2, self.q, self.r = v, v2, q, v2 if r is None else r


def coeffs(l, ch, keep=None, source=False):
    def body(r):
        p = l.pad + r
        e, so, no = ld(l.e, p, ch), ld(l.so, p, ch), ld(l.so, p - 1, ch)
        we = roll_l(e, l.s)
        wk = OMEGA / (((e + we) + so) + no)
        if keep is not None:
            row = rows_of(wk.shape) + r
            wk = jnp.where((row >= keep[0]) & (row < keep[1]), wk, 0.0)
        st(l.west, p, we)
        st(l.ae, p, wk * e)
        st(l.aw, p, wk * we)
        st(l.as_, p, wk * so)
        st(l.an, p, wk * no)
        if source:
            st(l.wf, p, wk * ld(l.f, p, ch))
        else:
            st(l.w, p, wk)

    loop(0, l.n, ch, body)


def sweep(l, src, dst, source, r0, count, ch, blocks=ALL):
    def body(r):
        p = l.pad + r
        v = ld(src, p, ch, blocks)
        x = ld(l.ae, p, ch, blocks) * roll_l(v, -l.s) + ld(l.aw, p, ch, blocks) * roll_l(v, l.s)
        y = ld(l.as_, p, ch, blocks) * ld(src, p + 1, ch, blocks) + ld(l.an, p, ch, blocks) * ld(src, p - 1, ch, blocks)
        z = (1.0 - OMEGA) * v
        if source:
            z = z + ld(l.wf, p, ch, blocks)
        st(dst, p, (y + z) + x, blocks)

    loop(r0, count, ch, body)


def operator(l, v, p, ch):
    x = ld(v, p, ch)
    lon = ld(l.e, p, ch) * (x - roll_l(x, -l.s)) + ld(l.west, p, ch) * (x - roll_l(x, l.s))
    lat = ld(l.so, p, ch) * (x - ld(v, p + 1, ch)) + ld(l.so, p - 1, ch) * (x - ld(v, p - 1, ch))
    return x, lat + lon


def remainder(l, ch):
    def body(r):
        p = l.pad + r
        st(l.r, p, ld(l.f, p, ch) - operator(l, l.v, p, ch)[1])

    loop(0, l.n, ch, body)


def pair(ref, start, n, odd, blocks=ALL):
    return ld(ref, start + odd, n, blocks, 2)


def restrict(l, c):
    ch = min(16, c.n)

    def body(a):
        x = pair(l.r, l.pad + 2 * a, ch, 0) + pair(l.r, l.pad + 2 * a, ch, 1)
        x = x + roll_l(x, -l.s)
        st(c.f, c.pad + a, x)
        st(c.wf, c.pad + a, x * ld(c.w, c.pad + a, ch))

    for a in range(0, c.n, ch):
        body(a)


def coarsen(l, c):
    ch = min(16, c.n)
    for a in range(0, c.n, ch):
        x = pair(l.e, l.pad + 2 * a, ch, 0) + pair(l.e, l.pad + 2 * a, ch, 1)
        st(c.e, c.pad + a, roll_l(x, -l.s))
        y = pair(l.so, l.pad + 2 * a, ch, 1)
        st(c.so, c.pad + a, y + roll_l(y, -l.s))


def spread_rows(v, start, e, add, blocks=ALL):
    for odd in (0, 1):
        x = e
        if add:
            x = x + ld(v, start + odd, e.shape[0], blocks, 2)
        st(v, start + odd, x, blocks, 2)


def prolong(c, l, src, dst, a0, n, add, blocks=ALL):
    for a in range(0, n, 8):
        e = ld(src, c.pad + a0 + a, 8, blocks)
        e = jnp.where((lanes(e.shape) & l.s) == 0, e, roll_l(e, l.s))
        spread_rows(dst, l.pad + 2 * (a0 + a), e, add, blocks)


def pick(x, index):
    return jnp.take_along_axis(x, index, axis=1, mode="promise_in_bounds")


def compact(x, offset):
    l = lanes((8, 128))
    index = (l % 32) * 4 + offset
    out = pick(x[:, 384:512], index)
    for j in (2, 1, 0):
        out = jnp.where(l < 32 * (j + 1), pick(x[:, 128 * j:128 * (j + 1)], index), out)
    return out


def expand(x, base):
    l = lanes((8, 128))
    q = l // 4
    own = x[2, pl.ds(base, 8), :]
    parts = [pick(own, q + 32 * j) for j in range(4)]
    east = pick(x[3, pl.ds(base, 8), :], q)
    west = pick(x[1, pl.ds(base, 8), :], q + 96)
    return jnp.concatenate(parts + [jnp.where(l < 64, east, west)], axis=1)


def kernel(
    b_in, e_in, s_in, sol, res,
    g, pk, re_, rw_, a0, ag, c, t1, got1, t2, got2,
    *rest,
):
    fine0, fine1, fine2, fine3, fine4, fine5 = rest[:9], rest[9:22], rest[22:32], rest[32:45], rest[45:58], rest[58:72]
    in_sem, a_send, a_recv, cs_send, cs_recv, fs_send, fs_recv, c1_send, c1_recv, c2_send, c2_recv = rest[72:]

    l0 = Level(1, PAD, N0, g.at[0], g.at[1], g.at[2], *fine0[:5], None, *fine0[5:])
    l1 = Level(2, PAD, N0 // 2, *fine1)
    l2 = Level(1, PAD2, 64, c.at[0], c.at[1], c.at[2], *fine2)
    l3 = Level(2, PAD, 32, *fine3)
    l4 = Level(4, PAD, 16, *fine4)
    l5 = Level(8, PAD, 8, *fine5)
    lat, lon = lax.axis_index("lat"), lax.axis_index("lon")

    def device(dlon, dlat):
        return {"lon": lax.rem(lon + dlon + NLON, NLON), "lat": lax.rem(lat + dlat + NLAT, NLAT)}

    block = (lon // BLOCK) * BLOCK
    inner = lax.rem(lon, BLOCK)

    def mate1(d):
        return {"lon": block + lax.rem(inner + d, BLOCK), "lat": lat}

    def mate2(d):
        return device(BLOCK * (d // 4), d % 4)

    top = PAD + H
    loads = [
        pltpu.make_async_copy(x.at[:, pl.ds(128 * j, 128)], g.at[i, j, pl.ds(top, ROWS)], in_sem.at[i, j])
        for i, x in enumerate((b_in, e_in, s_in))
        for j in range(4)
    ]
    barrier = pltpu.get_barrier_semaphore()
    greeted = [device(*d) for d in HALO] + [device(0, 2), device(2, 0), device(-2, 0)]
    greeted += [mate1(d) for d in range(1, BLOCK)] + [mate2(d) for d in range(4, 16)]
    for k, other in enumerate(greeted):
        pl.semaphore_signal(barrier, inc=1, device_id=other, device_id_type=MESH)
        if k == len(HALO) - 1:
            for copy in loads:
                copy.start()

    def clear(ref, l):
        zero = jnp.zeros((l.pad, WIDE), F32)
        st(ref, 0, zero)
        st(ref, l.pad + l.n, zero)

    for l in (l0, l1):
        for ref in (l.wf, l.v, l.v2, l.q):
            clear(ref, l)
    for l in (l2, l3, l4, l5):
        for ref in (l.wf, l.v, l.v2, l.q, l.so):
            clear(ref, l)
    for ref in (l2.ae, l2.aw, l2.as_, l2.an):
        clear(ref, l2)
    for ref in (l5.e, l5.r):
        clear(ref, l5)

    for copy in loads:
        copy.wait()

    l8 = lanes((8, 128))
    for k in range(ROWS // 8):
        rows = slice(top + 8 * k, top + 8 * k + 8)
        first = [g[i, 0, rows] for i in range(3)]
        last = [g[i, 3, rows] for i in range(3)]
        x = jnp.where(l8 < 16, first[0], jnp.where(l8 < 32, roll_l(first[1], 16), roll_l(first[2], 32)))
        y = jnp.where(l8 >= 112, last[0], jnp.where(l8 >= 96, roll_l(last[1], -16), roll_l(last[2], -32)))
        pk[8 * k:8 * k + 8] = jnp.where(l8 < 64, x, y)

    own_rows = pl.ds(pl.multiple_of(PAD2 + lat * 16, 16), 16)

    for a in range(0, 16, 8):
        x = ld(g.at[1], top + 4 * a, 8, range(4), 4)
        for j in (1, 2, 3):
            x = x + ld(g.at[1], top + 4 * a + j, 8, range(4), 4)
        y = ld(g.at[2], top + 4 * a + 3, 8, range(4), 4)
        y = y + roll_l(y, -1)
        y = y + roll_l(y, -2)
        rows = pl.ds(pl.multiple_of(PAD2 + lat * 16 + a, 8), 8)
        c[1, 2, rows, :] = compact(x, 3)
        c[2, 2, rows, :] = compact(y, 0)

    pl.semaphore_wait(barrier, len(greeted))

    def send(src, dst, s_sem, r_sem, k, to):
        copy = pltpu.make_async_remote_copy(
            src_ref=src, dst_ref=dst, send_sem=s_sem.at[k], recv_sem=r_sem.at[k], device_id=to, device_id_type=MESH
        )
        copy.start()
        return copy

    halos = []
    for k, (dlon, dlat) in enumerate(HALO):
        first_row, count = {0: (0, ROWS), 1: (ROWS - H, H), -1: (0, H)}[dlat]
        to = {0: H, 1: 0, -1: H + ROWS}[dlat]
        if dlon == 0:
            src = g.at[:, pl.ds(0, 4), pl.ds(top + first_row, count)]
            dst = g.at[:, pl.ds(0, 4), pl.ds(PAD + to, count)]
        else:
            src = pk.at[pl.ds(first_row, count)]
            dst = (rw_ if dlon == 1 else re_).at[pl.ds(to, count)]
        halos.append(send(src, dst, a_send, a_recv, k, device(dlon, dlat)))

    def spread_lat(index, s_sem, r_sem):
        part = c.at[index, 2, own_rows]
        return [send(part, part, s_sem, r_sem, k, device(0, d)) for k, d in enumerate(SPREAD_LAT)]

    def spread_lon(index, s_sem, r_sem):
        rows = pl.ds(PAD2, 64)
        return [
            send(c.at[index, 2, rows], c.at[index, 2 - d, rows], s_sem, r_sem, 3 + k, device(d, 0))
            for k, d in enumerate(SPREAD_LON)
        ]

    conds = spread_lat(pl.ds(1, 2), cs_send, cs_recv)

    for copy in halos:
        copy.wait_recv()
    for copy in conds:
        copy.wait_recv()
    conds_lon = spread_lon(pl.ds(1, 2), cs_send, cs_recv)

    has_north = jnp.where(lat > 0, 1.0, 0.0).astype(F32)
    used = (l8 < 16) | (l8 >= 112)
    for k in range(N0 // 8):
        x = jnp.where(l8 < 64, re_[8 * k:8 * k + 8], rw_[8 * k:8 * k + 8])
        for i, other in ((0, 0.0), (1, 1.0), (2, 1.0)):
            y = x if i == 0 else jnp.where(l8 < 64, roll_l(x, -16 * i), roll_l(x, 16 * i))
            g[i, 4, PAD + 8 * k:PAD + 8 * k + 8, :] = jnp.where(used, y, other)
    g[2, :, PAD:PAD + H] = g[2, :, PAD:PAD + H] * has_north

    def bounds(halo, own):
        return jnp.where(lat > 0, 0, halo), jnp.where(lat < NLAT - 1, 2 * halo + own, halo + own)

    coeffs(l0, 16, bounds(H, ROWS), True)
    sweep(l0, l0.wf, l0.v, True, 0, N0, 16)
    coarsen(l0, l1)
    remainder(l0, 16)
    coeffs(l1, 16, bounds(H // 2, ROWS // 2))
    restrict(l0, l1)
    sweep(l1, l1.wf, l1.v, True, 0, 48, 16)
    remainder(l1, 16)
    for a in range(0, 16, 8):
        x = ld(l1.r, PAD + 8 + 2 * a, 8, range(4), 2) + ld(l1.r, PAD + 9 + 2 * a, 8, range(4), 2)
        rows = pl.ds(pl.multiple_of(PAD2 + lat * 16 + a, 8), 8)
        c[0, 2, rows, :] = compact(x + roll_l(x, -2), 0)
    fields = spread_lat(0, fs_send, fs_recv)

    for copy in conds_lon:
        copy.wait_recv()
    coeffs(l2, 16)
    coarsen(l2, l3)
    coeffs(l3, 16)
    coarsen(l3, l4)
    coeffs(l4, 16)
    coarsen(l4, l5)
    coeffs(l5, 8)


    def twice(l, v, source, r0, count, ch, blocks=ALL):
        sweep(l, v, l.v2, source, r0, count, ch, blocks)
        sweep(l, l.v2, v, source, r0, count, ch, blocks)

    def rise_coarse(name, source):
        u = [getattr(l, name) for l in (l0, l1, l2, l3, l4, l5)]
        twice(l5, u[5], source, 0, 8, 8, MID)
        prolong(l5, l4, u[5], u[4], 0, 8, source, MID)
        twice(l4, u[4], source, 0, 16, 16, MID)
        prolong(l4, l3, u[4], u[3], 0, 16, source, MID)
        twice(l3, u[3], source, 0, 32, 16, MID)
        near = lat * 8 - 4
        prolong(l3, l2, u[3], u[2], near, 16, source, MID)
        near = pl.multiple_of(lat * 16 - 8, 8)
        twice(l2, u[2], source, near, 32, 16, MID)

    def rise_fine(name, source):
        u = [getattr(l, name) for l in (l0, l1, l2)]
        for i in range(3):
            e = expand(u[2], PAD2 + lat * 16 - 4 + 8 * i)
            spread_rows(u[1], PAD + 16 * i, e, source)
        twice(l1, u[1], source, 0, 48, 16)
        prolong(l1, l0, u[1], u[0], 0, 48, source)
        twice(l0, u[0], source, 8, 80, 16)

    def applied(v, out, sums, n):
        def body(r, carry):
            x, av = operator(l0, v, top + r, 16)
            x, av = x[:, :COLS], av[:, :COLS]
            out[pl.ds(r, 16)] = av
            more = sums(pl.ds(r, 16), ld(l0.f, top + r, 16, range(4)), x, av)
            return tuple(y + (z[:8] + z[8:]) for y, z in zip(carry, more))

        carry = (jnp.zeros((8, COLS), F32),) * n
        for r in range(0, ROWS, 16):
            carry = body(r, carry)
        return carry

    st(l5.q, PAD, jnp.ones((8, WIDE), F32))
    rise_coarse("q", False)
    for copy in halos + conds:
        copy.wait_send()
    for copy in fields:
        copy.wait_recv()
    fields_lon = spread_lon(0, fs_send, fs_recv)
    rise_fine("q", False)
    for copy in fields + conds_lon:
        copy.wait_send()
    sums_q = applied(l0.q, ag, lambda rows, b, v, av: (b * v, v * av), 2)

    for copy in fields_lon:
        copy.wait_recv()

    def first(r):
        st(l2.wf, PAD2 + r, ld(l2.w, PAD2 + r, 16) * ld(l2.f, PAD2 + r, 16))

    loop(0, 64, 16, first)
    sweep(l2, l2.wf, l2.v, True, 0, 64, 16)
    remainder(l2, 16)
    for l, coarse in ((l2, l3), (l3, l4), (l4, l5)):
        restrict(l, coarse)
        sweep(coarse, coarse.wf, coarse.v, True, 0, coarse.n, min(16, coarse.n))
        remainder(coarse, min(16, coarse.n))

    x = pair(l5.r, PAD, 8, 0) + pair(l5.r, PAD, 8, 1)
    f6 = x + roll_l(x, -8)
    x = pair(l5.e, PAD, 8, 0) + pair(l5.e, PAD, 8, 1)
    e6 = roll_l(x, -8)
    x = pair(l5.so, PAD, 8, 1)
    s6 = x + roll_l(x, -8)
    row6, lane6 = rows_of((8, WIDE)), lanes((8, WIDE))
    west6 = roll_l(e6, 16)
    north6 = jnp.where(row6 == 0, 0.0, pltpu.roll(s6, 1, 0))
    w6 = jnp.where(row6 < 4, OMEGA / (((e6 + west6) + s6) + north6), 0.0)
    ae6, aw6, as6, an6, wf6 = w6 * e6, w6 * west6, w6 * s6, w6 * north6, w6 * f6
    field = wf6
    for _ in range(COARSE_SWEEPS - 1):
        x = ae6 * roll_l(field, -16) + aw6 * roll_l(field, 16)
        y = as6 * pltpu.roll(field, 7, 0) + an6 * pltpu.roll(field, 1, 0)
        field = (((1.0 - OMEGA) * field + wf6) + y) + x
    lon6 = e6 * (field - roll_l(field, -16)) + west6 * (field - roll_l(field, 16))
    lat6 = s6 * (field - pltpu.roll(field, 7, 0)) + north6 * (field - pltpu.roll(field, 1, 0))
    left = f6 - (lon6 + lat6)
    mine = ((lane6 & 15) == 0) & (lane6 >= 256) & (lane6 < 384)
    left = jnp.where(mine & (row6 == lat), left, 0.0)[:, 256:384]
    last = jnp.where(mine & (row6 == 3) & (lat == 3), s6, 0.0)[:, 256:384]

    e = jnp.where((lane6 & 8) == 0, field, roll_l(field, 8))
    for odd in (0, 1):
        st(l5.r, odd, e, ALL, 2)
    st(l5.v, PAD, ld(l5.v, PAD, 8) + ld(l5.r, 0, 8))
    rise_coarse("v", True)
    rise_fine("v", True)
    sums_v = applied(l0.v, a0, lambda rows, b, v, av: (b * v, v * av, v * ag[rows]), 3)

    def wait_all(got, sem):
        pltpu.make_async_copy(got, got, sem.at[0]).wait()

    def fold(x):
        return (x[:, 0:128] + x[:, 128:256]) + (x[:, 256:384] + x[:, 384:512])

    seven = [left, last, fold(sums_v[0]), fold(sums_q[0]), fold(sums_v[1]), fold(sums_v[2]), fold(sums_q[1])]
    row = rows_of((8, 128))
    total = jnp.zeros((8, 128), F32)
    for i, x in enumerate(seven):
        total = jnp.where(row == i, jnp.sum(x, axis=0, keepdims=True), total)
    t1[...] = total
    for d in range(1, 16):
        send(t1, got1.at[d - 1], c1_send, c1_recv, 0, mate1(d))
    for copy in fields_lon:
        copy.wait_send()
    wait_all(got1, c1_recv)

    def gathered(total, got):
        parts = [total] + [got[d] for d in range(15)]
        while len(parts) > 1:
            parts = [x + y for x, y in zip(parts[::2], parts[1::2])]
        return parts[0]

    total = gathered(total, got1)
    t2[...] = total
    for d in range(1, 16):
        send(t2, got2.at[d - 1], c2_send, c2_recv, 0, mate2(d))
    wait_all(got1, c1_send)
    wait_all(got2, c2_recv)
    total = gathered(total, got2)
    for by in (64, 32, 16, 8, 4, 2, 1):
        total = total + pltpu.roll(total, by, 1)
    n_left, n_last, bv, bq, vav, vaq, qaq = [total[i:i + 1] for i in range(7)]
    const = n_left / n_last
    step = (bv + const * bq) / ((vav + (2.0 * const) * vaq) + (const * const) * qaq)
    both = jnp.concatenate([step * const] * 4, axis=1)
    step = jnp.concatenate([step] * 4, axis=1)

    for r in range(0, ROWS, 16):
        rows = pl.ds(r, 16)
        sol[rows] = step * ld(l0.v, top + r, 16, range(4)) + both * ld(l0.q, top + r, 16, range(4))
        res[rows] = ld(l0.f, top + r, 16, range(4)) - (step * a0[rows] + both * ag[rows])
    wait_all(got2, c2_send)


def body(guidance, cond_lon, cond_lat):
    def vm(*shape):
        return pltpu.VMEM(shape, F32)

    def wide(n, count):
        return [vm(5, n, 128)] * count

    dma = pltpu.SemaphoreType.DMA
    scratch = [vm(3, 5, N0 + 2 * PAD, 128), vm(ROWS, 128), vm(N0, 128), vm(N0, 128), vm(ROWS, COLS), vm(ROWS, COLS)]
    scratch += [vm(3, 5, 64 + 2 * PAD2, 128), vm(8, 128), vm(15, 8, 128), vm(8, 128), vm(15, 8, 128)]
    scratch += wide(N0 + 2 * PAD, 9) + wide(N0 // 2 + 2 * PAD, 13) + wide(64 + 2 * PAD2, 10)
    scratch += wide(32 + 2 * PAD, 13) + wide(16 + 2 * PAD, 13) + wide(8 + 2 * PAD, 14)
    scratch += [dma((3, 4)), dma((8,)), dma((8,)), dma((7,)), dma((7,)), dma((7,)), dma((7,))] + [dma((1,))] * 4
    return pl.pallas_call(
        kernel,
        out_shape=(jax.ShapeDtypeStruct((ROWS, COLS), F32),) * 2,
        in_specs=[pl.BlockSpec(memory_space=pltpu.HBM)] * 3,
        out_specs=(pl.BlockSpec(memory_space=pltpu.VMEM),) * 2,
        scratch_shapes=scratch,
        compiler_params=pltpu.CompilerParams(
            collective_id=0, has_side_effects=True, vmem_limit_bytes=63 * 1024 * 1024
        ),
        cost_estimate=pl.CostEstimate(flops=10_000_000, bytes_accessed=655360, transcendentals=0),
    )(guidance, cond_lon, cond_lat)


def solution(mesh):
    spec = P("lat", "lon")
    return jax.shard_map(body, mesh=mesh, in_specs=(spec,) * 3, out_specs=(spec,) * 2, check_vma=False)
```

```python
import jax
import jax.numpy as jnp
from jax import lax
from jax.experimental import pallas as pl
from jax.experimental.pallas import tpu as pltpu
from jax.sharding import PartitionSpec as P

OMEGA = 0.8
COARSE_SWEEPS = 8
NLAT, NLON, BLOCK = 4, 64, 8
ROWS, COLS = 64, 512
H = 16
PAD = 8
PAD2 = 16
N0 = ROWS + 2 * H
WIDE = COLS + 128
ALL = range(5)
MID = range(1, 4)
MESH = pl.DeviceIdType.MESH
F32 = jnp.float32

HALO = ((0, 1), (0, -1), (1, 0), (-1, 0), (1, 1), (1, -1), (-1, 1), (-1, -1))
SPREAD_LAT = (1, 2, 3)
SPREAD_LON = (1, -1, 2, -2)


def lanes(shape):
    return lax.broadcasted_iota(jnp.int32, shape, len(shape) - 1)


def rows_of(shape):
    return lax.broadcasted_iota(jnp.int32, shape, 0)


def roll_l(x, by):
    return pltpu.roll(x, by % x.shape[1], 1)


def ld(ref, start, n, blocks=ALL, stride=None):
    rows = pl.ds(start, n) if stride is None else pl.ds(start, n, stride=stride)
    return jnp.concatenate([ref[j, rows, :] for j in blocks], axis=1)


def st(ref, start, x, blocks=ALL, stride=None):
    n = x.shape[0]
    rows = pl.ds(start, n) if stride is None else pl.ds(start, n, stride=stride)
    for i, j in enumerate(blocks):
        ref[j, rows, :] = x[:, 128 * i:128 * (i + 1)]


def loop(r0, count, ch, body):
    for k in range(count // ch):
        body(r0 + k * ch)


class Level:
    def __init__(self, s, pad, n, f, e, so, west, ae, aw, as_, an, w, wf, v, v2, q, r=None):
        self.s, self.pad, self.n = s, pad, n
        self.f, self.e, self.so, self.west = f, e, so, west
        self.ae, self.aw, self.as_, self.an, self.w, self.wf = ae, aw, as_, an, w, wf
        self.v, self.v2, self.q, self.r = v, v2, q, v2 if r is None else r


def coeffs(l, ch, keep=None, source=False):
    def body(r):
        p = l.pad + r
        e, so, no = ld(l.e, p, ch), ld(l.so, p, ch), ld(l.so, p - 1, ch)
        we = roll_l(e, l.s)
        wk = OMEGA / (((e + we) + so) + no)
        if keep is not None:
            row = rows_of(wk.shape) + r
            wk = jnp.where((row >= keep[0]) & (row < keep[1]), wk, 0.0)
        st(l.west, p, we)
        st(l.ae, p, wk * e)
        st(l.aw, p, wk * we)
        st(l.as_, p, wk * so)
        st(l.an, p, wk * no)
        if source:
            st(l.wf, p, wk * ld(l.f, p, ch))
        else:
            st(l.w, p, wk)

    loop(0, l.n, ch, body)


def sweep(l, src, dst, source, r0, count, ch, blocks=ALL):
    def body(r):
        p = l.pad + r
        v = ld(src, p, ch, blocks)
        x = ld(l.ae, p, ch, blocks) * roll_l(v, -l.s) + ld(l.aw, p, ch, blocks) * roll_l(v, l.s)
        y = ld(l.as_, p, ch, blocks) * ld(src, p + 1, ch, blocks) + ld(l.an, p, ch, blocks) * ld(src, p - 1, ch, blocks)
        z = (1.0 - OMEGA) * v
        if source:
            z = z + ld(l.wf, p, ch, blocks)
        st(dst, p, (y + z) + x, blocks)

    loop(r0, count, ch, body)


def operator(l, v, p, ch):
    x = ld(v, p, ch)
    lon = ld(l.e, p, ch) * (x - roll_l(x, -l.s)) + ld(l.west, p, ch) * (x - roll_l(x, l.s))
    lat = ld(l.so, p, ch) * (x - ld(v, p + 1, ch)) + ld(l.so, p - 1, ch) * (x - ld(v, p - 1, ch))
    return x, lat + lon


def remainder(l, ch):
    def body(r):
        p = l.pad + r
        st(l.r, p, ld(l.f, p, ch) - operator(l, l.v, p, ch)[1])

    loop(0, l.n, ch, body)


def pair(ref, start, n, odd, blocks=ALL):
    return ld(ref, start + odd, n, blocks, 2)


def restrict(l, c):
    ch = min(16, c.n)

    def body(a):
        x = pair(l.r, l.pad + 2 * a, ch, 0) + pair(l.r, l.pad + 2 * a, ch, 1)
        x = x + roll_l(x, -l.s)
        st(c.f, c.pad + a, x)
        st(c.wf, c.pad + a, x * ld(c.w, c.pad + a, ch))

    for a in range(0, c.n, ch):
        body(a)


def coarsen(l, c):
    ch = min(16, c.n)
    for a in range(0, c.n, ch):
        x = pair(l.e, l.pad + 2 * a, ch, 0) + pair(l.e, l.pad + 2 * a, ch, 1)
        st(c.e, c.pad + a, roll_l(x, -l.s))
        y = pair(l.so, l.pad + 2 * a, ch, 1)
        st(c.so, c.pad + a, y + roll_l(y, -l.s))


def spread_rows(v, start, e, add, blocks=ALL):
    for odd in (0, 1):
        x = e
        if add:
            x = x + ld(v, start + odd, e.shape[0], blocks, 2)
        st(v, start + odd, x, blocks, 2)


def prolong(c, l, src, dst, a0, n, add, blocks=ALL):
    for a in range(0, n, 8):
        e = ld(src, c.pad + a0 + a, 8, blocks)
        e = jnp.where((lanes(e.shape) & l.s) == 0, e, roll_l(e, l.s))
        spread_rows(dst, l.pad + 2 * (a0 + a), e, add, blocks)


def pick(x, index):
    return jnp.take_along_axis(x, index, axis=1, mode="promise_in_bounds")


def compact(x, offset):
    l = lanes((8, 128))
    index = (l % 32) * 4 + offset
    out = pick(x[:, 384:512], index)
    for j in (2, 1, 0):
        out = jnp.where(l < 32 * (j + 1), pick(x[:, 128 * j:128 * (j + 1)], index), out)
    return out


def expand(x, base):
    l = lanes((8, 128))
    q = l // 4
    own = x[2, pl.ds(base, 8), :]
    parts = [pick(own, q + 32 * j) for j in range(4)]
    east = pick(x[3, pl.ds(base, 8), :], q)
    west = pick(x[1, pl.ds(base, 8), :], q + 96)
    return jnp.concatenate(parts + [jnp.where(l < 64, east, west)], axis=1)


def kernel(
    b_in, e_in, s_in, sol, res,
    g, pk, re_, rw_, a0, ag, c, t1, got1, t2, got2, t3, got3,
    *rest,
):
    fine0, fine1, fine2, fine3, fine4, fine5 = rest[:9], rest[9:22], rest[22:32], rest[32:45], rest[45:58], rest[58:72]
    in_sem, a_send, a_recv, cs_send, cs_recv, fs_send, fs_recv, c1_send, c1_recv, c2_send, c2_recv, c3_send, c3_recv = rest[72:]

    l0 = Level(1, PAD, N0, g.at[0], g.at[1], g.at[2], *fine0[:5], None, *fine0[5:])
    l1 = Level(2, PAD, N0 // 2, *fine1)
    l2 = Level(1, PAD2, 64, c.at[0], c.at[1], c.at[2], *fine2)
    l3 = Level(2, PAD, 32, *fine3)
    l4 = Level(4, PAD, 16, *fine4)
    l5 = Level(8, PAD, 8, *fine5)
    lat, lon = lax.axis_index("lat"), lax.axis_index("lon")

    def device(dlon, dlat):
        return {"lon": lax.rem(lon + dlon + NLON, NLON), "lat": lax.rem(lat + dlat + NLAT, NLAT)}

    block = (lon // BLOCK) * BLOCK
    inner = lax.rem(lon, BLOCK)

    def mate1(d):
        return device(0, d)

    def mate2(d):
        return {"lon": block + lax.rem(inner + d, BLOCK), "lat": lat}

    def mate3(d):
        return device(BLOCK * d, 0)

    top = PAD + H
    loads = [
        pltpu.make_async_copy(x.at[:, pl.ds(128 * j, 128)], g.at[i, j, pl.ds(top, ROWS)], in_sem.at[i, j])
        for i, x in enumerate((b_in, e_in, s_in))
        for j in range(4)
    ]
    barrier = pltpu.get_barrier_semaphore()
    greeted = [device(*d) for d in HALO] + [device(0, 2), device(2, 0), device(-2, 0)]
    greeted += [mate2(d) for d in range(1, 8)] + [mate3(d) for d in range(1, 8)]
    for k, other in enumerate(greeted):
        pl.semaphore_signal(barrier, inc=1, device_id=other, device_id_type=MESH)
        if k == len(HALO) - 1:
            for copy in loads:
                copy.start()

    def clear(ref, l):
        zero = jnp.zeros((l.pad, WIDE), F32)
        st(ref, 0, zero)
        st(ref, l.pad + l.n, zero)

    for l in (l0, l1):
        for ref in (l.wf, l.v, l.v2, l.q):
            clear(ref, l)
    for l in (l2, l3, l4, l5):
        for ref in (l.wf, l.v, l.v2, l.q, l.so):
            clear(ref, l)
    for ref in (l2.ae, l2.aw, l2.as_, l2.an):
        clear(ref, l2)
    for ref in (l5.e, l5.r):
        clear(ref, l5)

    for copy in loads:
        copy.wait()

    l8 = lanes((8, 128))
    for k in range(ROWS // 8):
        rows = slice(top + 8 * k, top + 8 * k + 8)
        first = [g[i, 0, rows] for i in range(3)]
        last = [g[i, 3, rows] for i in range(3)]
        x = jnp.where(l8 < 16, first[0], jnp.where(l8 < 32, roll_l(first[1], 16), roll_l(first[2], 32)))
        y = jnp.where(l8 >= 112, last[0], jnp.where(l8 >= 96, roll_l(last[1], -16), roll_l(last[2], -32)))
        pk[8 * k:8 * k + 8] = jnp.where(l8 < 64, x, y)

    own_rows = pl.ds(pl.multiple_of(PAD2 + lat * 16, 16), 16)

    for a in range(0, 16, 8):
        x = ld(g.at[1], top + 4 * a, 8, range(4), 4)
        for j in (1, 2, 3):
            x = x + ld(g.at[1], top + 4 * a + j, 8, range(4), 4)
        y = ld(g.at[2], top + 4 * a + 3, 8, range(4), 4)
        y = y + roll_l(y, -1)
        y = y + roll_l(y, -2)
        rows = pl.ds(pl.multiple_of(PAD2 + lat * 16 + a, 8), 8)
        c[1, 2, rows, :] = compact(x, 3)
        c[2, 2, rows, :] = compact(y, 0)

    pl.semaphore_wait(barrier, len(greeted))

    def send(src, dst, s_sem, r_sem, k, to):
        copy = pltpu.make_async_remote_copy(
            src_ref=src, dst_ref=dst, send_sem=s_sem.at[k], recv_sem=r_sem.at[k], device_id=to, device_id_type=MESH
        )
        copy.start()
        return copy

    halos = []
    for k, (dlon, dlat) in enumerate(HALO):
        first_row, count = {0: (0, ROWS), 1: (ROWS - H, H), -1: (0, H)}[dlat]
        to = {0: H, 1: 0, -1: H + ROWS}[dlat]
        if dlon == 0:
            src = g.at[:, pl.ds(0, 4), pl.ds(top + first_row, count)]
            dst = g.at[:, pl.ds(0, 4), pl.ds(PAD + to, count)]
        else:
            src = pk.at[pl.ds(first_row, count)]
            dst = (rw_ if dlon == 1 else re_).at[pl.ds(to, count)]
        halos.append(send(src, dst, a_send, a_recv, k, device(dlon, dlat)))

    def spread_lat(index, s_sem, r_sem):
        part = c.at[index, 2, own_rows]
        return [send(part, part, s_sem, r_sem, k, device(0, d)) for k, d in enumerate(SPREAD_LAT)]

    def spread_lon(index, s_sem, r_sem):
        rows = pl.ds(PAD2, 64)
        return [
            send(c.at[index, 2, rows], c.at[index, 2 - d, rows], s_sem, r_sem, 3 + k, device(d, 0))
            for k, d in enumerate(SPREAD_LON)
        ]

    conds = spread_lat(pl.ds(1, 2), cs_send, cs_recv)

    for copy in halos:
        copy.wait_recv()
    for copy in conds:
        copy.wait_recv()
    conds_lon = spread_lon(pl.ds(1, 2), cs_send, cs_recv)

    has_north = jnp.where(lat > 0, 1.0, 0.0).astype(F32)
    used = (l8 < 16) | (l8 >= 112)
    for k in range(N0 // 8):
        x = jnp.where(l8 < 64, re_[8 * k:8 * k + 8], rw_[8 * k:8 * k + 8])
        for i, other in ((0, 0.0), (1, 1.0), (2, 1.0)):
            y = x if i == 0 else jnp.where(l8 < 64, roll_l(x, -16 * i), roll_l(x, 16 * i))
            g[i, 4, PAD + 8 * k:PAD + 8 * k + 8, :] = jnp.where(used, y, other)
    g[2, :, PAD:PAD + H] = g[2, :, PAD:PAD + H] * has_north

    def bounds(halo, own):
        return jnp.where(lat > 0, 0, halo), jnp.where(lat < NLAT - 1, 2 * halo + own, halo + own)

    coeffs(l0, 16, bounds(H, ROWS), True)
    sweep(l0, l0.wf, l0.v, True, 0, N0, 16)
    coarsen(l0, l1)
    remainder(l0, 16)
    coeffs(l1, 16, bounds(H // 2, ROWS // 2))
    restrict(l0, l1)
    sweep(l1, l1.wf, l1.v, True, 0, 48, 16)
    remainder(l1, 16)
    for a in range(0, 16, 8):
        x = ld(l1.r, PAD + 8 + 2 * a, 8, range(4), 2) + ld(l1.r, PAD + 9 + 2 * a, 8, range(4), 2)
        rows = pl.ds(pl.multiple_of(PAD2 + lat * 16 + a, 8), 8)
        c[0, 2, rows, :] = compact(x + roll_l(x, -2), 0)
    fields = spread_lat(0, fs_send, fs_recv)

    for copy in conds_lon:
        copy.wait_recv()
    coeffs(l2, 16)
    coarsen(l2, l3)
    coeffs(l3, 16)
    coarsen(l3, l4)
    coeffs(l4, 16)
    coarsen(l4, l5)
    coeffs(l5, 8)


    def twice(l, v, source, r0, count, ch, blocks=ALL):
        sweep(l, v, l.v2, source, r0, count, ch, blocks)
        sweep(l, l.v2, v, source, r0, count, ch, blocks)

    def rise_coarse(name, source):
        u = [getattr(l, name) for l in (l0, l1, l2, l3, l4, l5)]
        twice(l5, u[5], source, 0, 8, 8, MID)
        prolong(l5, l4, u[5], u[4], 0, 8, source, MID)
        twice(l4, u[4], source, 0, 16, 16, MID)
        prolong(l4, l3, u[4], u[3], 0, 16, source, MID)
        twice(l3, u[3], source, 0, 32, 16, MID)
        near = lat * 8 - 4
        prolong(l3, l2, u[3], u[2], near, 16, source, MID)
        near = pl.multiple_of(lat * 16 - 8, 8)
        twice(l2, u[2], source, near, 32, 16, MID)

    def rise_fine(name, source):
        u = [getattr(l, name) for l in (l0, l1, l2)]
        for i in range(3):
            e = expand(u[2], PAD2 + lat * 16 - 4 + 8 * i)
            spread_rows(u[1], PAD + 16 * i, e, source)
        twice(l1, u[1], source, 0, 48, 16)
        prolong(l1, l0, u[1], u[0], 0, 48, source)
        twice(l0, u[0], source, 8, 80, 16)

    def applied(v, out, sums, n):
        def body(r, carry):
            x, av = operator(l0, v, top + r, 16)
            x, av = x[:, :COLS], av[:, :COLS]
            out[pl.ds(r, 16)] = av
            more = sums(pl.ds(r, 16), ld(l0.f, top + r, 16, range(4)), x, av)
            return tuple(y + (z[:8] + z[8:]) for y, z in zip(carry, more))

        carry = (jnp.zeros((8, COLS), F32),) * n
        for r in range(0, ROWS, 16):
            carry = body(r, carry)
        return carry

    st(l5.q, PAD, jnp.ones((8, WIDE), F32))
    rise_coarse("q", False)
    for copy in halos + conds:
        copy.wait_send()
    for copy in fields:
        copy.wait_recv()
    fields_lon = spread_lon(0, fs_send, fs_recv)
    rise_fine("q", False)
    for copy in fields + conds_lon:
        copy.wait_send()
    sums_q = applied(l0.q, ag, lambda rows, b, v, av: (b * v, v * av), 2)

    for copy in fields_lon:
        copy.wait_recv()

    def first(r):
        st(l2.wf, PAD2 + r, ld(l2.w, PAD2 + r, 16) * ld(l2.f, PAD2 + r, 16))

    loop(0, 64, 16, first)
    sweep(l2, l2.wf, l2.v, True, 0, 64, 16)
    remainder(l2, 16)
    for l, coarse in ((l2, l3), (l3, l4), (l4, l5)):
        restrict(l, coarse)
        sweep(coarse, coarse.wf, coarse.v, True, 0, coarse.n, min(16, coarse.n))
        remainder(coarse, min(16, coarse.n))

    x = pair(l5.r, PAD, 8, 0) + pair(l5.r, PAD, 8, 1)
    f6 = x + roll_l(x, -8)
    x = pair(l5.e, PAD, 8, 0) + pair(l5.e, PAD, 8, 1)
    e6 = roll_l(x, -8)
    x = pair(l5.so, PAD, 8, 1)
    s6 = x + roll_l(x, -8)
    row6, lane6 = rows_of((8, WIDE)), lanes((8, WIDE))
    west6 = roll_l(e6, 16)
    north6 = jnp.where(row6 == 0, 0.0, pltpu.roll(s6, 1, 0))
    w6 = jnp.where(row6 < 4, OMEGA / (((e6 + west6) + s6) + north6), 0.0)
    ae6, aw6, as6, an6, wf6 = w6 * e6, w6 * west6, w6 * s6, w6 * north6, w6 * f6
    field = wf6
    for _ in range(COARSE_SWEEPS - 1):
        x = ae6 * roll_l(field, -16) + aw6 * roll_l(field, 16)
        y = as6 * pltpu.roll(field, 7, 0) + an6 * pltpu.roll(field, 1, 0)
        field = (((1.0 - OMEGA) * field + wf6) + y) + x
    lon6 = e6 * (field - roll_l(field, -16)) + west6 * (field - roll_l(field, 16))
    lat6 = s6 * (field - pltpu.roll(field, 7, 0)) + north6 * (field - pltpu.roll(field, 1, 0))
    left = f6 - (lon6 + lat6)
    mine = ((lane6 & 15) == 0) & (lane6 >= 256) & (lane6 < 384)
    left = jnp.where(mine & (row6 == lat), left, 0.0)[:, 256:384]
    last = jnp.where(mine & (row6 == 3) & (lat == 3), s6, 0.0)[:, 256:384]

    e = jnp.where((lane6 & 8) == 0, field, roll_l(field, 8))
    for odd in (0, 1):
        st(l5.r, odd, e, ALL, 2)
    st(l5.v, PAD, ld(l5.v, PAD, 8) + ld(l5.r, 0, 8))
    rise_coarse("v", True)
    rise_fine("v", True)
    sums_v = applied(l0.v, a0, lambda rows, b, v, av: (b * v, v * av, v * ag[rows]), 3)

    def wait_all(got, sem):
        pltpu.make_async_copy(got, got, sem.at[0]).wait()

    def fold(x):
        return (x[:, 0:128] + x[:, 128:256]) + (x[:, 256:384] + x[:, 384:512])

    seven = [left, last, fold(sums_v[0]), fold(sums_q[0]), fold(sums_v[1]), fold(sums_v[2]), fold(sums_q[1])]
    row = rows_of((8, 128))
    total = jnp.zeros((8, 128), F32)
    for i, x in enumerate(seven):
        total = jnp.where(row == i, jnp.sum(x, axis=0, keepdims=True), total)
    def gathered(total, got, n):
        parts = [total] + [got[d] for d in range(n)]
        while len(parts) > 1:
            parts = [x + y for x, y in zip(parts[::2], parts[1::2])]
        return parts[0]

    stages = (
        (3, mate1, t1, got1, c1_send, c1_recv),
        (7, mate2, t2, got2, c2_send, c2_recv),
        (7, mate3, t3, got3, c3_send, c3_recv),
    )
    for n, mate, mine_, got, s_sem, r_sem in stages:
        mine_[...] = total
        for d in range(1, n + 1):
            send(mine_, got.at[d - 1], s_sem, r_sem, 0, mate(d))
        if n == 3:
            for copy in fields_lon:
                copy.wait_send()
        wait_all(got, r_sem)
        total = gathered(total, got, n)
    for by in (64, 32, 16, 8, 4, 2, 1):
        total = total + pltpu.roll(total, by, 1)
    n_left, n_last, bv, bq, vav, vaq, qaq = [total[i:i + 1] for i in range(7)]
    const = n_left / n_last
    step = (bv + const * bq) / ((vav + (2.0 * const) * vaq) + (const * const) * qaq)
    both = jnp.concatenate([step * const] * 4, axis=1)
    step = jnp.concatenate([step] * 4, axis=1)

    for r in range(0, ROWS, 16):
        rows = pl.ds(r, 16)
        sol[rows] = step * ld(l0.v, top + r, 16, range(4)) + both * ld(l0.q, top + r, 16, range(4))
        res[rows] = ld(l0.f, top + r, 16, range(4)) - (step * a0[rows] + both * ag[rows])
    wait_all(got1, c1_send)
    wait_all(got2, c2_send)
    wait_all(got3, c3_send)


def body(guidance, cond_lon, cond_lat):
    def vm(*shape):
        return pltpu.VMEM(shape, F32)

    def wide(n, count):
        return [vm(5, n, 128)] * count

    dma = pltpu.SemaphoreType.DMA
    scratch = [vm(3, 5, N0 + 2 * PAD, 128), vm(ROWS, 128), vm(N0, 128), vm(N0, 128), vm(ROWS, COLS), vm(ROWS, COLS)]
    scratch += [vm(3, 5, 64 + 2 * PAD2, 128), vm(8, 128), vm(3, 8, 128), vm(8, 128), vm(7, 8, 128), vm(8, 128), vm(7, 8, 128)]
    scratch += wide(N0 + 2 * PAD, 9) + wide(N0 // 2 + 2 * PAD, 13) + wide(64 + 2 * PAD2, 10)
    scratch += wide(32 + 2 * PAD, 13) + wide(16 + 2 * PAD, 13) + wide(8 + 2 * PAD, 14)
    scratch += [dma((3, 4)), dma((8,)), dma((8,)), dma((7,)), dma((7,)), dma((7,)), dma((7,))] + [dma((1,))] * 6
    return pl.pallas_call(
        kernel,
        out_shape=(jax.ShapeDtypeStruct((ROWS, COLS), F32),) * 2,
        in_specs=[pl.BlockSpec(memory_space=pltpu.HBM)] * 3,
        out_specs=(pl.BlockSpec(memory_space=pltpu.VMEM),) * 2,
        scratch_shapes=scratch,
        compiler_params=pltpu.CompilerParams(
            collective_id=0, has_side_effects=True, vmem_limit_bytes=63 * 1024 * 1024
        ),
        cost_estimate=pl.CostEstimate(flops=10_000_000, bytes_accessed=655360, transcendentals=0),
    )(guidance, cond_lon, cond_lat)


def solution(mesh):
    spec = P("lat", "lon")
    return jax.shard_map(body, mesh=mesh, in_specs=(spec,) * 3, out_specs=(spec,) * 2, check_vma=False)
```

```python
import jax
import jax.numpy as jnp
from jax import lax
from jax.experimental import pallas as pl
from jax.experimental.pallas import tpu as pltpu
from jax.sharding import PartitionSpec as P

OMEGA = 0.8
COARSE_SWEEPS = 8
NLAT, NLON, BLOCK = 4, 64, 16
ROWS, COLS = 64, 512
H = 16
PAD = 8
PAD2 = 16
N0 = ROWS + 2 * H
WIDE = COLS + 128
ALL = range(5)
MID = range(1, 4)
MESH = pl.DeviceIdType.MESH
F32 = jnp.float32

SPREAD_LAT = (1, 2, 3)
SPREAD_LON = (1, -1, 2, -2)


def lanes(shape):
    return lax.broadcasted_iota(jnp.int32, shape, len(shape) - 1)


def rows_of(shape):
    return lax.broadcasted_iota(jnp.int32, shape, 0)


def roll_l(x, by):
    return pltpu.roll(x, by % x.shape[1], 1)


def ld(ref, start, n, blocks=ALL, stride=None):
    rows = pl.ds(start, n) if stride is None else pl.ds(start, n, stride=stride)
    return jnp.concatenate([ref[j, rows, :] for j in blocks], axis=1)


def st(ref, start, x, blocks=ALL, stride=None):
    n = x.shape[0]
    rows = pl.ds(start, n) if stride is None else pl.ds(start, n, stride=stride)
    for i, j in enumerate(blocks):
        ref[j, rows, :] = x[:, 128 * i:128 * (i + 1)]


def loop(r0, count, ch, body):
    for k in range(count // ch):
        body(r0 + k * ch)


class Level:
    def __init__(self, s, pad, n, f, e, so, west, ae, aw, as_, an, w, wf, v, v2, q, r=None):
        self.s, self.pad, self.n = s, pad, n
        self.f, self.e, self.so, self.west = f, e, so, west
        self.ae, self.aw, self.as_, self.an, self.w, self.wf = ae, aw, as_, an, w, wf
        self.v, self.v2, self.q, self.r = v, v2, q, v2 if r is None else r


def coeffs(l, ch, keep=None, source=False):
    def body(r):
        p = l.pad + r
        e, so, no = ld(l.e, p, ch), ld(l.so, p, ch), ld(l.so, p - 1, ch)
        we = roll_l(e, l.s)
        wk = OMEGA / (((e + we) + so) + no)
        if keep is not None:
            row = rows_of(wk.shape) + r
            wk = jnp.where((row >= keep[0]) & (row < keep[1]), wk, 0.0)
        st(l.west, p, we)
        st(l.ae, p, wk * e)
        st(l.aw, p, wk * we)
        st(l.as_, p, wk * so)
        st(l.an, p, wk * no)
        if source:
            st(l.wf, p, wk * ld(l.f, p, ch))
        else:
            st(l.w, p, wk)

    loop(0, l.n, ch, body)


def sweep(l, src, dst, source, r0, count, ch, blocks=ALL):
    def body(r):
        p = l.pad + r
        v = ld(src, p, ch, blocks)
        x = ld(l.ae, p, ch, blocks) * roll_l(v, -l.s) + ld(l.aw, p, ch, blocks) * roll_l(v, l.s)
        y = ld(l.as_, p, ch, blocks) * ld(src, p + 1, ch, blocks) + ld(l.an, p, ch, blocks) * ld(src, p - 1, ch, blocks)
        z = (1.0 - OMEGA) * v
        if source:
            z = z + ld(l.wf, p, ch, blocks)
        st(dst, p, (y + z) + x, blocks)

    loop(r0, count, ch, body)


def operator(l, v, p, ch):
    x = ld(v, p, ch)
    lon = ld(l.e, p, ch) * (x - roll_l(x, -l.s)) + ld(l.west, p, ch) * (x - roll_l(x, l.s))
    lat = ld(l.so, p, ch) * (x - ld(v, p + 1, ch)) + ld(l.so, p - 1, ch) * (x - ld(v, p - 1, ch))
    return x, lat + lon


def remainder(l, ch):
    def body(r):
        p = l.pad + r
        st(l.r, p, ld(l.f, p, ch) - operator(l, l.v, p, ch)[1])

    loop(0, l.n, ch, body)


def pair(ref, start, n, odd, blocks=ALL):
    return ld(ref, start + odd, n, blocks, 2)


def restrict(l, c):
    ch = min(16, c.n)

    def body(a):
        x = pair(l.r, l.pad + 2 * a, ch, 0) + pair(l.r, l.pad + 2 * a, ch, 1)
        x = x + roll_l(x, -l.s)
        st(c.f, c.pad + a, x)
        st(c.wf, c.pad + a, x * ld(c.w, c.pad + a, ch))

    for a in range(0, c.n, ch):
        body(a)


def coarsen(l, c):
    ch = min(16, c.n)
    for a in range(0, c.n, ch):
        x = pair(l.e, l.pad + 2 * a, ch, 0) + pair(l.e, l.pad + 2 * a, ch, 1)
        st(c.e, c.pad + a, roll_l(x, -l.s))
        y = pair(l.so, l.pad + 2 * a, ch, 1)
        st(c.so, c.pad + a, y + roll_l(y, -l.s))


def spread_rows(v, start, e, add, blocks=ALL):
    for odd in (0, 1):
        x = e
        if add:
            x = x + ld(v, start + odd, e.shape[0], blocks, 2)
        st(v, start + odd, x, blocks, 2)


def prolong(c, l, src, dst, a0, n, add, blocks=ALL):
    for a in range(0, n, 8):
        e = ld(src, c.pad + a0 + a, 8, blocks)
        e = jnp.where((lanes(e.shape) & l.s) == 0, e, roll_l(e, l.s))
        spread_rows(dst, l.pad + 2 * (a0 + a), e, add, blocks)


def pick(x, index):
    return jnp.take_along_axis(x, index, axis=1, mode="promise_in_bounds")


def compact(x, offset):
    l = lanes((8, 128))
    index = (l % 32) * 4 + offset
    out = pick(x[:, 384:512], index)
    for j in (2, 1, 0):
        out = jnp.where(l < 32 * (j + 1), pick(x[:, 128 * j:128 * (j + 1)], index), out)
    return out


def expand(x, base):
    l = lanes((8, 128))
    q = l // 4
    own = x[2, pl.ds(base, 8), :]
    parts = [pick(own, q + 32 * j) for j in range(4)]
    east = pick(x[3, pl.ds(base, 8), :], q)
    west = pick(x[1, pl.ds(base, 8), :], q + 96)
    return jnp.concatenate(parts + [jnp.where(l < 64, east, west)], axis=1)


def kernel(
    b_in, e_in, s_in, sol, res,
    g, pk, re_, rw_, a0, ag, c, t1, got1, t2, got2,
    *rest,
):
    fine0, fine1, fine2, fine3, fine4, fine5 = rest[:9], rest[9:22], rest[22:32], rest[32:45], rest[45:58], rest[58:72]
    in_sem, a_send, a_recv, cs_send, cs_recv, fs_send, fs_recv, c1_send, c1_recv, c2_send, c2_recv, token = rest[72:]

    l0 = Level(1, PAD, N0, g.at[0], g.at[1], g.at[2], *fine0[:5], None, *fine0[5:])
    l1 = Level(2, PAD, N0 // 2, *fine1)
    l2 = Level(1, PAD2, 64, c.at[0], c.at[1], c.at[2], *fine2)
    l3 = Level(2, PAD, 32, *fine3)
    l4 = Level(4, PAD, 16, *fine4)
    l5 = Level(8, PAD, 8, *fine5)
    lat, lon = lax.axis_index("lat"), lax.axis_index("lon")

    def device(dlon, dlat):
        return {"lon": lax.rem(lon + dlon + NLON, NLON), "lat": lax.rem(lat + dlat + NLAT, NLAT)}

    block = (lon // BLOCK) * BLOCK
    inner = lax.rem(lon, BLOCK)

    def mate1(d):
        return {"lon": block + lax.rem(inner + d, BLOCK), "lat": lat}

    def mate2(d):
        return device(BLOCK * (d // 4), d % 4)

    top = PAD + H
    loads = [
        pltpu.make_async_copy(x.at[:, pl.ds(128 * j, 128)], g.at[i, j, pl.ds(top, ROWS)], in_sem.at[i, j])
        for i, x in enumerate((b_in, e_in, s_in))
        for j in range(4)
    ]
    barrier = pltpu.get_barrier_semaphore()
    greeted = [device(*d) for d in ((1, 0), (-1, 0), (0, 1), (0, -1), (2, 0), (-2, 0), (0, 2))]
    for other in greeted:
        pl.semaphore_signal(barrier, inc=1, device_id=other, device_id_type=MESH)
    for copy in loads:
        copy.start()

    rounds = [[(2, 0), (-2, 0)], [(4, 0), (-4, 0)], [(8, 0), (-8, 0)], [(16, 0), (-16, 0)], [(0, 1), (0, 2), (0, 3)]]

    def tell(k):
        for d in rounds[k]:
            pl.semaphore_signal(token.at[k], inc=1, device_id=device(*d), device_id_type=MESH)

    def hear(k):
        pl.semaphore_wait(token.at[k], len(rounds[k]))

    def clear(ref, l):
        zero = jnp.zeros((l.pad, WIDE), F32)
        st(ref, 0, zero)
        st(ref, l.pad + l.n, zero)

    for l in (l0, l1):
        for ref in (l.wf, l.v, l.v2, l.q):
            clear(ref, l)
    for l in (l2, l3, l4, l5):
        for ref in (l.wf, l.v, l.v2, l.q, l.so):
            clear(ref, l)
    for ref in (l2.ae, l2.aw, l2.as_, l2.an):
        clear(ref, l2)
    for ref in (l5.e, l5.r):
        clear(ref, l5)

    for copy in loads:
        copy.wait()

    l8 = lanes((8, 128))
    def pack(k):
        rows = slice(PAD + 8 * k, PAD + 8 * k + 8)
        first = [g[i, 0, rows] for i in range(3)]
        last = [g[i, 3, rows] for i in range(3)]
        x = jnp.where(l8 < 16, first[0], jnp.where(l8 < 32, roll_l(first[1], 16), roll_l(first[2], 32)))
        y = jnp.where(l8 >= 112, last[0], jnp.where(l8 >= 96, roll_l(last[1], -16), roll_l(last[2], -32)))
        pk[8 * k:8 * k + 8] = jnp.where(l8 < 64, x, y)

    for k in range(H // 8, (H + ROWS) // 8):
        pack(k)

    own_rows = pl.ds(pl.multiple_of(PAD2 + lat * 16, 16), 16)

    for a in range(0, 16, 8):
        x = ld(g.at[1], top + 4 * a, 8, range(4), 4)
        for j in (1, 2, 3):
            x = x + ld(g.at[1], top + 4 * a + j, 8, range(4), 4)
        y = ld(g.at[2], top + 4 * a + 3, 8, range(4), 4)
        y = y + roll_l(y, -1)
        y = y + roll_l(y, -2)
        rows = pl.ds(pl.multiple_of(PAD2 + lat * 16 + a, 8), 8)
        c[1, 2, rows, :] = compact(x, 3)
        c[2, 2, rows, :] = compact(y, 0)

    pl.semaphore_wait(barrier, len(greeted))

    def send(src, dst, s_sem, r_sem, k, to):
        copy = pltpu.make_async_remote_copy(
            src_ref=src, dst_ref=dst, send_sem=s_sem.at[k], recv_sem=r_sem.at[k], device_id=to, device_id_type=MESH
        )
        copy.start()
        return copy

    def rows_out(k, dlat, first, to):
        src = g.at[:, pl.ds(0, 4), pl.ds(PAD + first, H)]
        return send(src, g.at[:, pl.ds(0, 4), pl.ds(PAD + to, H)], a_send, a_recv, k, device(0, dlat))

    def edges_out(k, first, n):
        rows = pl.ds(first, n)
        return [
            send(pk.at[rows], rw_.at[rows], a_send, a_recv, k, device(1, 0)),
            send(pk.at[rows], re_.at[rows], a_send, a_recv, k + 1, device(-1, 0)),
        ]

    halos = [rows_out(0, 1, ROWS, 0), rows_out(1, -1, H, H + ROWS)] + edges_out(2, H, ROWS)
    tell(0)

    def spread_lat(index, s_sem, r_sem):
        part = c.at[index, 2, own_rows]
        return [send(part, part, s_sem, r_sem, k, device(0, d)) for k, d in enumerate(SPREAD_LAT)]

    def spread_lon(index, s_sem, r_sem):
        rows = pl.ds(PAD2, 64)
        return [
            send(c.at[index, 2, rows], c.at[index, 2 - d, rows], s_sem, r_sem, 3 + k, device(d, 0))
            for k, d in enumerate(SPREAD_LON)
        ]

    conds = spread_lat(pl.ds(1, 2), cs_send, cs_recv)

    for k, first in ((0, 0), (1, H + ROWS)):
        halos[k].wait_recv()
        for i in range(first // 8, (first + H) // 8):
            pack(i)
        halos += edges_out(4 + 2 * k, first, H)
    for copy in halos[2:]:
        copy.wait_recv()
    hear(0)
    tell(1)
    for copy in conds:
        copy.wait_recv()
    conds_lon = spread_lon(pl.ds(1, 2), cs_send, cs_recv)

    has_north = jnp.where(lat > 0, 1.0, 0.0).astype(F32)
    used = (l8 < 16) | (l8 >= 112)
    for k in range(N0 // 8):
        x = jnp.where(l8 < 64, re_[8 * k:8 * k + 8], rw_[8 * k:8 * k + 8])
        for i, other in ((0, 0.0), (1, 1.0), (2, 1.0)):
            y = x if i == 0 else jnp.where(l8 < 64, roll_l(x, -16 * i), roll_l(x, 16 * i))
            g[i, 4, PAD + 8 * k:PAD + 8 * k + 8, :] = jnp.where(used, y, other)
    g[2, :, PAD:PAD + H] = g[2, :, PAD:PAD + H] * has_north

    def bounds(halo, own):
        return jnp.where(lat > 0, 0, halo), jnp.where(lat < NLAT - 1, 2 * halo + own, halo + own)

    coeffs(l0, 16, bounds(H, ROWS), True)
    sweep(l0, l0.wf, l0.v, True, 0, N0, 16)
    coarsen(l0, l1)
    remainder(l0, 16)
    coeffs(l1, 16, bounds(H // 2, ROWS // 2))
    restrict(l0, l1)
    sweep(l1, l1.wf, l1.v, True, 0, 48, 16)
    remainder(l1, 16)
    for a in range(0, 16, 8):
        x = ld(l1.r, PAD + 8 + 2 * a, 8, range(4), 2) + ld(l1.r, PAD + 9 + 2 * a, 8, range(4), 2)
        rows = pl.ds(pl.multiple_of(PAD2 + lat * 16 + a, 8), 8)
        c[0, 2, rows, :] = compact(x + roll_l(x, -2), 0)
    fields = spread_lat(0, fs_send, fs_recv)
    hear(1)
    tell(2)

    for copy in conds_lon:
        copy.wait_recv()
    coeffs(l2, 16)
    coarsen(l2, l3)
    coeffs(l3, 16)
    coarsen(l3, l4)
    coeffs(l4, 16)
    coarsen(l4, l5)
    coeffs(l5, 8)


    def twice(l, v, source, r0, count, ch, blocks=ALL):
        sweep(l, v, l.v2, source, r0, count, ch, blocks)
        sweep(l, l.v2, v, source, r0, count, ch, blocks)

    def rise_coarse(name, source):
        u = [getattr(l, name) for l in (l0, l1, l2, l3, l4, l5)]
        twice(l5, u[5], source, 0, 8, 8, MID)
        prolong(l5, l4, u[5], u[4], 0, 8, source, MID)
        twice(l4, u[4], source, 0, 16, 16, MID)
        prolong(l4, l3, u[4], u[3], 0, 16, source, MID)
        twice(l3, u[3], source, 0, 32, 16, MID)
        near = lat * 8 - 4
        prolong(l3, l2, u[3], u[2], near, 16, source, MID)
        near = pl.multiple_of(lat * 16 - 8, 8)
        twice(l2, u[2], source, near, 32, 16, MID)

    def rise_fine(name, source):
        u = [getattr(l, name) for l in (l0, l1, l2)]
        for i in range(3):
            e = expand(u[2], PAD2 + lat * 16 - 4 + 8 * i)
            spread_rows(u[1], PAD + 16 * i, e, source)
        twice(l1, u[1], source, 0, 48, 16)
        prolong(l1, l0, u[1], u[0], 0, 48, source)
        twice(l0, u[0], source, 8, 80, 16)

    def applied(v, out, sums, n):
        def body(r, carry):
            x, av = operator(l0, v, top + r, 16)
            x, av = x[:, :COLS], av[:, :COLS]
            out[pl.ds(r, 16)] = av
            more = sums(pl.ds(r, 16), ld(l0.f, top + r, 16, range(4)), x, av)
            return tuple(y + (z[:8] + z[8:]) for y, z in zip(carry, more))

        carry = (jnp.zeros((8, COLS), F32),) * n
        for r in range(0, ROWS, 16):
            carry = body(r, carry)
        return carry

    st(l5.q, PAD, jnp.ones((8, WIDE), F32))
    rise_coarse("q", False)
    for copy in halos + conds:
        copy.wait_send()
    for copy in fields:
        copy.wait_recv()
    fields_lon = spread_lon(0, fs_send, fs_recv)
    hear(2)
    tell(3)
    rise_fine("q", False)
    for copy in fields + conds_lon:
        copy.wait_send()
    sums_q = applied(l0.q, ag, lambda rows, b, v, av: (b * v, v * av), 2)

    for copy in fields_lon:
        copy.wait_recv()
    hear(3)
    tell(4)

    def first(r):
        st(l2.wf, PAD2 + r, ld(l2.w, PAD2 + r, 16) * ld(l2.f, PAD2 + r, 16))

    loop(0, 64, 16, first)
    sweep(l2, l2.wf, l2.v, True, 0, 64, 16)
    remainder(l2, 16)
    for l, coarse in ((l2, l3), (l3, l4), (l4, l5)):
        restrict(l, coarse)
        sweep(coarse, coarse.wf, coarse.v, True, 0, coarse.n, min(16, coarse.n))
        remainder(coarse, min(16, coarse.n))

    x = pair(l5.r, PAD, 8, 0) + pair(l5.r, PAD, 8, 1)
    f6 = x + roll_l(x, -8)
    x = pair(l5.e, PAD, 8, 0) + pair(l5.e, PAD, 8, 1)
    e6 = roll_l(x, -8)
    x = pair(l5.so, PAD, 8, 1)
    s6 = x + roll_l(x, -8)
    row6, lane6 = rows_of((8, WIDE)), lanes((8, WIDE))
    west6 = roll_l(e6, 16)
    north6 = jnp.where(row6 == 0, 0.0, pltpu.roll(s6, 1, 0))
    w6 = jnp.where(row6 < 4, OMEGA / (((e6 + west6) + s6) + north6), 0.0)
    ae6, aw6, as6, an6, wf6 = w6 * e6, w6 * west6, w6 * s6, w6 * north6, w6 * f6
    field = wf6
    for _ in range(COARSE_SWEEPS - 1):
        x = ae6 * roll_l(field, -16) + aw6 * roll_l(field, 16)
        y = as6 * pltpu.roll(field, 7, 0) + an6 * pltpu.roll(field, 1, 0)
        field = (((1.0 - OMEGA) * field + wf6) + y) + x
    lon6 = e6 * (field - roll_l(field, -16)) + west6 * (field - roll_l(field, 16))
    lat6 = s6 * (field - pltpu.roll(field, 7, 0)) + north6 * (field - pltpu.roll(field, 1, 0))
    left = f6 - (lon6 + lat6)
    mine = ((lane6 & 15) == 0) & (lane6 >= 256) & (lane6 < 384)
    left = jnp.where(mine & (row6 == lat), left, 0.0)[:, 256:384]
    last = jnp.where(mine & (row6 == 3) & (lat == 3), s6, 0.0)[:, 256:384]

    e = jnp.where((lane6 & 8) == 0, field, roll_l(field, 8))
    for odd in (0, 1):
        st(l5.r, odd, e, ALL, 2)
    st(l5.v, PAD, ld(l5.v, PAD, 8) + ld(l5.r, 0, 8))
    rise_coarse("v", True)
    rise_fine("v", True)
    sums_v = applied(l0.v, a0, lambda rows, b, v, av: (b * v, v * av, v * ag[rows]), 3)

    def wait_all(got, sem):
        pltpu.make_async_copy(got, got, sem.at[0]).wait()

    def fold(x):
        return (x[:, 0:128] + x[:, 128:256]) + (x[:, 256:384] + x[:, 384:512])

    seven = [left, last, fold(sums_v[0]), fold(sums_q[0]), fold(sums_v[1]), fold(sums_v[2]), fold(sums_q[1])]
    row = rows_of((8, 128))
    total = jnp.zeros((8, 128), F32)
    for i, x in enumerate(seven):
        total = jnp.where(row == i, jnp.sum(x, axis=0, keepdims=True), total)
    hear(4)
    t1[...] = total
    for d in range(1, 16):
        send(t1, got1.at[d - 1], c1_send, c1_recv, 0, mate1(d))
    for copy in fields_lon:
        copy.wait_send()
    wait_all(got1, c1_recv)

    def gathered(total, got):
        parts = [total] + [got[d] for d in range(15)]
        while len(parts) > 1:
            parts = [x + y for x, y in zip(parts[::2], parts[1::2])]
        return parts[0]

    total = gathered(total, got1)
    t2[...] = total
    for d in range(1, 16):
        send(t2, got2.at[d - 1], c2_send, c2_recv, 0, mate2(d))
    wait_all(got1, c1_send)
    wait_all(got2, c2_recv)
    total = gathered(total, got2)
    for by in (64, 32, 16, 8, 4, 2, 1):
        total = total + pltpu.roll(total, by, 1)
    n_left, n_last, bv, bq, vav, vaq, qaq = [total[i:i + 1] for i in range(7)]
    const = n_left / n_last
    step = (bv + const * bq) / ((vav + (2.0 * const) * vaq) + (const * const) * qaq)
    both = jnp.concatenate([step * const] * 4, axis=1)
    step = jnp.concatenate([step] * 4, axis=1)

    for r in range(0, ROWS, 16):
        rows = pl.ds(r, 16)
        sol[rows] = step * ld(l0.v, top + r, 16, range(4)) + both * ld(l0.q, top + r, 16, range(4))
        res[rows] = ld(l0.f, top + r, 16, range(4)) - (step * a0[rows] + both * ag[rows])
    wait_all(got2, c2_send)


def body(guidance, cond_lon, cond_lat):
    def vm(*shape):
        return pltpu.VMEM(shape, F32)

    def wide(n, count):
        return [vm(5, n, 128)] * count

    dma = pltpu.SemaphoreType.DMA
    scratch = [vm(3, 5, N0 + 2 * PAD, 128), vm(N0, 128), vm(N0, 128), vm(N0, 128), vm(ROWS, COLS), vm(ROWS, COLS)]
    scratch += [vm(3, 5, 64 + 2 * PAD2, 128), vm(8, 128), vm(15, 8, 128), vm(8, 128), vm(15, 8, 128)]
    scratch += wide(N0 + 2 * PAD, 9) + wide(N0 // 2 + 2 * PAD, 13) + wide(64 + 2 * PAD2, 10)
    scratch += wide(32 + 2 * PAD, 13) + wide(16 + 2 * PAD, 13) + wide(8 + 2 * PAD, 14)
    scratch += [dma((3, 4)), dma((8,)), dma((8,)), dma((7,)), dma((7,)), dma((7,)), dma((7,))] + [dma((1,))] * 4 + [pltpu.SemaphoreType.REGULAR((5,))]
    return pl.pallas_call(
        kernel,
        out_shape=(jax.ShapeDtypeStruct((ROWS, COLS), F32),) * 2,
        in_specs=[pl.BlockSpec(memory_space=pltpu.HBM)] * 3,
        out_specs=(pl.BlockSpec(memory_space=pltpu.VMEM),) * 2,
        scratch_shapes=scratch,
        compiler_params=pltpu.CompilerParams(
            collective_id=0, has_side_effects=True, vmem_limit_bytes=63 * 1024 * 1024
        ),
        cost_estimate=pl.CostEstimate(flops=10_000_000, bytes_accessed=655360, transcendentals=0),
    )(guidance, cond_lon, cond_lat)


def solution(mesh):
    spec = P("lat", "lon")
    return jax.shard_map(body, mesh=mesh, in_specs=(spec,) * 3, out_specs=(spec,) * 2, check_vma=False)
```

```python
import jax
import jax.numpy as jnp
from jax import lax
from jax.experimental import pallas as pl
from jax.experimental.pallas import tpu as pltpu
from jax.sharding import PartitionSpec as P

OMEGA = 0.8
COARSE_SWEEPS = 8
NLAT, NLON, BLOCK = 4, 64, 16
ROWS, COLS = 64, 512
H = 16
PAD = 8
PAD2 = 16
N0 = ROWS + 2 * H
WIDE = COLS + 128
ALL = range(5)
MID = range(1, 4)
MESH = pl.DeviceIdType.MESH
F32 = jnp.float32

HALO = ((1, 1), (1, -1), (-1, 1), (-1, -1), (1, 0), (-1, 0), (0, 1), (0, -1))
SPREAD_LAT = (1, 2, 3)
SPREAD_LON = (2, -2, 1, -1)
SPREAD = ((2, 2), (-2, 2), (1, 2), (-1, 2), (2, 1), (2, -1), (-2, 1), (-2, -1), (0, 2), (2, 0), (-2, 0))
SPREAD += ((1, 1), (1, -1), (-1, 1), (-1, -1), (0, 1), (0, -1), (1, 0), (-1, 0))
FAR1 = (8, 7, 9, 6, 10, 5, 11, 4, 12, 3, 13, 2, 14, 1, 15)
FAR2 = (10, 9, 11, 6, 14, 2, 8, 5, 7, 13, 15, 1, 3, 4, 12)


def lanes(shape):
    return lax.broadcasted_iota(jnp.int32, shape, len(shape) - 1)


def rows_of(shape):
    return lax.broadcasted_iota(jnp.int32, shape, 0)


def roll_l(x, by):
    return pltpu.roll(x, by % x.shape[1], 1)


def ld(ref, start, n, blocks=ALL, stride=None):
    rows = pl.ds(start, n) if stride is None else pl.ds(start, n, stride=stride)
    return jnp.concatenate([ref[j, rows, :] for j in blocks], axis=1)


def st(ref, start, x, blocks=ALL, stride=None):
    n = x.shape[0]
    rows = pl.ds(start, n) if stride is None else pl.ds(start, n, stride=stride)
    for i, j in enumerate(blocks):
        ref[j, rows, :] = x[:, 128 * i:128 * (i + 1)]


def loop(r0, count, ch, body):
    for k in range(count // ch):
        body(r0 + k * ch)


class Level:
    def __init__(self, s, pad, n, f, e, so, west, ae, aw, as_, an, w, wf, v, v2, q, r=None):
        self.s, self.pad, self.n = s, pad, n
        self.f, self.e, self.so, self.west = f, e, so, west
        self.ae, self.aw, self.as_, self.an, self.w, self.wf = ae, aw, as_, an, w, wf
        self.v, self.v2, self.q, self.r = v, v2, q, v2 if r is None else r


def coeffs(l, ch, keep=None, source=False):
    def body(r):
        p = l.pad + r
        e, so, no = ld(l.e, p, ch), ld(l.so, p, ch), ld(l.so, p - 1, ch)
        we = roll_l(e, l.s)
        wk = OMEGA / (((e + we) + so) + no)
        if keep is not None:
            row = rows_of(wk.shape) + r
            wk = jnp.where((row >= keep[0]) & (row < keep[1]), wk, 0.0)
        st(l.west, p, we)
        st(l.ae, p, wk * e)
        st(l.aw, p, wk * we)
        st(l.as_, p, wk * so)
        st(l.an, p, wk * no)
        if source:
            st(l.wf, p, wk * ld(l.f, p, ch))
        else:
            st(l.w, p, wk)

    loop(0, l.n, ch, body)


def sweep(l, src, dst, source, r0, count, ch, blocks=ALL):
    def body(r):
        p = l.pad + r
        v = ld(src, p, ch, blocks)
        x = ld(l.ae, p, ch, blocks) * roll_l(v, -l.s) + ld(l.aw, p, ch, blocks) * roll_l(v, l.s)
        y = ld(l.as_, p, ch, blocks) * ld(src, p + 1, ch, blocks) + ld(l.an, p, ch, blocks) * ld(src, p - 1, ch, blocks)
        z = (1.0 - OMEGA) * v
        if source:
            z = z + ld(l.wf, p, ch, blocks)
        st(dst, p, (y + z) + x, blocks)

    loop(r0, count, ch, body)


def operator(l, v, p, ch):
    x = ld(v, p, ch)
    lon = ld(l.e, p, ch) * (x - roll_l(x, -l.s)) + ld(l.west, p, ch) * (x - roll_l(x, l.s))
    lat = ld(l.so, p, ch) * (x - ld(v, p + 1, ch)) + ld(l.so, p - 1, ch) * (x - ld(v, p - 1, ch))
    return x, lat + lon


def remainder(l, ch):
    def body(r):
        p = l.pad + r
        st(l.r, p, ld(l.f, p, ch) - operator(l, l.v, p, ch)[1])

    loop(0, l.n, ch, body)


def pair(ref, start, n, odd, blocks=ALL):
    return ld(ref, start + odd, n, blocks, 2)


def restrict(l, c):
    ch = min(16, c.n)

    def body(a):
        x = pair(l.r, l.pad + 2 * a, ch, 0) + pair(l.r, l.pad + 2 * a, ch, 1)
        x = x + roll_l(x, -l.s)
        st(c.f, c.pad + a, x)
        st(c.wf, c.pad + a, x * ld(c.w, c.pad + a, ch))

    for a in range(0, c.n, ch):
        body(a)


def coarsen(l, c):
    ch = min(16, c.n)
    for a in range(0, c.n, ch):
        x = pair(l.e, l.pad + 2 * a, ch, 0) + pair(l.e, l.pad + 2 * a, ch, 1)
        st(c.e, c.pad + a, roll_l(x, -l.s))
        y = pair(l.so, l.pad + 2 * a, ch, 1)
        st(c.so, c.pad + a, y + roll_l(y, -l.s))


def spread_rows(v, start, e, add, blocks=ALL):
    for odd in (0, 1):
        x = e
        if add:
            x = x + ld(v, start + odd, e.shape[0], blocks, 2)
        st(v, start + odd, x, blocks, 2)


def prolong(c, l, src, dst, a0, n, add, blocks=ALL):
    for a in range(0, n, 8):
        e = ld(src, c.pad + a0 + a, 8, blocks)
        e = jnp.where((lanes(e.shape) & l.s) == 0, e, roll_l(e, l.s))
        spread_rows(dst, l.pad + 2 * (a0 + a), e, add, blocks)


def pick(x, index):
    return jnp.take_along_axis(x, index, axis=1, mode="promise_in_bounds")


def compact(x, offset):
    l = lanes((8, 128))
    index = (l % 32) * 4 + offset
    out = pick(x[:, 384:512], index)
    for j in (2, 1, 0):
        out = jnp.where(l < 32 * (j + 1), pick(x[:, 128 * j:128 * (j + 1)], index), out)
    return out


def expand(x, base):
    l = lanes((8, 128))
    q = l // 4
    own = x[2, pl.ds(base, 8), :]
    parts = [pick(own, q + 32 * j) for j in range(4)]
    east = pick(x[3, pl.ds(base, 8), :], q)
    west = pick(x[1, pl.ds(base, 8), :], q + 96)
    return jnp.concatenate(parts + [jnp.where(l < 64, east, west)], axis=1)


def kernel(
    b_in, e_in, s_in, sol, res,
    g, pk, re_, rw_, a0, ag, c, t1, got1, t2, got2,
    *rest,
):
    fine0, fine1, fine2, fine3, fine4, fine5 = rest[:9], rest[9:22], rest[22:32], rest[32:45], rest[45:58], rest[58:72]
    in_sem, a_send, a_recv, cs_send, cs_recv, fs_send, fs_recv, c1_send, c1_recv, c2_send, c2_recv = rest[72:]

    l0 = Level(1, PAD, N0, g.at[0], g.at[1], g.at[2], *fine0[:5], None, *fine0[5:])
    l1 = Level(2, PAD, N0 // 2, *fine1)
    l2 = Level(1, PAD2, 64, c.at[0], c.at[1], c.at[2], *fine2)
    l3 = Level(2, PAD, 32, *fine3)
    l4 = Level(4, PAD, 16, *fine4)
    l5 = Level(8, PAD, 8, *fine5)
    lat, lon = lax.axis_index("lat"), lax.axis_index("lon")

    def device(dlon, dlat):
        return {"lon": lax.rem(lon + dlon + NLON, NLON), "lat": lax.rem(lat + dlat + NLAT, NLAT)}

    block = (lon // BLOCK) * BLOCK
    inner = lax.rem(lon, BLOCK)

    def mate1(d):
        return {"lon": block + lax.rem(inner + d, BLOCK), "lat": lat}

    def mate2(d):
        return device(BLOCK * (d // 4), d % 4)

    top = PAD + H
    loads = [
        pltpu.make_async_copy(x.at[:, pl.ds(128 * j, 128)], g.at[i, j, pl.ds(top, ROWS)], in_sem.at[i, j])
        for i, x in enumerate((b_in, e_in, s_in))
        for j in range(4)
    ]
    barrier = pltpu.get_barrier_semaphore()
    greeted = [device(*d) for d in HALO + SPREAD[:11]]
    greeted += [mate1(d) for d in range(1, BLOCK)] + [mate2(d) for d in range(4, 16)]
    for k, other in enumerate(greeted):
        pl.semaphore_signal(barrier, inc=1, device_id=other, device_id_type=MESH)
        if k == len(HALO) - 1:
            for copy in loads:
                copy.start()

    def clear(ref, l):
        zero = jnp.zeros((l.pad, WIDE), F32)
        st(ref, 0, zero)
        st(ref, l.pad + l.n, zero)

    for l in (l0, l1):
        for ref in (l.wf, l.v, l.v2, l.q):
            clear(ref, l)
    for l in (l2, l3, l4, l5):
        for ref in (l.wf, l.v, l.v2, l.q, l.so):
            clear(ref, l)
    for ref in (l2.ae, l2.aw, l2.as_, l2.an):
        clear(ref, l2)
    for ref in (l5.e, l5.r):
        clear(ref, l5)

    for copy in loads:
        copy.wait()

    l8 = lanes((8, 128))
    for k in range(ROWS // 8):
        rows = slice(top + 8 * k, top + 8 * k + 8)
        first = [g[i, 0, rows] for i in range(3)]
        last = [g[i, 3, rows] for i in range(3)]
        x = jnp.where(l8 < 16, first[0], jnp.where(l8 < 32, roll_l(first[1], 16), roll_l(first[2], 32)))
        y = jnp.where(l8 >= 112, last[0], jnp.where(l8 >= 96, roll_l(last[1], -16), roll_l(last[2], -32)))
        pk[8 * k:8 * k + 8] = jnp.where(l8 < 64, x, y)

    own_rows = pl.ds(pl.multiple_of(PAD2 + lat * 16, 16), 16)

    for a in range(0, 16, 8):
        x = ld(g.at[1], top + 4 * a, 8, range(4), 4)
        for j in (1, 2, 3):
            x = x + ld(g.at[1], top + 4 * a + j, 8, range(4), 4)
        y = ld(g.at[2], top + 4 * a + 3, 8, range(4), 4)
        y = y + roll_l(y, -1)
        y = y + roll_l(y, -2)
        rows = pl.ds(pl.multiple_of(PAD2 + lat * 16 + a, 8), 8)
        c[1, 2, rows, :] = compact(x, 3)
        c[2, 2, rows, :] = compact(y, 0)

    pl.semaphore_wait(barrier, len(greeted))

    def send(src, dst, s_sem, r_sem, k, to):
        copy = pltpu.make_async_remote_copy(
            src_ref=src, dst_ref=dst, send_sem=s_sem.at[k], recv_sem=r_sem.at[k], device_id=to, device_id_type=MESH
        )
        copy.start()
        return copy

    halos = []
    for k, (dlon, dlat) in enumerate(HALO):
        first_row, count = {0: (0, ROWS), 1: (ROWS - H, H), -1: (0, H)}[dlat]
        to = {0: H, 1: 0, -1: H + ROWS}[dlat]
        if dlon == 0:
            src = g.at[:, pl.ds(0, 4), pl.ds(top + first_row, count)]
            dst = g.at[:, pl.ds(0, 4), pl.ds(PAD + to, count)]
        else:
            src = pk.at[pl.ds(first_row, count)]
            dst = (rw_ if dlon == 1 else re_).at[pl.ds(to, count)]
        halos.append(send(src, dst, a_send, a_recv, k, device(dlon, dlat)))

    def spread_lat(index, s_sem, r_sem):
        part = c.at[index, 2, own_rows]
        return [send(part, part, s_sem, r_sem, k, device(0, d)) for k, d in enumerate(SPREAD_LAT)]

    def spread_lon(index, s_sem, r_sem):
        rows = pl.ds(PAD2, 64)
        return [
            send(c.at[index, 2, rows], c.at[index, 2 - d, rows], s_sem, r_sem, 3 + k, device(d, 0))
            for k, d in enumerate(SPREAD_LON)
        ]

    conds = spread_lat(pl.ds(1, 2), cs_send, cs_recv)

    for copy in halos:
        copy.wait_recv()
    for copy in conds:
        copy.wait_recv()
    conds_lon = spread_lon(pl.ds(1, 2), cs_send, cs_recv)

    has_north = jnp.where(lat > 0, 1.0, 0.0).astype(F32)
    used = (l8 < 16) | (l8 >= 112)
    for k in range(N0 // 8):
        x = jnp.where(l8 < 64, re_[8 * k:8 * k + 8], rw_[8 * k:8 * k + 8])
        for i, other in ((0, 0.0), (1, 1.0), (2, 1.0)):
            y = x if i == 0 else jnp.where(l8 < 64, roll_l(x, -16 * i), roll_l(x, 16 * i))
            g[i, 4, PAD + 8 * k:PAD + 8 * k + 8, :] = jnp.where(used, y, other)
    g[2, :, PAD:PAD + H] = g[2, :, PAD:PAD + H] * has_north

    def bounds(halo, own):
        return jnp.where(lat > 0, 0, halo), jnp.where(lat < NLAT - 1, 2 * halo + own, halo + own)

    coeffs(l0, 16, bounds(H, ROWS), True)
    sweep(l0, l0.wf, l0.v, True, 0, N0, 16)
    coarsen(l0, l1)
    remainder(l0, 16)
    coeffs(l1, 16, bounds(H // 2, ROWS // 2))
    restrict(l0, l1)
    sweep(l1, l1.wf, l1.v, True, 0, 48, 16)
    remainder(l1, 16)
    for a in range(0, 16, 8):
        x = ld(l1.r, PAD + 8 + 2 * a, 8, range(4), 2) + ld(l1.r, PAD + 9 + 2 * a, 8, range(4), 2)
        rows = pl.ds(pl.multiple_of(PAD2 + lat * 16 + a, 8), 8)
        c[0, 2, rows, :] = compact(x + roll_l(x, -2), 0)
    fields = [
        send(c.at[0, 2, own_rows], c.at[0, 2 - d[0], own_rows], fs_send, fs_recv, k, device(*d))
        for k, d in enumerate(SPREAD)
    ]

    for copy in conds_lon:
        copy.wait_recv()
    coeffs(l2, 16)
    coarsen(l2, l3)
    coeffs(l3, 16)
    coarsen(l3, l4)
    coeffs(l4, 16)
    coarsen(l4, l5)
    coeffs(l5, 8)


    def twice(l, v, source, r0, count, ch, blocks=ALL):
        sweep(l, v, l.v2, source, r0, count, ch, blocks)
        sweep(l, l.v2, v, source, r0, count, ch, blocks)

    def rise_coarse(name, source):
        u = [getattr(l, name) for l in (l0, l1, l2, l3, l4, l5)]
        twice(l5, u[5], source, 0, 8, 8, MID)
        prolong(l5, l4, u[5], u[4], 0, 8, source, MID)
        twice(l4, u[4], source, 0, 16, 16, MID)
        prolong(l4, l3, u[4], u[3], 0, 16, source, MID)
        twice(l3, u[3], source, 0, 32, 16, MID)
        near = lat * 8 - 4
        prolong(l3, l2, u[3], u[2], near, 16, source, MID)
        near = pl.multiple_of(lat * 16 - 8, 8)
        twice(l2, u[2], source, near, 32, 16, MID)

    def rise_fine(name, source):
        u = [getattr(l, name) for l in (l0, l1, l2)]
        for i in range(3):
            e = expand(u[2], PAD2 + lat * 16 - 4 + 8 * i)
            spread_rows(u[1], PAD + 16 * i, e, source)
        twice(l1, u[1], source, 0, 48, 16)
        prolong(l1, l0, u[1], u[0], 0, 48, source)
        twice(l0, u[0], source, 8, 80, 16)

    def applied(v, out, sums, n):
        def body(r, carry):
            x, av = operator(l0, v, top + r, 16)
            x, av = x[:, :COLS], av[:, :COLS]
            out[pl.ds(r, 16)] = av
            more = sums(pl.ds(r, 16), ld(l0.f, top + r, 16, range(4)), x, av)
            return tuple(y + (z[:8] + z[8:]) for y, z in zip(carry, more))

        carry = (jnp.zeros((8, COLS), F32),) * n
        for r in range(0, ROWS, 16):
            carry = body(r, carry)
        return carry

    st(l5.q, PAD, jnp.ones((8, WIDE), F32))
    rise_coarse("q", False)
    for copy in halos + conds:
        copy.wait_send()
    rise_fine("q", False)
    for copy in fields + conds_lon:
        copy.wait_send()
    sums_q = applied(l0.q, ag, lambda rows, b, v, av: (b * v, v * av), 2)

    for copy in fields:
        copy.wait_recv()

    def first(r):
        st(l2.wf, PAD2 + r, ld(l2.w, PAD2 + r, 16) * ld(l2.f, PAD2 + r, 16))

    loop(0, 64, 16, first)
    sweep(l2, l2.wf, l2.v, True, 0, 64, 16)
    remainder(l2, 16)
    for l, coarse in ((l2, l3), (l3, l4), (l4, l5)):
        restrict(l, coarse)
        sweep(coarse, coarse.wf, coarse.v, True, 0, coarse.n, min(16, coarse.n))
        remainder(coarse, min(16, coarse.n))

    x = pair(l5.r, PAD, 8, 0) + pair(l5.r, PAD, 8, 1)
    f6 = x + roll_l(x, -8)
    x = pair(l5.e, PAD, 8, 0) + pair(l5.e, PAD, 8, 1)
    e6 = roll_l(x, -8)
    x = pair(l5.so, PAD, 8, 1)
    s6 = x + roll_l(x, -8)
    row6, lane6 = rows_of((8, WIDE)), lanes((8, WIDE))
    west6 = roll_l(e6, 16)
    north6 = jnp.where(row6 == 0, 0.0, pltpu.roll(s6, 1, 0))
    w6 = jnp.where(row6 < 4, OMEGA / (((e6 + west6) + s6) + north6), 0.0)
    ae6, aw6, as6, an6, wf6 = w6 * e6, w6 * west6, w6 * s6, w6 * north6, w6 * f6
    field = wf6
    for _ in range(COARSE_SWEEPS - 1):
        x = ae6 * roll_l(field, -16) + aw6 * roll_l(field, 16)
        y = as6 * pltpu.roll(field, 7, 0) + an6 * pltpu.roll(field, 1, 0)
        field = (((1.0 - OMEGA) * field + wf6) + y) + x
    lon6 = e6 * (field - roll_l(field, -16)) + west6 * (field - roll_l(field, 16))
    lat6 = s6 * (field - pltpu.roll(field, 7, 0)) + north6 * (field - pltpu.roll(field, 1, 0))
    left = f6 - (lon6 + lat6)
    mine = ((lane6 & 15) == 0) & (lane6 >= 256) & (lane6 < 384)
    left = jnp.where(mine & (row6 == lat), left, 0.0)[:, 256:384]
    last = jnp.where(mine & (row6 == 3) & (lat == 3), s6, 0.0)[:, 256:384]

    e = jnp.where((lane6 & 8) == 0, field, roll_l(field, 8))
    for odd in (0, 1):
        st(l5.r, odd, e, ALL, 2)
    st(l5.v, PAD, ld(l5.v, PAD, 8) + ld(l5.r, 0, 8))
    rise_coarse("v", True)
    rise_fine("v", True)
    sums_v = applied(l0.v, a0, lambda rows, b, v, av: (b * v, v * av, v * ag[rows]), 3)

    def wait_all(got, sem):
        pltpu.make_async_copy(got, got, sem.at[0]).wait()

    def fold(x):
        return (x[:, 0:128] + x[:, 128:256]) + (x[:, 256:384] + x[:, 384:512])

    seven = [left, last, fold(sums_v[0]), fold(sums_q[0]), fold(sums_v[1]), fold(sums_v[2]), fold(sums_q[1])]
    row = rows_of((8, 128))
    total = jnp.zeros((8, 128), F32)
    for i, x in enumerate(seven):
        total = jnp.where(row == i, jnp.sum(x, axis=0, keepdims=True), total)
    t1[...] = total
    for d in FAR1:
        send(t1, got1.at[d - 1], c1_send, c1_recv, 0, mate1(d))
    wait_all(got1, c1_recv)

    def gathered(total, got):
        parts = [total] + [got[d] for d in range(15)]
        while len(parts) > 1:
            parts = [x + y for x, y in zip(parts[::2], parts[1::2])]
        return parts[0]

    total = gathered(total, got1)
    t2[...] = total
    for d in FAR2:
        send(t2, got2.at[d - 1], c2_send, c2_recv, 0, mate2(d))
    wait_all(got1, c1_send)
    wait_all(got2, c2_recv)
    total = gathered(total, got2)
    for by in (64, 32, 16, 8, 4, 2, 1):
        total = total + pltpu.roll(total, by, 1)
    n_left, n_last, bv, bq, vav, vaq, qaq = [total[i:i + 1] for i in range(7)]
    const = n_left / n_last
    step = (bv + const * bq) / ((vav + (2.0 * const) * vaq) + (const * const) * qaq)
    both = jnp.concatenate([step * const] * 4, axis=1)
    step = jnp.concatenate([step] * 4, axis=1)

    for r in range(0, ROWS, 16):
        rows = pl.ds(r, 16)
        sol[rows] = step * ld(l0.v, top + r, 16, range(4)) + both * ld(l0.q, top + r, 16, range(4))
        res[rows] = ld(l0.f, top + r, 16, range(4)) - (step * a0[rows] + both * ag[rows])
    wait_all(got2, c2_send)


def body(guidance, cond_lon, cond_lat):
    def vm(*shape):
        return pltpu.VMEM(shape, F32)

    def wide(n, count):
        return [vm(5, n, 128)] * count

    dma = pltpu.SemaphoreType.DMA
    scratch = [vm(3, 5, N0 + 2 * PAD, 128), vm(ROWS, 128), vm(N0, 128), vm(N0, 128), vm(ROWS, COLS), vm(ROWS, COLS)]
    scratch += [vm(3, 5, 64 + 2 * PAD2, 128), vm(8, 128), vm(15, 8, 128), vm(8, 128), vm(15, 8, 128)]
    scratch += wide(N0 + 2 * PAD, 9) + wide(N0 // 2 + 2 * PAD, 13) + wide(64 + 2 * PAD2, 10)
    scratch += wide(32 + 2 * PAD, 13) + wide(16 + 2 * PAD, 13) + wide(8 + 2 * PAD, 14)
    scratch += [dma((3, 4)), dma((8,)), dma((8,)), dma((7,)), dma((7,)), dma((19,)), dma((19,))] + [dma((1,))] * 4
    return pl.pallas_call(
        kernel,
        out_shape=(jax.ShapeDtypeStruct((ROWS, COLS), F32),) * 2,
        in_specs=[pl.BlockSpec(memory_space=pltpu.HBM)] * 3,
        out_specs=(pl.BlockSpec(memory_space=pltpu.VMEM),) * 2,
        scratch_shapes=scratch,
        compiler_params=pltpu.CompilerParams(
            collective_id=0, has_side_effects=True, vmem_limit_bytes=63 * 1024 * 1024
        ),
        cost_estimate=pl.CostEstimate(flops=10_000_000, bytes_accessed=655360, transcendentals=0),
    )(guidance, cond_lon, cond_lat)


def solution(mesh):
    spec = P("lat", "lon")
    return jax.shard_map(body, mesh=mesh, in_specs=(spec,) * 3, out_specs=(spec,) * 2, check_vma=False)
```

```python
import jax
import jax.numpy as jnp
from jax import lax
from jax.experimental import pallas as pl
from jax.experimental.pallas import tpu as pltpu
from jax.sharding import PartitionSpec as P

OMEGA = 0.8
COARSE_SWEEPS = 8
NLAT, NLON, BLOCK = 4, 64, 16
ROWS, COLS = 64, 512
H = 16
PAD = 8
PAD2 = 16
N0 = ROWS + 2 * H
WIDE = COLS + 128
ALL = range(5)
MID = range(1, 4)
MESH = pl.DeviceIdType.MESH
F32 = jnp.float32

HALO = ((1, 1), (1, -1), (-1, 1), (-1, -1), (1, 0), (-1, 0), (0, 1), (0, -1))
SPREAD_LAT = (1, 2, 3)
SPREAD_LON = (2, -2, 1, -1)
SPREAD = ((2, 2), (-2, 2), (1, 2), (-1, 2), (2, 1), (2, -1), (-2, 1), (-2, -1), (0, 2), (2, 0), (-2, 0))
SPREAD += ((1, 1), (1, -1), (-1, 1), (-1, -1), (0, 1), (0, -1), (1, 0), (-1, 0))
FAR1 = (8, 7, 9, 6, 10, 5, 11, 4, 12, 3, 13, 2, 14, 1, 15)
FAR2 = (10, 9, 11, 6, 14, 2, 8, 5, 7, 13, 15, 1, 3, 4, 12)


def lanes(shape):
    return lax.broadcasted_iota(jnp.int32, shape, len(shape) - 1)


def rows_of(shape):
    return lax.broadcasted_iota(jnp.int32, shape, 0)


def roll_l(x, by):
    return pltpu.roll(x, by % x.shape[1], 1)


def ld(ref, start, n, blocks=ALL, stride=None):
    rows = pl.ds(start, n) if stride is None else pl.ds(start, n, stride=stride)
    return jnp.concatenate([ref[j, rows, :] for j in blocks], axis=1)


def st(ref, start, x, blocks=ALL, stride=None):
    n = x.shape[0]
    rows = pl.ds(start, n) if stride is None else pl.ds(start, n, stride=stride)
    for i, j in enumerate(blocks):
        ref[j, rows, :] = x[:, 128 * i:128 * (i + 1)]


def loop(r0, count, ch, body):
    for k in range(count // ch):
        body(r0 + k * ch)


class Level:
    def __init__(self, s, pad, n, f, e, so, west, ae, aw, as_, an, w, wf, v, v2, q, r=None):
        self.s, self.pad, self.n = s, pad, n
        self.f, self.e, self.so, self.west = f, e, so, west
        self.ae, self.aw, self.as_, self.an, self.w, self.wf = ae, aw, as_, an, w, wf
        self.v, self.v2, self.q, self.r = v, v2, q, v2 if r is None else r


def coeffs(l, ch, keep=None, source=False):
    def body(r):
        p = l.pad + r
        e, so, no = ld(l.e, p, ch), ld(l.so, p, ch), ld(l.so, p - 1, ch)
        we = roll_l(e, l.s)
        wk = OMEGA / (((e + we) + so) + no)
        if keep is not None:
            row = rows_of(wk.shape) + r
            wk = jnp.where((row >= keep[0]) & (row < keep[1]), wk, 0.0)
        st(l.west, p, we)
        st(l.ae, p, wk * e)
        st(l.aw, p, wk * we)
        st(l.as_, p, wk * so)
        st(l.an, p, wk * no)
        if source:
            st(l.wf, p, wk * ld(l.f, p, ch))
        else:
            st(l.w, p, wk)

    loop(0, l.n, ch, body)


def sweep(l, src, dst, source, r0, count, ch, blocks=ALL):
    def body(r):
        p = l.pad + r
        v = ld(src, p, ch, blocks)
        x = ld(l.ae, p, ch, blocks) * roll_l(v, -l.s) + ld(l.aw, p, ch, blocks) * roll_l(v, l.s)
        y = ld(l.as_, p, ch, blocks) * ld(src, p + 1, ch, blocks) + ld(l.an, p, ch, blocks) * ld(src, p - 1, ch, blocks)
        z = (1.0 - OMEGA) * v
        if source:
            z = z + ld(l.wf, p, ch, blocks)
        st(dst, p, (y + z) + x, blocks)

    loop(r0, count, ch, body)


def operator(l, v, p, ch):
    x = ld(v, p, ch)
    lon = ld(l.e, p, ch) * (x - roll_l(x, -l.s)) + ld(l.west, p, ch) * (x - roll_l(x, l.s))
    lat = ld(l.so, p, ch) * (x - ld(v, p + 1, ch)) + ld(l.so, p - 1, ch) * (x - ld(v, p - 1, ch))
    return x, lat + lon


def remainder(l, ch):
    def body(r):
        p = l.pad + r
        st(l.r, p, ld(l.f, p, ch) - operator(l, l.v, p, ch)[1])

    loop(0, l.n, ch, body)


def pair(ref, start, n, odd, blocks=ALL):
    return ld(ref, start + odd, n, blocks, 2)


def restrict(l, c):
    ch = min(16, c.n)

    def body(a):
        x = pair(l.r, l.pad + 2 * a, ch, 0) + pair(l.r, l.pad + 2 * a, ch, 1)
        x = x + roll_l(x, -l.s)
        st(c.f, c.pad + a, x)
        st(c.wf, c.pad + a, x * ld(c.w, c.pad + a, ch))

    for a in range(0, c.n, ch):
        body(a)


def coarsen(l, c):
    ch = min(16, c.n)
    for a in range(0, c.n, ch):
        x = pair(l.e, l.pad + 2 * a, ch, 0) + pair(l.e, l.pad + 2 * a, ch, 1)
        st(c.e, c.pad + a, roll_l(x, -l.s))
        y = pair(l.so, l.pad + 2 * a, ch, 1)
        st(c.so, c.pad + a, y + roll_l(y, -l.s))


def spread_rows(v, start, e, add, blocks=ALL):
    for odd in (0, 1):
        x = e
        if add:
            x = x + ld(v, start + odd, e.shape[0], blocks, 2)
        st(v, start + odd, x, blocks, 2)


def prolong(c, l, src, dst, a0, n, add, blocks=ALL):
    for a in range(0, n, 8):
        e = ld(src, c.pad + a0 + a, 8, blocks)
        e = jnp.where((lanes(e.shape) & l.s) == 0, e, roll_l(e, l.s))
        spread_rows(dst, l.pad + 2 * (a0 + a), e, add, blocks)


def pick(x, index):
    return jnp.take_along_axis(x, index, axis=1, mode="promise_in_bounds")


def compact(x, offset):
    l = lanes((8, 128))
    index = (l % 32) * 4 + offset
    out = pick(x[:, 384:512], index)
    for j in (2, 1, 0):
        out = jnp.where(l < 32 * (j + 1), pick(x[:, 128 * j:128 * (j + 1)], index), out)
    return out


def expand(x, base):
    l = lanes((8, 128))
    q = l // 4
    own = x[2, pl.ds(base, 8), :]
    parts = [pick(own, q + 32 * j) for j in range(4)]
    east = pick(x[3, pl.ds(base, 8), :], q)
    west = pick(x[1, pl.ds(base, 8), :], q + 96)
    return jnp.concatenate(parts + [jnp.where(l < 64, east, west)], axis=1)


def kernel(
    b_in, e_in, s_in, sol, res,
    g, pk, re_, rw_, a0, ag, c, t1, got1, t2, got2,
    *rest,
):
    fine0, fine1, fine2, fine3, fine4, fine5 = rest[:9], rest[9:22], rest[22:32], rest[32:45], rest[45:58], rest[58:72]
    in_sem, a_send, a_recv, cs_send, cs_recv, fs_send, fs_recv, c1_send, c1_recv, c2_send, c2_recv = rest[72:]

    l0 = Level(1, PAD, N0, g.at[0], g.at[1], g.at[2], *fine0[:5], None, *fine0[5:])
    l1 = Level(2, PAD, N0 // 2, *fine1)
    l2 = Level(1, PAD2, 64, c.at[0], c.at[1], c.at[2], *fine2)
    l3 = Level(2, PAD, 32, *fine3)
    l4 = Level(4, PAD, 16, *fine4)
    l5 = Level(8, PAD, 8, *fine5)
    lat, lon = lax.axis_index("lat"), lax.axis_index("lon")

    def device(dlon, dlat):
        return {"lon": lax.rem(lon + dlon + NLON, NLON), "lat": lax.rem(lat + dlat + NLAT, NLAT)}

    block = (lon // BLOCK) * BLOCK
    inner = lax.rem(lon, BLOCK)

    def mate1(d):
        return {"lon": block + lax.rem(inner + d, BLOCK), "lat": lat}

    def mate2(d):
        return device(BLOCK * (d // 4), d % 4)

    top = PAD + H
    loads = [
        pltpu.make_async_copy(x.at[:, pl.ds(128 * j, 128)], g.at[i, j, pl.ds(top, ROWS)], in_sem.at[i, j])
        for i, x in enumerate((b_in, e_in, s_in))
        for j in range(4)
    ]
    barrier = pltpu.get_barrier_semaphore()
    greeted = [device(*d) for d in HALO + SPREAD[:11]]
    greeted += [mate1(d) for d in range(1, BLOCK)] + [mate2(d) for d in range(4, 16)]
    for k, other in enumerate(greeted):
        pl.semaphore_signal(barrier, inc=1, device_id=other, device_id_type=MESH)
        if k == len(HALO) - 1:
            for copy in loads:
                copy.start()

    def clear(ref, l):
        zero = jnp.zeros((l.pad, WIDE), F32)
        st(ref, 0, zero)
        st(ref, l.pad + l.n, zero)

    for l in (l0, l1):
        for ref in (l.wf, l.v, l.v2, l.q):
            clear(ref, l)
    for l in (l2, l3, l4, l5):
        for ref in (l.wf, l.v, l.v2, l.q, l.so):
            clear(ref, l)
    for ref in (l2.ae, l2.aw, l2.as_, l2.an):
        clear(ref, l2)
    for ref in (l5.e, l5.r):
        clear(ref, l5)

    for copy in loads:
        copy.wait()

    l8 = lanes((8, 128))
    for k in range(ROWS // 8):
        rows = slice(top + 8 * k, top + 8 * k + 8)
        first = [g[i, 0, rows] for i in range(3)]
        last = [g[i, 3, rows] for i in range(3)]
        x = jnp.where(l8 < 16, first[0], jnp.where(l8 < 32, roll_l(first[1], 16), roll_l(first[2], 32)))
        y = jnp.where(l8 >= 112, last[0], jnp.where(l8 >= 96, roll_l(last[1], -16), roll_l(last[2], -32)))
        pk[8 * k:8 * k + 8] = jnp.where(l8 < 64, x, y)

    own_rows = pl.ds(pl.multiple_of(PAD2 + lat * 16, 16), 16)

    pl.semaphore_wait(barrier, len(greeted))

    def send(src, dst, s_sem, r_sem, k, to):
        copy = pltpu.make_async_remote_copy(
            src_ref=src, dst_ref=dst, send_sem=s_sem.at[k], recv_sem=r_sem.at[k], device_id=to, device_id_type=MESH
        )
        copy.start()
        return copy

    halos = []
    for k, (dlon, dlat) in enumerate(HALO):
        first_row, count = {0: (0, ROWS), 1: (ROWS - H, H), -1: (0, H)}[dlat]
        to = {0: H, 1: 0, -1: H + ROWS}[dlat]
        if dlon == 0:
            src = g.at[:, pl.ds(0, 4), pl.ds(top + first_row, count)]
            dst = g.at[:, pl.ds(0, 4), pl.ds(PAD + to, count)]
        else:
            src = pk.at[pl.ds(first_row, count)]
            dst = (rw_ if dlon == 1 else re_).at[pl.ds(to, count)]
        halos.append(send(src, dst, a_send, a_recv, k, device(dlon, dlat)))

    def spread_lat(index, s_sem, r_sem):
        part = c.at[index, 2, own_rows]
        return [send(part, part, s_sem, r_sem, k, device(0, d)) for k, d in enumerate(SPREAD_LAT)]

    def spread_lon(index, s_sem, r_sem):
        rows = pl.ds(PAD2, 64)
        return [
            send(c.at[index, 2, rows], c.at[index, 2 - d, rows], s_sem, r_sem, 3 + k, device(d, 0))
            for k, d in enumerate(SPREAD_LON)
        ]

    for a in range(0, 16, 8):
        x = ld(g.at[1], top + 4 * a, 8, range(4), 4)
        for j in (1, 2, 3):
            x = x + ld(g.at[1], top + 4 * a + j, 8, range(4), 4)
        y = ld(g.at[2], top + 4 * a + 3, 8, range(4), 4)
        y = y + roll_l(y, -1)
        y = y + roll_l(y, -2)
        rows = pl.ds(pl.multiple_of(PAD2 + lat * 16 + a, 8), 8)
        c[1, 2, rows, :] = compact(x, 3)
        c[2, 2, rows, :] = compact(y, 0)

    conds = spread_lat(pl.ds(1, 2), cs_send, cs_recv)

    for copy in halos:
        copy.wait_recv()

    has_north = jnp.where(lat > 0, 1.0, 0.0).astype(F32)
    used = (l8 < 16) | (l8 >= 112)
    for k in range(N0 // 8):
        x = jnp.where(l8 < 64, re_[8 * k:8 * k + 8], rw_[8 * k:8 * k + 8])
        for i, other in ((0, 0.0), (1, 1.0), (2, 1.0)):
            y = x if i == 0 else jnp.where(l8 < 64, roll_l(x, -16 * i), roll_l(x, 16 * i))
            g[i, 4, PAD + 8 * k:PAD + 8 * k + 8, :] = jnp.where(used, y, other)
    g[2, :, PAD:PAD + H] = g[2, :, PAD:PAD + H] * has_north

    def bounds(halo, own):
        return jnp.where(lat > 0, 0, halo), jnp.where(lat < NLAT - 1, 2 * halo + own, halo + own)

    coeffs(l0, 16, bounds(H, ROWS), True)
    sweep(l0, l0.wf, l0.v, True, 0, N0, 16)
    for copy in conds:
        copy.wait_recv()
    conds_lon = spread_lon(pl.ds(1, 2), cs_send, cs_recv)
    coarsen(l0, l1)
    remainder(l0, 16)
    coeffs(l1, 16, bounds(H // 2, ROWS // 2))
    restrict(l0, l1)
    sweep(l1, l1.wf, l1.v, True, 0, 48, 16)
    remainder(l1, 16)
    for a in range(0, 16, 8):
        x = ld(l1.r, PAD + 8 + 2 * a, 8, range(4), 2) + ld(l1.r, PAD + 9 + 2 * a, 8, range(4), 2)
        rows = pl.ds(pl.multiple_of(PAD2 + lat * 16 + a, 8), 8)
        c[0, 2, rows, :] = compact(x + roll_l(x, -2), 0)
    fields = [
        send(c.at[0, 2, own_rows], c.at[0, 2 - d[0], own_rows], fs_send, fs_recv, k, device(*d))
        for k, d in enumerate(SPREAD)
    ]

    for copy in conds_lon:
        copy.wait_recv()
    coeffs(l2, 16)
    coarsen(l2, l3)
    coeffs(l3, 16)
    coarsen(l3, l4)
    coeffs(l4, 16)
    coarsen(l4, l5)
    coeffs(l5, 8)


    def twice(l, v, source, r0, count, ch, blocks=ALL):
        sweep(l, v, l.v2, source, r0, count, ch, blocks)
        sweep(l, l.v2, v, source, r0, count, ch, blocks)

    def rise_coarse(name, source):
        u = [getattr(l, name) for l in (l0, l1, l2, l3, l4, l5)]
        twice(l5, u[5], source, 0, 8, 8, MID)
        prolong(l5, l4, u[5], u[4], 0, 8, source, MID)
        twice(l4, u[4], source, 0, 16, 16, MID)
        prolong(l4, l3, u[4], u[3], 0, 16, source, MID)
        twice(l3, u[3], source, 0, 32, 16, MID)
        near = lat * 8 - 4
        prolong(l3, l2, u[3], u[2], near, 16, source, MID)
        near = pl.multiple_of(lat * 16 - 8, 8)
        twice(l2, u[2], source, near, 32, 16, MID)

    def rise_fine(name, source):
        u = [getattr(l, name) for l in (l0, l1, l2)]
        for i in range(3):
            e = expand(u[2], PAD2 + lat * 16 - 4 + 8 * i)
            spread_rows(u[1], PAD + 16 * i, e, source)
        twice(l1, u[1], source, 0, 48, 16)
        prolong(l1, l0, u[1], u[0], 0, 48, source)
        twice(l0, u[0], source, 8, 80, 16)

    def applied(v, out, sums, n):
        def body(r, carry):
            x, av = operator(l0, v, top + r, 16)
            x, av = x[:, :COLS], av[:, :COLS]
            out[pl.ds(r, 16)] = av
            more = sums(pl.ds(r, 16), ld(l0.f, top + r, 16, range(4)), x, av)
            return tuple(y + (z[:8] + z[8:]) for y, z in zip(carry, more))

        carry = (jnp.zeros((8, COLS), F32),) * n
        for r in range(0, ROWS, 16):
            carry = body(r, carry)
        return carry

    st(l5.q, PAD, jnp.ones((8, WIDE), F32))
    rise_coarse("q", False)
    for copy in halos + conds:
        copy.wait_send()
    rise_fine("q", False)
    for copy in fields + conds_lon:
        copy.wait_send()
    sums_q = applied(l0.q, ag, lambda rows, b, v, av: (b * v, v * av), 2)

    for copy in fields:
        copy.wait_recv()

    def first(r):
        st(l2.wf, PAD2 + r, ld(l2.w, PAD2 + r, 16) * ld(l2.f, PAD2 + r, 16))

    loop(0, 64, 16, first)
    sweep(l2, l2.wf, l2.v, True, 0, 64, 16)
    remainder(l2, 16)
    for l, coarse in ((l2, l3), (l3, l4), (l4, l5)):
        restrict(l, coarse)
        sweep(coarse, coarse.wf, coarse.v, True, 0, coarse.n, min(16, coarse.n))
        remainder(coarse, min(16, coarse.n))

    x = pair(l5.r, PAD, 8, 0) + pair(l5.r, PAD, 8, 1)
    f6 = x + roll_l(x, -8)
    x = pair(l5.e, PAD, 8, 0) + pair(l5.e, PAD, 8, 1)
    e6 = roll_l(x, -8)
    x = pair(l5.so, PAD, 8, 1)
    s6 = x + roll_l(x, -8)
    row6, lane6 = rows_of((8, WIDE)), lanes((8, WIDE))
    west6 = roll_l(e6, 16)
    north6 = jnp.where(row6 == 0, 0.0, pltpu.roll(s6, 1, 0))
    w6 = jnp.where(row6 < 4, OMEGA / (((e6 + west6) + s6) + north6), 0.0)
    ae6, aw6, as6, an6, wf6 = w6 * e6, w6 * west6, w6 * s6, w6 * north6, w6 * f6
    field = wf6
    for _ in range(COARSE_SWEEPS - 1):
        x = ae6 * roll_l(field, -16) + aw6 * roll_l(field, 16)
        y = as6 * pltpu.roll(field, 7, 0) + an6 * pltpu.roll(field, 1, 0)
        field = (((1.0 - OMEGA) * field + wf6) + y) + x
    lon6 = e6 * (field - roll_l(field, -16)) + west6 * (field - roll_l(field, 16))
    lat6 = s6 * (field - pltpu.roll(field, 7, 0)) + north6 * (field - pltpu.roll(field, 1, 0))
    left = f6 - (lon6 + lat6)
    mine = ((lane6 & 15) == 0) & (lane6 >= 256) & (lane6 < 384)
    left = jnp.where(mine & (row6 == lat), left, 0.0)[:, 256:384]
    last = jnp.where(mine & (row6 == 3) & (lat == 3), s6, 0.0)[:, 256:384]

    e = jnp.where((lane6 & 8) == 0, field, roll_l(field, 8))
    for odd in (0, 1):
        st(l5.r, odd, e, ALL, 2)
    st(l5.v, PAD, ld(l5.v, PAD, 8) + ld(l5.r, 0, 8))
    rise_coarse("v", True)
    rise_fine("v", True)
    sums_v = applied(l0.v, a0, lambda rows, b, v, av: (b * v, v * av, v * ag[rows]), 3)

    def wait_all(got, sem):
        pltpu.make_async_copy(got, got, sem.at[0]).wait()

    def fold(x):
        return (x[:, 0:128] + x[:, 128:256]) + (x[:, 256:384] + x[:, 384:512])

    seven = [left, last, fold(sums_v[0]), fold(sums_q[0]), fold(sums_v[1]), fold(sums_v[2]), fold(sums_q[1])]
    row = rows_of((8, 128))
    total = jnp.zeros((8, 128), F32)
    for i, x in enumerate(seven):
        total = jnp.where(row == i, jnp.sum(x, axis=0, keepdims=True), total)
    t1[...] = total
    for d in FAR1:
        send(t1, got1.at[d - 1], c1_send, c1_recv, 0, mate1(d))
    wait_all(got1, c1_recv)

    def gathered(total, got):
        parts = [total] + [got[d] for d in range(15)]
        while len(parts) > 1:
            parts = [x + y for x, y in zip(parts[::2], parts[1::2])]
        return parts[0]

    total = gathered(total, got1)
    t2[...] = total
    for d in FAR2:
        send(t2, got2.at[d - 1], c2_send, c2_recv, 0, mate2(d))
    wait_all(got1, c1_send)
    wait_all(got2, c2_recv)
    total = gathered(total, got2)
    for by in (64, 32, 16, 8, 4, 2, 1):
        total = total + pltpu.roll(total, by, 1)
    n_left, n_last, bv, bq, vav, vaq, qaq = [total[i:i + 1] for i in range(7)]
    const = n_left / n_last
    step = (bv + const * bq) / ((vav + (2.0 * const) * vaq) + (const * const) * qaq)
    both = jnp.concatenate([step * const] * 4, axis=1)
    step = jnp.concatenate([step] * 4, axis=1)

    for r in range(0, ROWS, 16):
        rows = pl.ds(r, 16)
        sol[rows] = step * ld(l0.v, top + r, 16, range(4)) + both * ld(l0.q, top + r, 16, range(4))
        res[rows] = ld(l0.f, top + r, 16, range(4)) - (step * a0[rows] + both * ag[rows])
    wait_all(got2, c2_send)


def body(guidance, cond_lon, cond_lat):
    def vm(*shape):
        return pltpu.VMEM(shape, F32)

    def wide(n, count):
        return [vm(5, n, 128)] * count

    dma = pltpu.SemaphoreType.DMA
    scratch = [vm(3, 5, N0 + 2 * PAD, 128), vm(ROWS, 128), vm(N0, 128), vm(N0, 128), vm(ROWS, COLS), vm(ROWS, COLS)]
    scratch += [vm(3, 5, 64 + 2 * PAD2, 128), vm(8, 128), vm(15, 8, 128), vm(8, 128), vm(15, 8, 128)]
    scratch += wide(N0 + 2 * PAD, 9) + wide(N0 // 2 + 2 * PAD, 13) + wide(64 + 2 * PAD2, 10)
    scratch += wide(32 + 2 * PAD, 13) + wide(16 + 2 * PAD, 13) + wide(8 + 2 * PAD, 14)
    scratch += [dma((3, 4)), dma((8,)), dma((8,)), dma((7,)), dma((7,)), dma((19,)), dma((19,))] + [dma((1,))] * 4
    return pl.pallas_call(
        kernel,
        out_shape=(pltpu.VMEM((ROWS, COLS), F32),) * 2,
        in_specs=[pl.BlockSpec(memory_space=pltpu.HBM)] * 3,
        out_specs=(pl.BlockSpec(memory_space=pltpu.VMEM),) * 2,
        scratch_shapes=scratch,
        compiler_params=pltpu.CompilerParams(
            collective_id=0, has_side_effects=True, vmem_limit_bytes=60 * 1024 * 1024
        ),
        cost_estimate=pl.CostEstimate(flops=10_000_000, bytes_accessed=655360, transcendentals=0),
    )(guidance, cond_lon, cond_lat)


def solution(mesh):
    spec = P("lat", "lon")
    return jax.shard_map(body, mesh=mesh, in_specs=(spec,) * 3, out_specs=(spec,) * 2, check_vma=False)
```

```python
import jax
import jax.numpy as jnp
from jax import lax
from jax.experimental import pallas as pl
from jax.experimental.pallas import tpu as pltpu
from jax.sharding import PartitionSpec as P

OMEGA = 0.8
COARSE_SWEEPS = 8
NLAT, NLON, BLOCK = 4, 64, 16
ROWS, COLS = 64, 512
H = 16
PAD = 8
PAD2 = 16
N0 = ROWS + 2 * H
WIDE = COLS + 128
ALL = range(5)
MID = range(1, 4)
MESH = pl.DeviceIdType.MESH
F32 = jnp.float32

HALO = ((1, 1), (1, -1), (-1, 1), (-1, -1), (1, 0), (-1, 0), (0, 1), (0, -1))
SPREAD_LAT = (1, 2, 3)
SPREAD_LON = (2, -2, 1, -1)
SPREAD = ((2, 2), (-2, 2), (1, 2), (-1, 2), (2, 1), (2, -1), (-2, 1), (-2, -1), (0, 2), (2, 0), (-2, 0))
SPREAD += ((1, 1), (1, -1), (-1, 1), (-1, -1), (0, 1), (0, -1), (1, 0), (-1, 0))
FAR1 = (8, 7, 9, 6, 10, 5, 11, 4, 12, 3, 13, 2, 14, 1, 15)
FAR2 = (10, 9, 11, 6, 14, 2, 8, 5, 7, 13, 15, 1, 3, 4, 12)


def lanes(shape):
    return lax.broadcasted_iota(jnp.int32, shape, len(shape) - 1)


def rows_of(shape):
    return lax.broadcasted_iota(jnp.int32, shape, 0)


def roll_l(x, by):
    return pltpu.roll(x, by % x.shape[1], 1)


def ld(ref, start, n, blocks=ALL, stride=None):
    rows = pl.ds(start, n) if stride is None else pl.ds(start, n, stride=stride)
    return jnp.concatenate([ref[j, rows, :] for j in blocks], axis=1)


def st(ref, start, x, blocks=ALL, stride=None):
    n = x.shape[0]
    rows = pl.ds(start, n) if stride is None else pl.ds(start, n, stride=stride)
    for i, j in enumerate(blocks):
        ref[j, rows, :] = x[:, 128 * i:128 * (i + 1)]


def loop(r0, count, ch, body):
    for k in range(count // ch):
        body(r0 + k * ch)


class Level:
    def __init__(self, s, pad, n, f, e, so, west, ae, aw, as_, an, w, wf, v, v2, q, r=None):
        self.s, self.pad, self.n = s, pad, n
        self.f, self.e, self.so, self.west = f, e, so, west
        self.ae, self.aw, self.as_, self.an, self.w, self.wf = ae, aw, as_, an, w, wf
        self.v, self.v2, self.q, self.r = v, v2, q, v2 if r is None else r


def coeffs(l, ch, keep=None, source=False):
    def body(r):
        p = l.pad + r
        e, so, no = ld(l.e, p, ch), ld(l.so, p, ch), ld(l.so, p - 1, ch)
        we = roll_l(e, l.s)
        wk = OMEGA / (((e + we) + so) + no)
        if keep is not None:
            row = rows_of(wk.shape) + r
            wk = jnp.where((row >= keep[0]) & (row < keep[1]), wk, 0.0)
        st(l.west, p, we)
        st(l.ae, p, wk * e)
        st(l.aw, p, wk * we)
        st(l.as_, p, wk * so)
        st(l.an, p, wk * no)
        if source:
            st(l.wf, p, wk * ld(l.f, p, ch))
        else:
            st(l.w, p, wk)

    loop(0, l.n, ch, body)


def sweep(l, src, dst, source, r0, count, ch, blocks=ALL):
    def body(r):
        p = l.pad + r
        v = ld(src, p, ch, blocks)
        x = ld(l.ae, p, ch, blocks) * roll_l(v, -l.s) + ld(l.aw, p, ch, blocks) * roll_l(v, l.s)
        y = ld(l.as_, p, ch, blocks) * ld(src, p + 1, ch, blocks) + ld(l.an, p, ch, blocks) * ld(src, p - 1, ch, blocks)
        z = (1.0 - OMEGA) * v
        if source:
            z = z + ld(l.wf, p, ch, blocks)
        st(dst, p, (y + z) + x, blocks)

    loop(r0, count, ch, body)


def operator(l, v, p, ch):
    x = ld(v, p, ch)
    lon = ld(l.e, p, ch) * (x - roll_l(x, -l.s)) + ld(l.west, p, ch) * (x - roll_l(x, l.s))
    lat = ld(l.so, p, ch) * (x - ld(v, p + 1, ch)) + ld(l.so, p - 1, ch) * (x - ld(v, p - 1, ch))
    return x, lat + lon


def remainder(l, ch):
    def body(r):
        p = l.pad + r
        st(l.r, p, ld(l.f, p, ch) - operator(l, l.v, p, ch)[1])

    loop(0, l.n, ch, body)


def pair(ref, start, n, odd, blocks=ALL):
    return ld(ref, start + odd, n, blocks, 2)


def restrict(l, c):
    ch = min(16, c.n)

    def body(a):
        x = pair(l.r, l.pad + 2 * a, ch, 0) + pair(l.r, l.pad + 2 * a, ch, 1)
        x = x + roll_l(x, -l.s)
        st(c.f, c.pad + a, x)
        st(c.wf, c.pad + a, x * ld(c.w, c.pad + a, ch))

    for a in range(0, c.n, ch):
        body(a)


def coarsen(l, c):
    ch = min(16, c.n)
    for a in range(0, c.n, ch):
        x = pair(l.e, l.pad + 2 * a, ch, 0) + pair(l.e, l.pad + 2 * a, ch, 1)
        st(c.e, c.pad + a, roll_l(x, -l.s))
        y = pair(l.so, l.pad + 2 * a, ch, 1)
        st(c.so, c.pad + a, y + roll_l(y, -l.s))


def spread_rows(v, start, e, add, blocks=ALL):
    for odd in (0, 1):
        x = e
        if add:
            x = x + ld(v, start + odd, e.shape[0], blocks, 2)
        st(v, start + odd, x, blocks, 2)


def prolong(c, l, src, dst, a0, n, add, blocks=ALL):
    for a in range(0, n, 8):
        e = ld(src, c.pad + a0 + a, 8, blocks)
        e = jnp.where((lanes(e.shape) & l.s) == 0, e, roll_l(e, l.s))
        spread_rows(dst, l.pad + 2 * (a0 + a), e, add, blocks)


def pick(x, index):
    return jnp.take_along_axis(x, index, axis=1, mode="promise_in_bounds")


def compact(x, offset):
    l = lanes((8, 128))
    index = (l % 32) * 4 + offset
    out = pick(x[:, 384:512], index)
    for j in (2, 1, 0):
        out = jnp.where(l < 32 * (j + 1), pick(x[:, 128 * j:128 * (j + 1)], index), out)
    return out


def expand(x, base):
    l = lanes((8, 128))
    q = l // 4
    own = x[2, pl.ds(base, 8), :]
    parts = [pick(own, q + 32 * j) for j in range(4)]
    east = pick(x[3, pl.ds(base, 8), :], q)
    west = pick(x[1, pl.ds(base, 8), :], q + 96)
    return jnp.concatenate(parts + [jnp.where(l < 64, east, west)], axis=1)


def kernel(
    b_in, e_in, s_in, sol, res,
    g, pk, re_, rw_, a0, ag, c, t1, got1, t2, got2, l6,
    *rest,
):
    fine0, fine1, fine2, fine3, fine4, fine5 = rest[:9], rest[9:22], rest[22:32], rest[32:45], rest[45:58], rest[58:72]
    in_sem, a_send, a_recv, cs_send, cs_recv, fs_send, fs_recv, c1_send, c1_recv, c2_send, c2_recv, token = rest[72:]

    l0 = Level(1, PAD, N0, g.at[0], g.at[1], g.at[2], *fine0[:5], None, *fine0[5:])
    l1 = Level(2, PAD, N0 // 2, *fine1)
    l2 = Level(1, PAD2, 64, c.at[0], c.at[1], c.at[2], *fine2)
    l3 = Level(2, PAD, 32, *fine3)
    l4 = Level(4, PAD, 16, *fine4)
    l5 = Level(8, PAD, 8, *fine5)
    lat, lon = lax.axis_index("lat"), lax.axis_index("lon")

    def device(dlon, dlat):
        return {"lon": lax.rem(lon + dlon + NLON, NLON), "lat": lax.rem(lat + dlat + NLAT, NLAT)}

    block = (lon // BLOCK) * BLOCK
    inner = lax.rem(lon, BLOCK)

    def mate1(d):
        return {"lon": block + lax.rem(inner + d, BLOCK), "lat": lat}

    def mate2(d):
        return device(BLOCK * (d // 4), d % 4)

    top = PAD + H
    loads = [
        pltpu.make_async_copy(x.at[:, pl.ds(128 * j, 128)], g.at[i, j, pl.ds(top, ROWS)], in_sem.at[i, j])
        for i, x in enumerate((b_in, e_in, s_in))
        for j in range(4)
    ]
    barrier = pltpu.get_barrier_semaphore()
    greeted = [device(*d) for d in HALO + ((0, 2),)]
    for other in greeted:
        pl.semaphore_signal(barrier, inc=1, device_id=other, device_id_type=MESH)
    for copy in loads:
        copy.start()

    def tell(k):
        for s in (2 << k, -(2 << k)):
            pl.semaphore_signal(token.at[k], inc=1, device_id=device(s, 0), device_id_type=MESH)

    def hear(k):
        pl.semaphore_wait(token.at[k], 2)

    def clear(ref, l):
        zero = jnp.zeros((l.pad, WIDE), F32)
        st(ref, 0, zero)
        st(ref, l.pad + l.n, zero)

    for l in (l0, l1):
        for ref in (l.wf, l.v, l.v2, l.q):
            clear(ref, l)
    for l in (l2, l3, l4, l5):
        for ref in (l.wf, l.v, l.v2, l.q, l.so):
            clear(ref, l)
    for ref in (l2.ae, l2.aw, l2.as_, l2.an):
        clear(ref, l2)
    for ref in (l5.e, l5.r):
        clear(ref, l5)

    for copy in loads:
        copy.wait()

    l8 = lanes((8, 128))
    for k in range(ROWS // 8):
        rows = slice(top + 8 * k, top + 8 * k + 8)
        first = [g[i, 0, rows] for i in range(3)]
        last = [g[i, 3, rows] for i in range(3)]
        x = jnp.where(l8 < 16, first[0], jnp.where(l8 < 32, roll_l(first[1], 16), roll_l(first[2], 32)))
        y = jnp.where(l8 >= 112, last[0], jnp.where(l8 >= 96, roll_l(last[1], -16), roll_l(last[2], -32)))
        pk[8 * k:8 * k + 8] = jnp.where(l8 < 64, x, y)

    own_rows = pl.ds(pl.multiple_of(PAD2 + lat * 16, 16), 16)

    pl.semaphore_wait(barrier, len(greeted))

    def send(src, dst, s_sem, r_sem, k, to):
        copy = pltpu.make_async_remote_copy(
            src_ref=src, dst_ref=dst, send_sem=s_sem.at[k], recv_sem=r_sem.at[k], device_id=to, device_id_type=MESH
        )
        copy.start()
        return copy

    halos = []
    for k, (dlon, dlat) in enumerate(HALO):
        first_row, count = {0: (0, ROWS), 1: (ROWS - H, H), -1: (0, H)}[dlat]
        to = {0: H, 1: 0, -1: H + ROWS}[dlat]
        if dlon == 0:
            src = g.at[:, pl.ds(0, 4), pl.ds(top + first_row, count)]
            dst = g.at[:, pl.ds(0, 4), pl.ds(PAD + to, count)]
        else:
            src = pk.at[pl.ds(first_row, count)]
            dst = (rw_ if dlon == 1 else re_).at[pl.ds(to, count)]
        halos.append(send(src, dst, a_send, a_recv, k, device(dlon, dlat)))

    def spread_lat(index, s_sem, r_sem):
        part = c.at[index, 2, own_rows]
        return [send(part, part, s_sem, r_sem, k, device(0, d)) for k, d in enumerate(SPREAD_LAT)]

    def spread_lon(index, s_sem, r_sem):
        rows = pl.ds(PAD2, 64)
        return [
            send(c.at[index, 2, rows], c.at[index, 2 - d, rows], s_sem, r_sem, 3 + k, device(d, 0))
            for k, d in enumerate(SPREAD_LON)
        ]

    for a in range(0, 16, 8):
        x = ld(g.at[1], top + 4 * a, 8, range(4), 4)
        for j in (1, 2, 3):
            x = x + ld(g.at[1], top + 4 * a + j, 8, range(4), 4)
        y = ld(g.at[2], top + 4 * a + 3, 8, range(4), 4)
        y = y + roll_l(y, -1)
        y = y + roll_l(y, -2)
        rows = pl.ds(pl.multiple_of(PAD2 + lat * 16 + a, 8), 8)
        c[1, 2, rows, :] = compact(x, 3)
        c[2, 2, rows, :] = compact(y, 0)

    conds = spread_lat(pl.ds(1, 2), cs_send, cs_recv)

    for copy in halos:
        copy.wait_recv()

    tell(0)
    has_north = jnp.where(lat > 0, 1.0, 0.0).astype(F32)
    used = (l8 < 16) | (l8 >= 112)
    for k in range(N0 // 8):
        x = jnp.where(l8 < 64, re_[8 * k:8 * k + 8], rw_[8 * k:8 * k + 8])
        for i, other in ((0, 0.0), (1, 1.0), (2, 1.0)):
            y = x if i == 0 else jnp.where(l8 < 64, roll_l(x, -16 * i), roll_l(x, 16 * i))
            g[i, 4, PAD + 8 * k:PAD + 8 * k + 8, :] = jnp.where(used, y, other)
    g[2, :, PAD:PAD + H] = g[2, :, PAD:PAD + H] * has_north

    def bounds(halo, own):
        return jnp.where(lat > 0, 0, halo), jnp.where(lat < NLAT - 1, 2 * halo + own, halo + own)

    coeffs(l0, 16, bounds(H, ROWS), True)
    sweep(l0, l0.wf, l0.v, True, 0, N0, 16)
    for copy in conds:
        copy.wait_recv()
    conds_lon = spread_lon(pl.ds(1, 2), cs_send, cs_recv)
    coarsen(l0, l1)
    remainder(l0, 16)
    coeffs(l1, 16, bounds(H // 2, ROWS // 2))
    restrict(l0, l1)
    sweep(l1, l1.wf, l1.v, True, 0, 48, 16)
    remainder(l1, 16)
    for a in range(0, 16, 8):
        x = ld(l1.r, PAD + 8 + 2 * a, 8, range(4), 2) + ld(l1.r, PAD + 9 + 2 * a, 8, range(4), 2)
        rows = pl.ds(pl.multiple_of(PAD2 + lat * 16 + a, 8), 8)
        c[0, 2, rows, :] = compact(x + roll_l(x, -2), 0)
    fields = [
        send(c.at[0, 2, own_rows], c.at[0, 2 - d[0], own_rows], fs_send, fs_recv, k, device(*d))
        for k, d in enumerate(SPREAD)
    ]

    hear(0)
    tell(1)
    for copy in conds_lon:
        copy.wait_recv()
    coeffs(l2, 16)
    coarsen(l2, l3)
    coeffs(l3, 16)
    coarsen(l3, l4)
    coeffs(l4, 16)
    coarsen(l4, l5)
    coeffs(l5, 8)


    def twice(l, v, source, r0, count, ch, blocks=ALL):
        sweep(l, v, l.v2, source, r0, count, ch, blocks)
        sweep(l, l.v2, v, source, r0, count, ch, blocks)

    def rise_coarse(name, source):
        u = [getattr(l, name) for l in (l0, l1, l2, l3, l4, l5)]
        twice(l5, u[5], source, 0, 8, 8, MID)
        prolong(l5, l4, u[5], u[4], 0, 8, source, MID)
        twice(l4, u[4], source, 0, 16, 16, MID)
        prolong(l4, l3, u[4], u[3], 0, 16, source, MID)
        twice(l3, u[3], source, 0, 32, 16, MID)
        near = lat * 8 - 4
        prolong(l3, l2, u[3], u[2], near, 16, source, MID)
        near = pl.multiple_of(lat * 16 - 8, 8)
        twice(l2, u[2], source, near, 32, 16, MID)

    def rise_fine(name, source):
        u = [getattr(l, name) for l in (l0, l1, l2)]
        for i in range(3):
            e = expand(u[2], PAD2 + lat * 16 - 4 + 8 * i)
            spread_rows(u[1], PAD + 16 * i, e, source)
        twice(l1, u[1], source, 0, 48, 16)
        prolong(l1, l0, u[1], u[0], 0, 48, source)
        twice(l0, u[0], source, 8, 80, 16)

    def applied(v, out, sums, n):
        def body(r, carry):
            x, av = operator(l0, v, top + r, 16)
            x, av = x[:, :COLS], av[:, :COLS]
            out[pl.ds(r, 16)] = av
            more = sums(pl.ds(r, 16), ld(l0.f, top + r, 16, range(4)), x, av)
            return tuple(y + (z[:8] + z[8:]) for y, z in zip(carry, more))

        carry = (jnp.zeros((8, COLS), F32),) * n
        for r in range(0, ROWS, 16):
            carry = body(r, carry)
        return carry

    x = pair(l5.e, PAD, 8, 0) + pair(l5.e, PAD, 8, 1)
    e6 = roll_l(x, -8)
    x = pair(l5.so, PAD, 8, 1)
    s6 = x + roll_l(x, -8)
    row6, lane6 = rows_of((8, WIDE)), lanes((8, WIDE))
    west6 = roll_l(e6, 16)
    north6 = jnp.where(row6 == 0, 0.0, pltpu.roll(s6, 1, 0))
    w6 = jnp.where(row6 < 4, OMEGA / (((e6 + west6) + s6) + north6), 0.0)
    for i, x in enumerate((e6, west6, s6, north6, w6, w6 * e6, w6 * west6, w6 * s6, w6 * north6)):
        st(l6, 8 * i, x)

    st(l5.q, PAD, jnp.ones((8, WIDE), F32))
    rise_coarse("q", False)
    for copy in halos + conds:
        copy.wait_send()
    rise_fine("q", False)
    for copy in fields + conds_lon:
        copy.wait_send()
    sums_q = applied(l0.q, ag, lambda rows, b, v, av: (b * v, v * av), 2)

    hear(1)
    tell(2)
    for copy in fields:
        copy.wait_recv()

    def first(r):
        st(l2.wf, PAD2 + r, ld(l2.w, PAD2 + r, 16) * ld(l2.f, PAD2 + r, 16))

    loop(0, 64, 16, first)
    sweep(l2, l2.wf, l2.v, True, 0, 64, 16)
    remainder(l2, 16)
    for l, coarse in ((l2, l3), (l3, l4), (l4, l5)):
        restrict(l, coarse)
        sweep(coarse, coarse.wf, coarse.v, True, 0, coarse.n, min(16, coarse.n))
        remainder(coarse, min(16, coarse.n))

    x = pair(l5.r, PAD, 8, 0) + pair(l5.r, PAD, 8, 1)
    f6 = x + roll_l(x, -8)
    e6, west6, s6, north6, w6, ae6, aw6, as6, an6 = [ld(l6, 8 * i, 8) for i in range(9)]
    wf6 = w6 * f6
    field = wf6
    for _ in range(COARSE_SWEEPS - 1):
        x = ae6 * roll_l(field, -16) + aw6 * roll_l(field, 16)
        y = as6 * pltpu.roll(field, 7, 0) + an6 * pltpu.roll(field, 1, 0)
        field = (((1.0 - OMEGA) * field + wf6) + y) + x
    lon6 = e6 * (field - roll_l(field, -16)) + west6 * (field - roll_l(field, 16))
    lat6 = s6 * (field - pltpu.roll(field, 7, 0)) + north6 * (field - pltpu.roll(field, 1, 0))
    left = f6 - (lon6 + lat6)
    mine = ((lane6 & 15) == 0) & (lane6 >= 256) & (lane6 < 384)
    left = jnp.where(mine & (row6 == lat), left, 0.0)[:, 256:384]
    last = jnp.where(mine & (row6 == 3) & (lat == 3), s6, 0.0)[:, 256:384]

    e = jnp.where((lane6 & 8) == 0, field, roll_l(field, 8))
    for odd in (0, 1):
        st(l5.r, odd, e, ALL, 2)
    st(l5.v, PAD, ld(l5.v, PAD, 8) + ld(l5.r, 0, 8))
    rise_coarse("v", True)
    hear(2)
    tell(3)
    rise_fine("v", True)
    sums_v = applied(l0.v, a0, lambda rows, b, v, av: (b * v, v * av, v * ag[rows]), 3)

    def wait_all(got, sem):
        pltpu.make_async_copy(got, got, sem.at[0]).wait()

    def fold(x):
        return (x[:, 0:128] + x[:, 128:256]) + (x[:, 256:384] + x[:, 384:512])

    seven = [left, last, fold(sums_v[0]), fold(sums_q[0]), fold(sums_v[1]), fold(sums_v[2]), fold(sums_q[1])]
    row = rows_of((8, 128))
    total = jnp.zeros((8, 128), F32)
    for i, x in enumerate(seven):
        total = jnp.where(row == i, jnp.sum(x, axis=0, keepdims=True), total)
    t1[...] = total
    for d in FAR1:
        send(t1, got1.at[d - 1], c1_send, c1_recv, 0, mate1(d))
    wait_all(got1, c1_recv)

    def gathered(total, got):
        parts = [total] + [got[d] for d in range(15)]
        while len(parts) > 1:
            parts = [x + y for x, y in zip(parts[::2], parts[1::2])]
        return parts[0]

    total = gathered(total, got1)
    hear(3)
    t2[...] = total
    for d in FAR2:
        send(t2, got2.at[d - 1], c2_send, c2_recv, 0, mate2(d))
    wait_all(got1, c1_send)
    wait_all(got2, c2_recv)
    total = gathered(total, got2)
    for by in (64, 32, 16, 8, 4, 2, 1):
        total = total + pltpu.roll(total, by, 1)
    n_left, n_last, bv, bq, vav, vaq, qaq = [total[i:i + 1] for i in range(7)]
    const = n_left / n_last
    step = (bv + const * bq) / ((vav + (2.0 * const) * vaq) + (const * const) * qaq)
    both = jnp.concatenate([step * const] * 4, axis=1)
    step = jnp.concatenate([step] * 4, axis=1)

    for r in range(0, ROWS, 16):
        rows = pl.ds(r, 16)
        sol[rows] = step * ld(l0.v, top + r, 16, range(4)) + both * ld(l0.q, top + r, 16, range(4))
        res[rows] = ld(l0.f, top + r, 16, range(4)) - (step * a0[rows] + both * ag[rows])
    wait_all(got2, c2_send)


def body(guidance, cond_lon, cond_lat):
    def vm(*shape):
        return pltpu.VMEM(shape, F32)

    def wide(n, count):
        return [vm(5, n, 128)] * count

    dma = pltpu.SemaphoreType.DMA
    scratch = [vm(3, 5, N0 + 2 * PAD, 128), vm(ROWS, 128), vm(N0, 128), vm(N0, 128), vm(ROWS, COLS), vm(ROWS, COLS)]
    scratch += [vm(3, 5, 64 + 2 * PAD2, 128), vm(8, 128), vm(15, 8, 128), vm(8, 128), vm(15, 8, 128), vm(5, 72, 128)]
    scratch += wide(N0 + 2 * PAD, 9) + wide(N0 // 2 + 2 * PAD, 13) + wide(64 + 2 * PAD2, 10)
    scratch += wide(32 + 2 * PAD, 13) + wide(16 + 2 * PAD, 13) + wide(8 + 2 * PAD, 14)
    scratch += [dma((3, 4)), dma((8,)), dma((8,)), dma((7,)), dma((7,)), dma((19,)), dma((19,))] + [dma((1,))] * 4 + [pltpu.SemaphoreType.REGULAR((4,))]
    return pl.pallas_call(
        kernel,
        out_shape=(pltpu.VMEM((ROWS, COLS), F32),) * 2,
        in_specs=[pl.BlockSpec(memory_space=pltpu.HBM)] * 3,
        out_specs=(pl.BlockSpec(memory_space=pltpu.VMEM),) * 2,
        scratch_shapes=scratch,
        compiler_params=pltpu.CompilerParams(
            collective_id=0, has_side_effects=True, vmem_limit_bytes=60 * 1024 * 1024
        ),
        cost_estimate=pl.CostEstimate(flops=10_000_000, bytes_accessed=655360, transcendentals=0),
    )(guidance, cond_lon, cond_lat)


def solution(mesh):
    spec = P("lat", "lon")
    return jax.shard_map(body, mesh=mesh, in_specs=(spec,) * 3, out_specs=(spec,) * 2, check_vma=False)
```

```python
import jax
import jax.numpy as jnp
from jax import lax
from jax.experimental import pallas as pl
from jax.experimental.pallas import tpu as pltpu
from jax.sharding import PartitionSpec as P

OMEGA = 0.8
COARSE_SWEEPS = 8
NLAT, NLON, BLOCK = 4, 64, 16
ROWS, COLS = 64, 512
H = 16
PAD = 8
PAD2 = 16
N0 = ROWS + 2 * H
WIDE = COLS + 128
ALL = range(5)
MID = range(1, 4)
MESH = pl.DeviceIdType.MESH
F32 = jnp.float32

HALO = ((1, 1), (1, -1), (-1, 1), (-1, -1), (1, 0), (-1, 0), (0, 1), (0, -1))
SPREAD_LAT = (1, 2, 3)
SPREAD_LON = (2, -2, 1, -1)
SPREAD = ((2, 2), (-2, 2), (1, 2), (-1, 2), (2, 1), (2, -1), (-2, 1), (-2, -1), (0, 2), (2, 0), (-2, 0))
SPREAD += ((1, 1), (1, -1), (-1, 1), (-1, -1), (0, 1), (0, -1), (1, 0), (-1, 0))
FAR1 = (8, 7, 9, 6, 10, 5, 11, 4, 12, 3, 13, 2, 14, 1, 15)
FAR2 = (10, 9, 11, 6, 14, 2, 8, 5, 7, 13, 15, 1, 3, 4, 12)


def lanes(shape):
    return lax.broadcasted_iota(jnp.int32, shape, len(shape) - 1)


def rows_of(shape):
    return lax.broadcasted_iota(jnp.int32, shape, 0)


def roll_l(x, by):
    return pltpu.roll(x, by % x.shape[1], 1)


def ld(ref, start, n, blocks=ALL, stride=None):
    rows = pl.ds(start, n) if stride is None else pl.ds(start, n, stride=stride)
    return jnp.concatenate([ref[j, rows, :] for j in blocks], axis=1)


def st(ref, start, x, blocks=ALL, stride=None):
    n = x.shape[0]
    rows = pl.ds(start, n) if stride is None else pl.ds(start, n, stride=stride)
    for i, j in enumerate(blocks):
        ref[j, rows, :] = x[:, 128 * i:128 * (i + 1)]


def loop(r0, count, ch, body):
    for k in range(count // ch):
        body(r0 + k * ch)


class Level:
    def __init__(self, s, pad, n, f, e, so, west, ae, aw, as_, an, w, wf, v, v2, q, r=None):
        self.s, self.pad, self.n = s, pad, n
        self.f, self.e, self.so, self.west = f, e, so, west
        self.ae, self.aw, self.as_, self.an, self.w, self.wf = ae, aw, as_, an, w, wf
        self.v, self.v2, self.q, self.r = v, v2, q, v2 if r is None else r


def coeffs(l, ch, keep=None, source=False, r0=0, count=None):
    def body(r):
        p = l.pad + r
        e, so, no = ld(l.e, p, ch), ld(l.so, p, ch), ld(l.so, p - 1, ch)
        we = roll_l(e, l.s)
        wk = OMEGA / (((e + we) + so) + no)
        if keep is not None:
            row = rows_of(wk.shape) + r
            wk = jnp.where((row >= keep[0]) & (row < keep[1]), wk, 0.0)
        st(l.west, p, we)
        st(l.ae, p, wk * e)
        st(l.aw, p, wk * we)
        st(l.as_, p, wk * so)
        st(l.an, p, wk * no)
        if source:
            st(l.wf, p, wk * ld(l.f, p, ch))
        else:
            st(l.w, p, wk)

    loop(r0, l.n if count is None else count, ch, body)


def sweep(l, src, dst, source, r0, count, ch, blocks=ALL):
    def body(r):
        p = l.pad + r
        v = ld(src, p, ch, blocks)
        x = ld(l.ae, p, ch, blocks) * roll_l(v, -l.s) + ld(l.aw, p, ch, blocks) * roll_l(v, l.s)
        y = ld(l.as_, p, ch, blocks) * ld(src, p + 1, ch, blocks) + ld(l.an, p, ch, blocks) * ld(src, p - 1, ch, blocks)
        z = (1.0 - OMEGA) * v
        if source:
            z = z + ld(l.wf, p, ch, blocks)
        st(dst, p, (y + z) + x, blocks)

    loop(r0, count, ch, body)


def operator(l, v, p, ch):
    x = ld(v, p, ch)
    lon = ld(l.e, p, ch) * (x - roll_l(x, -l.s)) + ld(l.west, p, ch) * (x - roll_l(x, l.s))
    lat = ld(l.so, p, ch) * (x - ld(v, p + 1, ch)) + ld(l.so, p - 1, ch) * (x - ld(v, p - 1, ch))
    return x, lat + lon


def remainder(l, ch, r0=0, count=None):
    def body(r):
        p = l.pad + r
        st(l.r, p, ld(l.f, p, ch) - operator(l, l.v, p, ch)[1])

    loop(r0, l.n if count is None else count, ch, body)


def pair(ref, start, n, odd, blocks=ALL):
    return ld(ref, start + odd, n, blocks, 2)


def restrict(l, c, a0=0, count=None):
    count = c.n if count is None else count
    ch = min(16, count)

    def body(a):
        x = pair(l.r, l.pad + 2 * a, ch, 0) + pair(l.r, l.pad + 2 * a, ch, 1)
        x = x + roll_l(x, -l.s)
        st(c.f, c.pad + a, x)
        st(c.wf, c.pad + a, x * ld(c.w, c.pad + a, ch))

    for a in range(a0, a0 + count, ch):
        body(a)


def coarsen(l, c, a0=0, count=None):
    count = c.n if count is None else count
    ch = min(16, count)
    for a in range(a0, a0 + count, ch):
        x = pair(l.e, l.pad + 2 * a, ch, 0) + pair(l.e, l.pad + 2 * a, ch, 1)
        st(c.e, c.pad + a, roll_l(x, -l.s))
        y = pair(l.so, l.pad + 2 * a, ch, 1)
        st(c.so, c.pad + a, y + roll_l(y, -l.s))


def spread_rows(v, start, e, add, blocks=ALL):
    for odd in (0, 1):
        x = e
        if add:
            x = x + ld(v, start + odd, e.shape[0], blocks, 2)
        st(v, start + odd, x, blocks, 2)


def prolong(c, l, src, dst, a0, n, add, blocks=ALL):
    for a in range(0, n, 8):
        e = ld(src, c.pad + a0 + a, 8, blocks)
        e = jnp.where((lanes(e.shape) & l.s) == 0, e, roll_l(e, l.s))
        spread_rows(dst, l.pad + 2 * (a0 + a), e, add, blocks)


def pick(x, index):
    return jnp.take_along_axis(x, index, axis=1, mode="promise_in_bounds")


def compact(x, offset):
    l = lanes((8, 128))
    index = (l % 32) * 4 + offset
    out = pick(x[:, 384:512], index)
    for j in (2, 1, 0):
        out = jnp.where(l < 32 * (j + 1), pick(x[:, 128 * j:128 * (j + 1)], index), out)
    return out


def expand(x, base):
    l = lanes((8, 128))
    q = l // 4
    own = x[2, pl.ds(base, 8), :]
    parts = [pick(own, q + 32 * j) for j in range(4)]
    east = pick(x[3, pl.ds(base, 8), :], q)
    west = pick(x[1, pl.ds(base, 8), :], q + 96)
    return jnp.concatenate(parts + [jnp.where(l < 64, east, west)], axis=1)


def kernel(
    b_in, e_in, s_in, sol, res,
    g, pk, re_, rw_, a0, ag, c, t1, got1, t2, got2, l6, far,
    *rest,
):
    fine0, fine1, fine2, fine3, fine4, fine5 = rest[:9], rest[9:22], rest[22:32], rest[32:45], rest[45:58], rest[58:72]
    in_sem, a_send, a_recv, cs_send, cs_recv, fs_send, fs_recv, c1_send, c1_recv, c2_send, c2_recv = rest[72:]

    l0 = Level(1, PAD, N0, g.at[0], g.at[1], g.at[2], *fine0[:5], None, *fine0[5:])
    l1 = Level(2, PAD, N0 // 2, *fine1)
    l2 = Level(1, PAD2, 64, c.at[0], c.at[1], c.at[2], *fine2)
    l3 = Level(2, PAD, 32, *fine3)
    l4 = Level(4, PAD, 16, *fine4)
    l5 = Level(8, PAD, 8, *fine5)
    lat, lon = lax.axis_index("lat"), lax.axis_index("lon")

    def device(dlon, dlat):
        return {"lon": lax.rem(lon + dlon + NLON, NLON), "lat": lax.rem(lat + dlat + NLAT, NLAT)}

    block = (lon // BLOCK) * BLOCK
    inner = lax.rem(lon, BLOCK)

    def mate1(d):
        return {"lon": block + lax.rem(inner + d, BLOCK), "lat": lat}

    def mate2(d):
        return device(BLOCK * (d // 4), d % 4)

    top = PAD + H
    loads = [
        pltpu.make_async_copy(x.at[:, pl.ds(128 * j, 128)], g.at[i, j, pl.ds(top, ROWS)], in_sem.at[i, j])
        for i, x in enumerate((b_in, e_in, s_in))
        for j in range(4)
    ]
    barrier = pltpu.get_barrier_semaphore()
    greeted = [device(*d) for d in HALO + SPREAD[:11]]
    greeted += [mate1(d) for d in range(1, BLOCK)] + [mate2(d) for d in range(4, 16)]
    for k, other in enumerate(greeted):
        pl.semaphore_signal(barrier, inc=1, device_id=other, device_id_type=MESH)
        if k == len(HALO) - 1:
            for copy in loads:
                copy.start()

    def clear(ref, l):
        zero = jnp.zeros((l.pad, WIDE), F32)
        st(ref, 0, zero)
        st(ref, l.pad + l.n, zero)

    for l in (l0, l1):
        for ref in (l.wf, l.v, l.v2, l.q):
            clear(ref, l)
    for l in (l2, l3, l4, l5):
        for ref in (l.wf, l.v, l.v2, l.q, l.so):
            clear(ref, l)
    for ref in (l2.ae, l2.aw, l2.as_, l2.an):
        clear(ref, l2)
    for ref in (l5.e, l5.r):
        clear(ref, l5)

    for copy in loads:
        copy.wait()

    l8 = lanes((8, 128))
    for k in range(ROWS // 8):
        rows = slice(top + 8 * k, top + 8 * k + 8)
        first = [g[i, 0, rows] for i in range(3)]
        last = [g[i, 3, rows] for i in range(3)]
        x = jnp.where(l8 < 16, first[0], jnp.where(l8 < 32, roll_l(first[1], 16), roll_l(first[2], 32)))
        y = jnp.where(l8 >= 112, last[0], jnp.where(l8 >= 96, roll_l(last[1], -16), roll_l(last[2], -32)))
        pk[8 * k:8 * k + 8] = jnp.where(l8 < 64, x, y)

    own_rows = pl.ds(pl.multiple_of(PAD2 + lat * 16, 16), 16)

    pl.semaphore_wait(barrier, len(greeted))

    def send(src, dst, s_sem, r_sem, k, to):
        copy = pltpu.make_async_remote_copy(
            src_ref=src, dst_ref=dst, send_sem=s_sem.at[k], recv_sem=r_sem.at[k], device_id=to, device_id_type=MESH
        )
        copy.start()
        return copy

    halos = []
    for k, (dlon, dlat) in enumerate(HALO):
        first_row, count = {0: (0, ROWS), 1: (ROWS - H, H), -1: (0, H)}[dlat]
        to = {0: H, 1: 0, -1: H + ROWS}[dlat]
        if dlon == 0:
            first_row, to = (ROWS - 8, H - 8) if dlat == 1 else (0, H + ROWS)
            src = g.at[:, pl.ds(0, 4), pl.ds(top + first_row, 8)]
            dst = g.at[:, pl.ds(0, 4), pl.ds(PAD + to, 8)]
        else:
            src = pk.at[pl.ds(first_row, count)]
            dst = (rw_ if dlon == 1 else re_).at[pl.ds(to, count)]
        halos.append(send(src, dst, a_send, a_recv, k, device(dlon, dlat)))

    far_halos = [
        send(g.at[:, pl.ds(0, 4), pl.ds(top + first, 8)], far.at[i], a_send, a_recv, 8 + i, device(0, dlat))
        for i, (dlat, first) in enumerate(((1, ROWS - 16), (-1, 8)))
    ]

    def spread_lat(index, s_sem, r_sem):
        part = c.at[index, 2, own_rows]
        return [send(part, part, s_sem, r_sem, k, device(0, d)) for k, d in enumerate(SPREAD_LAT)]

    def spread_lon(index, s_sem, r_sem):
        rows = pl.ds(PAD2, 64)
        return [
            send(c.at[index, 2, rows], c.at[index, 2 - d, rows], s_sem, r_sem, 3 + k, device(d, 0))
            for k, d in enumerate(SPREAD_LON)
        ]

    for a in range(0, 16, 8):
        x = ld(g.at[1], top + 4 * a, 8, range(4), 4)
        for j in (1, 2, 3):
            x = x + ld(g.at[1], top + 4 * a + j, 8, range(4), 4)
        y = ld(g.at[2], top + 4 * a + 3, 8, range(4), 4)
        y = y + roll_l(y, -1)
        y = y + roll_l(y, -2)
        rows = pl.ds(pl.multiple_of(PAD2 + lat * 16 + a, 8), 8)
        c[1, 2, rows, :] = compact(x, 3)
        c[2, 2, rows, :] = compact(y, 0)

    conds = spread_lat(pl.ds(1, 2), cs_send, cs_recv)

    for copy in halos:
        copy.wait_recv()

    has_north = jnp.where(lat > 0, 1.0, 0.0).astype(F32)
    used = (l8 < 16) | (l8 >= 112)
    for k in range(N0 // 8):
        x = jnp.where(l8 < 64, re_[8 * k:8 * k + 8], rw_[8 * k:8 * k + 8])
        for i, other in ((0, 0.0), (1, 1.0), (2, 1.0)):
            y = x if i == 0 else jnp.where(l8 < 64, roll_l(x, -16 * i), roll_l(x, 16 * i))
            g[i, 4, PAD + 8 * k:PAD + 8 * k + 8, :] = jnp.where(used, y, other)
    g[2, :, PAD + 8:PAD + H] = g[2, :, PAD + 8:PAD + H] * has_north

    def bounds(halo, own):
        return jnp.where(lat > 0, 0, halo), jnp.where(lat < NLAT - 1, 2 * halo + own, halo + own)

    coeffs(l0, 16, bounds(H, ROWS), True, 8, 80)
    sweep(l0, l0.wf, l0.v, True, 8, 80, 16)
    for copy in conds:
        copy.wait_recv()
    conds_lon = spread_lon(pl.ds(1, 2), cs_send, cs_recv)
    coarsen(l0, l1)
    remainder(l0, 16, 8, 80)
    coeffs(l1, 16, bounds(H // 2, ROWS // 2))
    restrict(l0, l1)
    sweep(l1, l1.wf, l1.v, True, 0, 48, 16)
    remainder(l1, 16)
    for a in range(0, 16, 8):
        x = ld(l1.r, PAD + 8 + 2 * a, 8, range(4), 2) + ld(l1.r, PAD + 9 + 2 * a, 8, range(4), 2)
        rows = pl.ds(pl.multiple_of(PAD2 + lat * 16 + a, 8), 8)
        c[0, 2, rows, :] = compact(x + roll_l(x, -2), 0)
    fields = [
        send(c.at[0, 2, own_rows], c.at[0, 2 - d[0], own_rows], fs_send, fs_recv, k, device(*d))
        for k, d in enumerate(SPREAD)
    ]

    for i, first in enumerate((PAD, PAD + N0 - 8)):
        far_halos[i].wait_recv()
        for k in range(3):
            for j in range(4):
                g[k, j, first:first + 8] = far[i, k, j]
    g[2, :, PAD:PAD + 8] = g[2, :, PAD:PAD + 8] * has_north
    for r0 in (0, N0 - 16):
        coeffs(l0, 16, bounds(H, ROWS), True, r0, 16)
    for r0 in (0, N0 - 16):
        sweep(l0, l0.wf, l0.v, True, r0, 16, 16)
        coarsen(l0, l1, r0 // 2, 8)
    for r0 in (0, N0 - 16):
        remainder(l0, 16, r0, 16)
        coeffs(l1, 8, bounds(H // 2, ROWS // 2), False, r0 // 2, 8)
    for r0 in (0, N0 - 16):
        restrict(l0, l1, r0 // 2, 8)
    for r0 in (0, N0 // 2 - 8):
        sweep(l1, l1.wf, l1.v, True, r0, 8, 8)

    for copy in conds_lon:
        copy.wait_recv()
    coeffs(l2, 16)
    coarsen(l2, l3)
    coeffs(l3, 16)
    coarsen(l3, l4)
    coeffs(l4, 16)
    coarsen(l4, l5)
    coeffs(l5, 8)


    def twice(l, v, source, r0, count, ch, blocks=ALL):
        sweep(l, v, l.v2, source, r0, count, ch, blocks)
        sweep(l, l.v2, v, source, r0, count, ch, blocks)

    def rise_coarse(name, source):
        u = [getattr(l, name) for l in (l0, l1, l2, l3, l4, l5)]
        twice(l5, u[5], source, 0, 8, 8, MID)
        prolong(l5, l4, u[5], u[4], 0, 8, source, MID)
        twice(l4, u[4], source, 0, 16, 16, MID)
        prolong(l4, l3, u[4], u[3], 0, 16, source, MID)
        twice(l3, u[3], source, 0, 32, 16, MID)
        near = lat * 8 - 4
        prolong(l3, l2, u[3], u[2], near, 16, source, MID)
        near = pl.multiple_of(lat * 16 - 8, 8)
        twice(l2, u[2], source, near, 32, 16, MID)

    def rise_fine(name, source):
        u = [getattr(l, name) for l in (l0, l1, l2)]
        for i in range(3):
            e = expand(u[2], PAD2 + lat * 16 - 4 + 8 * i)
            spread_rows(u[1], PAD + 16 * i, e, source)
        twice(l1, u[1], source, 0, 48, 16)
        prolong(l1, l0, u[1], u[0], 0, 48, source)
        twice(l0, u[0], source, 8, 80, 16)

    def applied(v, out, sums, n):
        def body(r, carry):
            x, av = operator(l0, v, top + r, 16)
            x, av = x[:, :COLS], av[:, :COLS]
            out[pl.ds(r, 16)] = av
            more = sums(pl.ds(r, 16), ld(l0.f, top + r, 16, range(4)), x, av)
            return tuple(y + (z[:8] + z[8:]) for y, z in zip(carry, more))

        carry = (jnp.zeros((8, COLS), F32),) * n
        for r in range(0, ROWS, 16):
            carry = body(r, carry)
        return carry

    x = pair(l5.e, PAD, 8, 0) + pair(l5.e, PAD, 8, 1)
    e6 = roll_l(x, -8)
    x = pair(l5.so, PAD, 8, 1)
    s6 = x + roll_l(x, -8)
    row6, lane6 = rows_of((8, WIDE)), lanes((8, WIDE))
    west6 = roll_l(e6, 16)
    north6 = jnp.where(row6 == 0, 0.0, pltpu.roll(s6, 1, 0))
    w6 = jnp.where(row6 < 4, OMEGA / (((e6 + west6) + s6) + north6), 0.0)
    for i, x in enumerate((e6, west6, s6, north6, w6, w6 * e6, w6 * west6, w6 * s6, w6 * north6)):
        st(l6, 8 * i, x)

    st(l5.q, PAD, jnp.ones((8, WIDE), F32))
    rise_coarse("q", False)
    for copy in halos + far_halos + conds:
        copy.wait_send()
    rise_fine("q", False)
    for copy in fields + conds_lon:
        copy.wait_send()
    sums_q = applied(l0.q, ag, lambda rows, b, v, av: (b * v, v * av), 2)

    for copy in fields:
        copy.wait_recv()

    def first(r):
        st(l2.wf, PAD2 + r, ld(l2.w, PAD2 + r, 16) * ld(l2.f, PAD2 + r, 16))

    loop(0, 64, 16, first)
    sweep(l2, l2.wf, l2.v, True, 0, 64, 16)
    remainder(l2, 16)
    for l, coarse in ((l2, l3), (l3, l4), (l4, l5)):
        restrict(l, coarse)
        sweep(coarse, coarse.wf, coarse.v, True, 0, coarse.n, min(16, coarse.n))
        remainder(coarse, min(16, coarse.n))

    x = pair(l5.r, PAD, 8, 0) + pair(l5.r, PAD, 8, 1)
    f6 = x + roll_l(x, -8)
    e6, west6, s6, north6, w6, ae6, aw6, as6, an6 = [ld(l6, 8 * i, 8) for i in range(9)]
    wf6 = w6 * f6
    field = wf6
    for _ in range(COARSE_SWEEPS - 1):
        x = ae6 * roll_l(field, -16) + aw6 * roll_l(field, 16)
        y = as6 * pltpu.roll(field, 7, 0) + an6 * pltpu.roll(field, 1, 0)
        field = (((1.0 - OMEGA) * field + wf6) + y) + x
    lon6 = e6 * (field - roll_l(field, -16)) + west6 * (field - roll_l(field, 16))
    lat6 = s6 * (field - pltpu.roll(field, 7, 0)) + north6 * (field - pltpu.roll(field, 1, 0))
    left = f6 - (lon6 + lat6)
    mine = ((lane6 & 15) == 0) & (lane6 >= 256) & (lane6 < 384)
    left = jnp.where(mine & (row6 == lat), left, 0.0)[:, 256:384]
    last = jnp.where(mine & (row6 == 3) & (lat == 3), s6, 0.0)[:, 256:384]

    e = jnp.where((lane6 & 8) == 0, field, roll_l(field, 8))
    for odd in (0, 1):
        st(l5.r, odd, e, ALL, 2)
    st(l5.v, PAD, ld(l5.v, PAD, 8) + ld(l5.r, 0, 8))
    rise_coarse("v", True)
    rise_fine("v", True)
    sums_v = applied(l0.v, a0, lambda rows, b, v, av: (b * v, v * av, v * ag[rows]), 3)

    def wait_all(got, sem):
        pltpu.make_async_copy(got, got, sem.at[0]).wait()

    def fold(x):
        return (x[:, 0:128] + x[:, 128:256]) + (x[:, 256:384] + x[:, 384:512])

    seven = [left, last, fold(sums_v[0]), fold(sums_q[0]), fold(sums_v[1]), fold(sums_v[2]), fold(sums_q[1])]
    row = rows_of((8, 128))
    total = jnp.zeros((8, 128), F32)
    for i, x in enumerate(seven):
        total = jnp.where(row == i, jnp.sum(x, axis=0, keepdims=True), total)
    t1[...] = total
    for d in FAR1:
        send(t1, got1.at[d - 1], c1_send, c1_recv, 0, mate1(d))
    wait_all(got1, c1_recv)

    def gathered(total, got):
        parts = [total] + [got[d] for d in range(15)]
        while len(parts) > 1:
            parts = [x + y for x, y in zip(parts[::2], parts[1::2])]
        return parts[0]

    total = gathered(total, got1)
    t2[...] = total
    for d in FAR2:
        send(t2, got2.at[d - 1], c2_send, c2_recv, 0, mate2(d))
    wait_all(got1, c1_send)
    wait_all(got2, c2_recv)
    total = gathered(total, got2)
    for by in (64, 32, 16, 8, 4, 2, 1):
        total = total + pltpu.roll(total, by, 1)
    n_left, n_last, bv, bq, vav, vaq, qaq = [total[i:i + 1] for i in range(7)]
    const = n_left / n_last
    step = (bv + const * bq) / ((vav + (2.0 * const) * vaq) + (const * const) * qaq)
    both = jnp.concatenate([step * const] * 4, axis=1)
    step = jnp.concatenate([step] * 4, axis=1)

    for r in range(0, ROWS, 16):
        rows = pl.ds(r, 16)
        sol[rows] = step * ld(l0.v, top + r, 16, range(4)) + both * ld(l0.q, top + r, 16, range(4))
        res[rows] = ld(l0.f, top + r, 16, range(4)) - (step * a0[rows] + both * ag[rows])
    wait_all(got2, c2_send)


def body(guidance, cond_lon, cond_lat):
    def vm(*shape):
        return pltpu.VMEM(shape, F32)

    def wide(n, count):
        return [vm(5, n, 128)] * count

    dma = pltpu.SemaphoreType.DMA
    scratch = [vm(3, 5, N0 + 2 * PAD, 128), vm(ROWS, 128), vm(N0, 128), vm(N0, 128), vm(ROWS, COLS), vm(ROWS, COLS)]
    scratch += [vm(3, 5, 64 + 2 * PAD2, 128), vm(8, 128), vm(15, 8, 128), vm(8, 128), vm(15, 8, 128), vm(5, 72, 128), vm(2, 3, 4, 8, 128)]
    scratch += wide(N0 + 2 * PAD, 9) + wide(N0 // 2 + 2 * PAD, 13) + wide(64 + 2 * PAD2, 10)
    scratch += wide(32 + 2 * PAD, 13) + wide(16 + 2 * PAD, 13) + wide(8 + 2 * PAD, 14)
    scratch += [dma((3, 4)), dma((10,)), dma((10,)), dma((7,)), dma((7,)), dma((19,)), dma((19,))] + [dma((1,))] * 4
    return pl.pallas_call(
        kernel,
        out_shape=(pltpu.VMEM((ROWS, COLS), F32),) * 2,
        in_specs=[pl.BlockSpec(memory_space=pltpu.HBM)] * 3,
        out_specs=(pl.BlockSpec(memory_space=pltpu.VMEM),) * 2,
        scratch_shapes=scratch,
        compiler_params=pltpu.CompilerParams(
            collective_id=0, has_side_effects=True, vmem_limit_bytes=60 * 1024 * 1024
        ),
        cost_estimate=pl.CostEstimate(flops=10_000_000, bytes_accessed=655360, transcendentals=0),
    )(guidance, cond_lon, cond_lat)


def solution(mesh):
    spec = P("lat", "lon")
    return jax.shard_map(body, mesh=mesh, in_specs=(spec,) * 3, out_specs=(spec,) * 2, check_vma=False)
```

```python
import jax
import jax.numpy as jnp
from jax import lax
from jax.experimental import pallas as pl
from jax.experimental.pallas import tpu as pltpu
from jax.sharding import PartitionSpec as P

OMEGA = 0.8
COARSE_SWEEPS = 8
NLAT, NLON, BLOCK = 4, 64, 16
ROWS, COLS = 64, 512
H = 16
PAD = 8
PAD2 = 16
N0 = ROWS + 2 * H
WIDE = COLS + 128
ALL = range(5)
MID = range(1, 4)
MESH = pl.DeviceIdType.MESH
F32 = jnp.float32

HALO = ((1, 1), (1, -1), (-1, 1), (-1, -1), (1, 0), (-1, 0), (0, 1), (0, -1))
SPREAD_LAT = (1, 2, 3)
SPREAD_LON = (2, -2, 1, -1)
SPREAD = ((2, 2), (-2, 2), (1, 2), (-1, 2), (2, 1), (2, -1), (-2, 1), (-2, -1), (0, 2), (2, 0), (-2, 0))
SPREAD += ((1, 1), (1, -1), (-1, 1), (-1, -1), (0, 1), (0, -1), (1, 0), (-1, 0))
FAR1 = (8, 7, 9, 6, 10, 5, 11, 4, 12, 3, 13, 2, 14, 1, 15)
FAR2 = (10, 9, 11, 6, 14, 2, 8, 5, 7, 13, 15, 1, 3, 4, 12)


def lanes(shape):
    return lax.broadcasted_iota(jnp.int32, shape, len(shape) - 1)


def rows_of(shape):
    return lax.broadcasted_iota(jnp.int32, shape, 0)


def roll_l(x, by):
    return pltpu.roll(x, by % x.shape[1], 1)


def ld(ref, start, n, blocks=ALL, stride=None):
    rows = pl.ds(start, n) if stride is None else pl.ds(start, n, stride=stride)
    return jnp.concatenate([ref[j, rows, :] for j in blocks], axis=1)


def st(ref, start, x, blocks=ALL, stride=None):
    n = x.shape[0]
    rows = pl.ds(start, n) if stride is None else pl.ds(start, n, stride=stride)
    for i, j in enumerate(blocks):
        ref[j, rows, :] = x[:, 128 * i:128 * (i + 1)]


def loop(r0, count, ch, body):
    for k in range(count // ch):
        body(r0 + k * ch)


class Level:
    def __init__(self, s, pad, n, f, e, so, west, ae, aw, as_, an, w, wf, v, v2, q, r=None):
        self.s, self.pad, self.n = s, pad, n
        self.f, self.e, self.so, self.west = f, e, so, west
        self.ae, self.aw, self.as_, self.an, self.w, self.wf = ae, aw, as_, an, w, wf
        self.v, self.v2, self.q, self.r = v, v2, q, v2 if r is None else r


def coeffs(l, ch, keep=None, source=False, r0=0, count=None):
    def body(r):
        p = l.pad + r
        e, so, no = ld(l.e, p, ch), ld(l.so, p, ch), ld(l.so, p - 1, ch)
        we = roll_l(e, l.s)
        wk = OMEGA / (((e + we) + so) + no)
        if keep is not None:
            row = rows_of(wk.shape) + r
            wk = jnp.where((row >= keep[0]) & (row < keep[1]), wk, 0.0)
        st(l.west, p, we)
        st(l.ae, p, wk * e)
        st(l.aw, p, wk * we)
        st(l.as_, p, wk * so)
        st(l.an, p, wk * no)
        if source:
            st(l.wf, p, wk * ld(l.f, p, ch))
        else:
            st(l.w, p, wk)

    loop(r0, l.n if count is None else count, ch, body)


def sweep(l, src, dst, source, r0, count, ch, blocks=ALL):
    def body(r):
        p = l.pad + r
        v = ld(src, p, ch, blocks)
        x = ld(l.ae, p, ch, blocks) * roll_l(v, -l.s) + ld(l.aw, p, ch, blocks) * roll_l(v, l.s)
        y = ld(l.as_, p, ch, blocks) * ld(src, p + 1, ch, blocks) + ld(l.an, p, ch, blocks) * ld(src, p - 1, ch, blocks)
        z = (1.0 - OMEGA) * v
        if source:
            z = z + ld(l.wf, p, ch, blocks)
        st(dst, p, (y + z) + x, blocks)

    loop(r0, count, ch, body)


def operator(l, v, p, ch):
    x = ld(v, p, ch)
    lon = ld(l.e, p, ch) * (x - roll_l(x, -l.s)) + ld(l.west, p, ch) * (x - roll_l(x, l.s))
    lat = ld(l.so, p, ch) * (x - ld(v, p + 1, ch)) + ld(l.so, p - 1, ch) * (x - ld(v, p - 1, ch))
    return x, lat + lon


def remainder(l, ch, r0=0, count=None):
    def body(r):
        p = l.pad + r
        st(l.r, p, ld(l.f, p, ch) - operator(l, l.v, p, ch)[1])

    loop(r0, l.n if count is None else count, ch, body)


def pair(ref, start, n, odd, blocks=ALL):
    return ld(ref, start + odd, n, blocks, 2)


def restrict(l, c, a0=0, count=None):
    count = c.n if count is None else count
    ch = min(16, count)

    def body(a):
        x = pair(l.r, l.pad + 2 * a, ch, 0) + pair(l.r, l.pad + 2 * a, ch, 1)
        x = x + roll_l(x, -l.s)
        st(c.f, c.pad + a, x)
        st(c.wf, c.pad + a, x * ld(c.w, c.pad + a, ch))

    for a in range(a0, a0 + count, ch):
        body(a)


def coarsen(l, c, a0=0, count=None):
    count = c.n if count is None else count
    ch = min(16, count)
    for a in range(a0, a0 + count, ch):
        x = pair(l.e, l.pad + 2 * a, ch, 0) + pair(l.e, l.pad + 2 * a, ch, 1)
        st(c.e, c.pad + a, roll_l(x, -l.s))
        y = pair(l.so, l.pad + 2 * a, ch, 1)
        st(c.so, c.pad + a, y + roll_l(y, -l.s))


def spread_rows(v, start, e, add, blocks=ALL):
    for odd in (0, 1):
        x = e
        if add:
            x = x + ld(v, start + odd, e.shape[0], blocks, 2)
        st(v, start + odd, x, blocks, 2)


def prolong(c, l, src, dst, a0, n, add, blocks=ALL):
    for a in range(0, n, 8):
        e = ld(src, c.pad + a0 + a, 8, blocks)
        e = jnp.where((lanes(e.shape) & l.s) == 0, e, roll_l(e, l.s))
        spread_rows(dst, l.pad + 2 * (a0 + a), e, add, blocks)


def pick(x, index):
    return jnp.take_along_axis(x, index, axis=1, mode="promise_in_bounds")


def compact(x, offset):
    l = lanes((8, 128))
    index = (l % 32) * 4 + offset
    out = pick(x[:, 384:512], index)
    for j in (2, 1, 0):
        out = jnp.where(l < 32 * (j + 1), pick(x[:, 128 * j:128 * (j + 1)], index), out)
    return out


def expand(x, base):
    l = lanes((8, 128))
    q = l // 4
    own = x[2, pl.ds(base, 8), :]
    parts = [pick(own, q + 32 * j) for j in range(4)]
    east = pick(x[3, pl.ds(base, 8), :], q)
    west = pick(x[1, pl.ds(base, 8), :], q + 96)
    return jnp.concatenate(parts + [jnp.where(l < 64, east, west)], axis=1)


def kernel(
    b_in, e_in, s_in, sol, res,
    g, pk, re_, rw_, a0, ag, c, t1, got1, t2, got2, l6, far,
    *rest,
):
    fine0, fine1, fine2, fine3, fine4, fine5 = rest[:9], rest[9:22], rest[22:32], rest[32:45], rest[45:58], rest[58:72]
    in_sem, a_send, a_recv, cs_send, cs_recv, fs_send, fs_recv, c1_send, c1_recv, c2_send, c2_recv = rest[72:]

    l0 = Level(1, PAD, N0, g.at[0], g.at[1], g.at[2], *fine0[:5], None, *fine0[5:])
    l1 = Level(2, PAD, N0 // 2, *fine1)
    l2 = Level(1, PAD2, 64, c.at[0], c.at[1], c.at[2], *fine2)
    l3 = Level(2, PAD, 32, *fine3)
    l4 = Level(4, PAD, 16, *fine4)
    l5 = Level(8, PAD, 8, *fine5)
    lat, lon = lax.axis_index("lat"), lax.axis_index("lon")

    def device(dlon, dlat):
        return {"lon": lax.rem(lon + dlon + NLON, NLON), "lat": lax.rem(lat + dlat + NLAT, NLAT)}

    block = (lon // BLOCK) * BLOCK
    inner = lax.rem(lon, BLOCK)

    def mate1(d):
        return {"lon": block + lax.rem(inner + d, BLOCK), "lat": lat}

    def mate2(d):
        return device(BLOCK * (d // 4), d % 4)

    top = PAD + H
    loads = [
        pltpu.make_async_copy(x.at[:, pl.ds(128 * j, 128)], g.at[i, j, pl.ds(top, ROWS)], in_sem.at[i, j])
        for i, x in enumerate((b_in, e_in, s_in))
        for j in range(4)
    ]
    barrier = pltpu.get_barrier_semaphore()
    greeted = [device(*d) for d in HALO + SPREAD[:11]]
    greeted += [mate1(d) for d in range(1, BLOCK)] + [mate2(d) for d in range(4, 16)]
    for k, other in enumerate(greeted):
        pl.semaphore_signal(barrier, inc=1, device_id=other, device_id_type=MESH)
        if k == len(HALO) - 1:
            for copy in loads:
                copy.start()

    def clear(ref, l):
        zero = jnp.zeros((l.pad, WIDE), F32)
        st(ref, 0, zero)
        st(ref, l.pad + l.n, zero)

    for l in (l0, l1):
        for ref in (l.wf, l.v, l.v2, l.q):
            clear(ref, l)
    for l in (l2, l3, l4, l5):
        for ref in (l.wf, l.v, l.v2, l.q, l.so):
            clear(ref, l)
    for ref in (l2.ae, l2.aw, l2.as_, l2.an):
        clear(ref, l2)
    for ref in (l5.e, l5.r):
        clear(ref, l5)

    for copy in loads:
        copy.wait()

    l8 = lanes((8, 128))
    for k in range(ROWS // 8):
        rows = slice(top + 8 * k, top + 8 * k + 8)
        first = [g[i, 0, rows] for i in range(3)]
        last = [g[i, 3, rows] for i in range(3)]
        x = jnp.where(l8 < 16, first[0], jnp.where(l8 < 32, roll_l(first[1], 16), roll_l(first[2], 32)))
        y = jnp.where(l8 >= 112, last[0], jnp.where(l8 >= 96, roll_l(last[1], -16), roll_l(last[2], -32)))
        pk[8 * k:8 * k + 8] = jnp.where(l8 < 64, x, y)

    own_rows = pl.ds(pl.multiple_of(PAD2 + lat * 16, 16), 16)

    for a in range(0, 16, 8):
        x = ld(g.at[1], top + 4 * a, 8, range(4), 4)
        for j in (1, 2, 3):
            x = x + ld(g.at[1], top + 4 * a + j, 8, range(4), 4)
        y = ld(g.at[2], top + 4 * a + 3, 8, range(4), 4)
        y = y + roll_l(y, -1)
        y = y + roll_l(y, -2)
        rows = pl.ds(pl.multiple_of(PAD2 + lat * 16 + a, 8), 8)
        c[1, 2, rows, :] = compact(x, 3)
        c[2, 2, rows, :] = compact(y, 0)

    pl.semaphore_wait(barrier, len(greeted))

    def send(src, dst, s_sem, r_sem, k, to):
        copy = pltpu.make_async_remote_copy(
            src_ref=src, dst_ref=dst, send_sem=s_sem.at[k], recv_sem=r_sem.at[k], device_id=to, device_id_type=MESH
        )
        copy.start()
        return copy

    def spread_lat(index, s_sem, r_sem):
        part = c.at[index, 2, own_rows]
        return [send(part, part, s_sem, r_sem, k, device(0, d)) for k, d in enumerate(SPREAD_LAT)]

    def spread_lon(index, s_sem, r_sem):
        rows = pl.ds(PAD2, 64)
        return [
            send(c.at[index, 2, rows], c.at[index, 2 - d, rows], s_sem, r_sem, 3 + k, device(d, 0))
            for k, d in enumerate(SPREAD_LON)
        ]

    conds = spread_lat(pl.ds(1, 2), cs_send, cs_recv)
    halos = []
    for k, (dlon, dlat) in enumerate(HALO):
        first_row, count = {0: (0, ROWS), 1: (ROWS - H, H), -1: (0, H)}[dlat]
        to = {0: H, 1: 0, -1: H + ROWS}[dlat]
        if dlon == 0:
            first_row, to = (ROWS - 8, H - 8) if dlat == 1 else (0, H + ROWS)
            src = g.at[:, pl.ds(0, 4), pl.ds(top + first_row, 8)]
            dst = g.at[:, pl.ds(0, 4), pl.ds(PAD + to, 8)]
        else:
            src = pk.at[pl.ds(first_row, count)]
            dst = (rw_ if dlon == 1 else re_).at[pl.ds(to, count)]
        halos.append(send(src, dst, a_send, a_recv, k, device(dlon, dlat)))

    far_halos = [
        send(g.at[:, pl.ds(0, 4), pl.ds(top + first, 8)], far.at[i], a_send, a_recv, 8 + i, device(0, dlat))
        for i, (dlat, first) in enumerate(((1, ROWS - 16), (-1, 8)))
    ]


    for copy in conds:
        copy.wait_recv()
    conds_lon = spread_lon(pl.ds(1, 2), cs_send, cs_recv)

    for copy in halos:
        copy.wait_recv()

    has_north = jnp.where(lat > 0, 1.0, 0.0).astype(F32)
    used = (l8 < 16) | (l8 >= 112)
    for k in range(N0 // 8):
        x = jnp.where(l8 < 64, re_[8 * k:8 * k + 8], rw_[8 * k:8 * k + 8])
        for i, other in ((0, 0.0), (1, 1.0), (2, 1.0)):
            y = x if i == 0 else jnp.where(l8 < 64, roll_l(x, -16 * i), roll_l(x, 16 * i))
            g[i, 4, PAD + 8 * k:PAD + 8 * k + 8, :] = jnp.where(used, y, other)
    g[2, :, PAD + 8:PAD + H] = g[2, :, PAD + 8:PAD + H] * has_north

    def bounds(halo, own):
        return jnp.where(lat > 0, 0, halo), jnp.where(lat < NLAT - 1, 2 * halo + own, halo + own)

    coeffs(l0, 16, bounds(H, ROWS), True, 8, 80)
    sweep(l0, l0.wf, l0.v, True, 8, 80, 16)
    coarsen(l0, l1)
    remainder(l0, 16, 8, 80)
    coeffs(l1, 16, bounds(H // 2, ROWS // 2))
    restrict(l0, l1)
    sweep(l1, l1.wf, l1.v, True, 0, 48, 16)
    remainder(l1, 16)
    for a in range(0, 16, 8):
        x = ld(l1.r, PAD + 8 + 2 * a, 8, range(4), 2) + ld(l1.r, PAD + 9 + 2 * a, 8, range(4), 2)
        rows = pl.ds(pl.multiple_of(PAD2 + lat * 16 + a, 8), 8)
        c[0, 2, rows, :] = compact(x + roll_l(x, -2), 0)
    fields = [
        send(c.at[0, 2, own_rows], c.at[0, 2 - d[0], own_rows], fs_send, fs_recv, k, device(*d))
        for k, d in enumerate(SPREAD)
    ]

    for i, first in enumerate((PAD, PAD + N0 - 8)):
        far_halos[i].wait_recv()
        for k in range(3):
            for j in range(4):
                g[k, j, first:first + 8] = far[i, k, j]
    g[2, :, PAD:PAD + 8] = g[2, :, PAD:PAD + 8] * has_north
    for r0 in (0, N0 - 16):
        coeffs(l0, 16, bounds(H, ROWS), True, r0, 16)
    for r0 in (0, N0 - 16):
        sweep(l0, l0.wf, l0.v, True, r0, 16, 16)
        coarsen(l0, l1, r0 // 2, 8)
    for r0 in (0, N0 - 16):
        remainder(l0, 16, r0, 16)
        coeffs(l1, 8, bounds(H // 2, ROWS // 2), False, r0 // 2, 8)
    for r0 in (0, N0 - 16):
        restrict(l0, l1, r0 // 2, 8)
    for r0 in (0, N0 // 2 - 8):
        sweep(l1, l1.wf, l1.v, True, r0, 8, 8)

    for copy in conds_lon:
        copy.wait_recv()
    coeffs(l2, 16)
    coarsen(l2, l3)
    coeffs(l3, 16)
    coarsen(l3, l4)
    coeffs(l4, 16)
    coarsen(l4, l5)
    coeffs(l5, 8)


    def twice(l, v, source, r0, count, ch, blocks=ALL):
        sweep(l, v, l.v2, source, r0, count, ch, blocks)
        sweep(l, l.v2, v, source, r0, count, ch, blocks)

    def rise_coarse(name, source):
        u = [getattr(l, name) for l in (l0, l1, l2, l3, l4, l5)]
        twice(l5, u[5], source, 0, 8, 8, MID)
        prolong(l5, l4, u[5], u[4], 0, 8, source, MID)
        twice(l4, u[4], source, 0, 16, 16, MID)
        prolong(l4, l3, u[4], u[3], 0, 16, source, MID)
        twice(l3, u[3], source, 0, 32, 16, MID)
        near = lat * 8 - 4
        prolong(l3, l2, u[3], u[2], near, 16, source, MID)
        near = pl.multiple_of(lat * 16 - 8, 8)
        twice(l2, u[2], source, near, 32, 16, MID)

    def rise_fine(name, source):
        u = [getattr(l, name) for l in (l0, l1, l2)]
        for i in range(3):
            e = expand(u[2], PAD2 + lat * 16 - 4 + 8 * i)
            spread_rows(u[1], PAD + 16 * i, e, source)
        twice(l1, u[1], source, 0, 48, 16)
        prolong(l1, l0, u[1], u[0], 0, 48, source)
        twice(l0, u[0], source, 8, 80, 16)

    def applied(v, out, sums, n):
        def body(r, carry):
            x, av = operator(l0, v, top + r, 16)
            x, av = x[:, :COLS], av[:, :COLS]
            out[pl.ds(r, 16)] = av
            more = sums(pl.ds(r, 16), ld(l0.f, top + r, 16, range(4)), x, av)
            return tuple(y + (z[:8] + z[8:]) for y, z in zip(carry, more))

        carry = (jnp.zeros((8, COLS), F32),) * n
        for r in range(0, ROWS, 16):
            carry = body(r, carry)
        return carry

    x = pair(l5.e, PAD, 8, 0) + pair(l5.e, PAD, 8, 1)
    e6 = roll_l(x, -8)
    x = pair(l5.so, PAD, 8, 1)
    s6 = x + roll_l(x, -8)
    row6, lane6 = rows_of((8, WIDE)), lanes((8, WIDE))
    west6 = roll_l(e6, 16)
    north6 = jnp.where(row6 == 0, 0.0, pltpu.roll(s6, 1, 0))
    w6 = jnp.where(row6 < 4, OMEGA / (((e6 + west6) + s6) + north6), 0.0)
    for i, x in enumerate((e6, west6, s6, north6, w6, w6 * e6, w6 * west6, w6 * s6, w6 * north6)):
        st(l6, 8 * i, x)

    st(l5.q, PAD, jnp.ones((8, WIDE), F32))
    rise_coarse("q", False)
    for copy in halos + far_halos + conds:
        copy.wait_send()
    rise_fine("q", False)
    for copy in fields + conds_lon:
        copy.wait_send()
    sums_q = applied(l0.q, ag, lambda rows, b, v, av: (b * v, v * av), 2)

    for copy in fields:
        copy.wait_recv()

    def first(r):
        st(l2.wf, PAD2 + r, ld(l2.w, PAD2 + r, 16) * ld(l2.f, PAD2 + r, 16))

    loop(0, 64, 16, first)
    sweep(l2, l2.wf, l2.v, True, 0, 64, 16)
    remainder(l2, 16)
    for l, coarse in ((l2, l3), (l3, l4), (l4, l5)):
        restrict(l, coarse)
        sweep(coarse, coarse.wf, coarse.v, True, 0, coarse.n, min(16, coarse.n))
        remainder(coarse, min(16, coarse.n))

    x = pair(l5.r, PAD, 8, 0) + pair(l5.r, PAD, 8, 1)
    f6 = x + roll_l(x, -8)
    e6, west6, s6, north6, w6, ae6, aw6, as6, an6 = [ld(l6, 8 * i, 8) for i in range(9)]
    wf6 = w6 * f6
    field = wf6
    for _ in range(COARSE_SWEEPS - 1):
        x = ae6 * roll_l(field, -16) + aw6 * roll_l(field, 16)
        y = as6 * pltpu.roll(field, 7, 0) + an6 * pltpu.roll(field, 1, 0)
        field = (((1.0 - OMEGA) * field + wf6) + y) + x
    lon6 = e6 * (field - roll_l(field, -16)) + west6 * (field - roll_l(field, 16))
    lat6 = s6 * (field - pltpu.roll(field, 7, 0)) + north6 * (field - pltpu.roll(field, 1, 0))
    left = f6 - (lon6 + lat6)
    mine = ((lane6 & 15) == 0) & (lane6 >= 256) & (lane6 < 384)
    left = jnp.where(mine & (row6 == lat), left, 0.0)[:, 256:384]
    last = jnp.where(mine & (row6 == 3) & (lat == 3), s6, 0.0)[:, 256:384]

    e = jnp.where((lane6 & 8) == 0, field, roll_l(field, 8))
    for odd in (0, 1):
        st(l5.r, odd, e, ALL, 2)
    st(l5.v, PAD, ld(l5.v, PAD, 8) + ld(l5.r, 0, 8))
    rise_coarse("v", True)
    rise_fine("v", True)
    sums_v = applied(l0.v, a0, lambda rows, b, v, av: (b * v, v * av, v * ag[rows]), 3)

    def wait_all(got, sem):
        pltpu.make_async_copy(got, got, sem.at[0]).wait()

    def fold(x):
        return (x[:, 0:128] + x[:, 128:256]) + (x[:, 256:384] + x[:, 384:512])

    seven = [left, last, fold(sums_v[0]), fold(sums_q[0]), fold(sums_v[1]), fold(sums_v[2]), fold(sums_q[1])]
    row = rows_of((8, 128))
    total = jnp.zeros((8, 128), F32)
    for i, x in enumerate(seven):
        total = jnp.where(row == i, jnp.sum(x, axis=0, keepdims=True), total)
    t1[...] = total
    for d in FAR1:
        send(t1, got1.at[d - 1], c1_send, c1_recv, 0, mate1(d))
    wait_all(got1, c1_recv)

    def gathered(total, got):
        parts = [total] + [got[d] for d in range(15)]
        while len(parts) > 1:
            parts = [x + y for x, y in zip(parts[::2], parts[1::2])]
        return parts[0]

    total = gathered(total, got1)
    t2[...] = total
    for d in FAR2:
        send(t2, got2.at[d - 1], c2_send, c2_recv, 0, mate2(d))
    wait_all(got1, c1_send)
    wait_all(got2, c2_recv)
    total = gathered(total, got2)
    for by in (64, 32, 16, 8, 4, 2, 1):
        total = total + pltpu.roll(total, by, 1)
    n_left, n_last, bv, bq, vav, vaq, qaq = [total[i:i + 1] for i in range(7)]
    const = n_left / n_last
    step = (bv + const * bq) / ((vav + (2.0 * const) * vaq) + (const * const) * qaq)
    both = jnp.concatenate([step * const] * 4, axis=1)
    step = jnp.concatenate([step] * 4, axis=1)

    for r in range(0, ROWS, 16):
        rows = pl.ds(r, 16)
        sol[rows] = step * ld(l0.v, top + r, 16, range(4)) + both * ld(l0.q, top + r, 16, range(4))
        res[rows] = ld(l0.f, top + r, 16, range(4)) - (step * a0[rows] + both * ag[rows])
    wait_all(got2, c2_send)


def body(guidance, cond_lon, cond_lat):
    def vm(*shape):
        return pltpu.VMEM(shape, F32)

    def wide(n, count):
        return [vm(5, n, 128)] * count

    dma = pltpu.SemaphoreType.DMA
    scratch = [vm(3, 5, N0 + 2 * PAD, 128), vm(ROWS, 128), vm(N0, 128), vm(N0, 128), vm(ROWS, COLS), vm(ROWS, COLS)]
    scratch += [vm(3, 5, 64 + 2 * PAD2, 128), vm(8, 128), vm(15, 8, 128), vm(8, 128), vm(15, 8, 128), vm(5, 72, 128), vm(2, 3, 4, 8, 128)]
    scratch += wide(N0 + 2 * PAD, 9) + wide(N0 // 2 + 2 * PAD, 13) + wide(64 + 2 * PAD2, 10)
    scratch += wide(32 + 2 * PAD, 13) + wide(16 + 2 * PAD, 13) + wide(8 + 2 * PAD, 14)
    scratch += [dma((3, 4)), dma((10,)), dma((10,)), dma((7,)), dma((7,)), dma((19,)), dma((19,))] + [dma((1,))] * 4
    return pl.pallas_call(
        kernel,
        out_shape=(pltpu.VMEM((ROWS, COLS), F32),) * 2,
        in_specs=[pl.BlockSpec(memory_space=pltpu.HBM)] * 3,
        out_specs=(pl.BlockSpec(memory_space=pltpu.VMEM),) * 2,
        scratch_shapes=scratch,
        compiler_params=pltpu.CompilerParams(
            collective_id=0, has_side_effects=True, vmem_limit_bytes=60 * 1024 * 1024
        ),
        cost_estimate=pl.CostEstimate(flops=10_000_000, bytes_accessed=655360, transcendentals=0),
    )(guidance, cond_lon, cond_lat)


def solution(mesh):
    spec = P("lat", "lon")
    return jax.shard_map(body, mesh=mesh, in_specs=(spec,) * 3, out_specs=(spec,) * 2, check_vma=False)
```

```python
import jax
import jax.numpy as jnp
from jax import lax
from jax.experimental import pallas as pl
from jax.experimental.pallas import tpu as pltpu
from jax.sharding import PartitionSpec as P

OMEGA = 0.8
COARSE_SWEEPS = 8
NLAT, NLON, BLOCK = 4, 64, 16
ROWS, COLS = 64, 512
H = 16
PAD = 8
PAD2 = 16
N0 = ROWS + 2 * H
WIDE = COLS + 128
ALL = range(5)
MID = range(1, 4)
MESH = pl.DeviceIdType.MESH
F32 = jnp.float32

HALO = ((1, 1), (1, -1), (-1, 1), (-1, -1), (1, 0), (-1, 0), (0, 1), (0, -1))
SPREAD_LAT = (1, 2, 3)
SPREAD_LON = (2, -2, 1, -1)
SPREAD = ((2, 2), (-2, 2), (1, 2), (-1, 2), (2, 1), (2, -1), (-2, 1), (-2, -1), (0, 2), (2, 0), (-2, 0))
SPREAD += ((1, 1), (1, -1), (-1, 1), (-1, -1), (0, 1), (0, -1), (1, 0), (-1, 0))
FAR1 = (8, 7, 9, 6, 10, 5, 11, 4, 12, 3, 13, 2, 14, 1, 15)
FAR2 = (10, 9, 11, 6, 14, 2, 8, 5, 7, 13, 15, 1, 3, 4, 12)


def lanes(shape):
    return lax.broadcasted_iota(jnp.int32, shape, len(shape) - 1)


def rows_of(shape):
    return lax.broadcasted_iota(jnp.int32, shape, 0)


def roll_l(x, by):
    return pltpu.roll(x, by % x.shape[1], 1)


def ld(ref, start, n, blocks=ALL, stride=None):
    rows = pl.ds(start, n) if stride is None else pl.ds(start, n, stride=stride)
    return jnp.concatenate([ref[j, rows, :] for j in blocks], axis=1)


def st(ref, start, x, blocks=ALL, stride=None):
    n = x.shape[0]
    rows = pl.ds(start, n) if stride is None else pl.ds(start, n, stride=stride)
    for i, j in enumerate(blocks):
        ref[j, rows, :] = x[:, 128 * i:128 * (i + 1)]


def loop(r0, count, ch, body):
    for k in range(count // ch):
        body(r0 + k * ch)


class Level:
    def __init__(self, s, pad, n, f, e, so, west, ae, aw, as_, an, w, wf, v, v2, q, r=None):
        self.s, self.pad, self.n = s, pad, n
        self.f, self.e, self.so, self.west = f, e, so, west
        self.ae, self.aw, self.as_, self.an, self.w, self.wf = ae, aw, as_, an, w, wf
        self.v, self.v2, self.q, self.r = v, v2, q, v2 if r is None else r


def coeffs(l, ch, keep=None, source=False, r0=0, count=None):
    def body(r):
        p = l.pad + r
        e, so, no = ld(l.e, p, ch), ld(l.so, p, ch), ld(l.so, p - 1, ch)
        we = roll_l(e, l.s)
        wk = OMEGA / (((e + we) + so) + no)
        if keep is not None:
            row = rows_of(wk.shape) + r
            wk = jnp.where((row >= keep[0]) & (row < keep[1]), wk, 0.0)
        st(l.west, p, we)
        st(l.ae, p, wk * e)
        st(l.aw, p, wk * we)
        st(l.as_, p, wk * so)
        st(l.an, p, wk * no)
        if source:
            st(l.wf, p, wk * ld(l.f, p, ch))
        else:
            st(l.w, p, wk)

    loop(r0, l.n if count is None else count, ch, body)


def sweep(l, src, dst, source, r0, count, ch, blocks=ALL):
    def body(r):
        p = l.pad + r
        v = ld(src, p, ch, blocks)
        x = ld(l.ae, p, ch, blocks) * roll_l(v, -l.s) + ld(l.aw, p, ch, blocks) * roll_l(v, l.s)
        y = ld(l.as_, p, ch, blocks) * ld(src, p + 1, ch, blocks) + ld(l.an, p, ch, blocks) * ld(src, p - 1, ch, blocks)
        z = (1.0 - OMEGA) * v
        if source:
            z = z + ld(l.wf, p, ch, blocks)
        st(dst, p, (y + z) + x, blocks)

    loop(r0, count, ch, body)


def operator(l, v, p, ch):
    x = ld(v, p, ch)
    lon = ld(l.e, p, ch) * (x - roll_l(x, -l.s)) + ld(l.west, p, ch) * (x - roll_l(x, l.s))
    lat = ld(l.so, p, ch) * (x - ld(v, p + 1, ch)) + ld(l.so, p - 1, ch) * (x - ld(v, p - 1, ch))
    return x, lat + lon


def remainder(l, ch, r0=0, count=None):
    def body(r):
        p = l.pad + r
        st(l.r, p, ld(l.f, p, ch) - operator(l, l.v, p, ch)[1])

    loop(r0, l.n if count is None else count, ch, body)


def pair(ref, start, n, odd, blocks=ALL):
    return ld(ref, start + odd, n, blocks, 2)


def restrict(l, c, a0=0, count=None):
    count = c.n if count is None else count
    ch = min(16, count)

    def body(a):
        x = pair(l.r, l.pad + 2 * a, ch, 0) + pair(l.r, l.pad + 2 * a, ch, 1)
        x = x + roll_l(x, -l.s)
        st(c.f, c.pad + a, x)
        st(c.wf, c.pad + a, x * ld(c.w, c.pad + a, ch))

    for a in range(a0, a0 + count, ch):
        body(a)


def coarsen(l, c, a0=0, count=None):
    count = c.n if count is None else count
    ch = min(16, count)
    for a in range(a0, a0 + count, ch):
        x = pair(l.e, l.pad + 2 * a, ch, 0) + pair(l.e, l.pad + 2 * a, ch, 1)
        st(c.e, c.pad + a, roll_l(x, -l.s))
        y = pair(l.so, l.pad + 2 * a, ch, 1)
        st(c.so, c.pad + a, y + roll_l(y, -l.s))


def spread_rows(v, start, e, add, blocks=ALL):
    for odd in (0, 1):
        x = e
        if add:
            x = x + ld(v, start + odd, e.shape[0], blocks, 2)
        st(v, start + odd, x, blocks, 2)


def prolong(c, l, src, dst, a0, n, add, blocks=ALL):
    for a in range(0, n, 8):
        e = ld(src, c.pad + a0 + a, 8, blocks)
        e = jnp.where((lanes(e.shape) & l.s) == 0, e, roll_l(e, l.s))
        spread_rows(dst, l.pad + 2 * (a0 + a), e, add, blocks)


def pick(x, index):
    return jnp.take_along_axis(x, index, axis=1, mode="promise_in_bounds")


def compact(x, offset):
    l = lanes((8, 128))
    index = (l % 32) * 4 + offset
    out = pick(x[:, 384:512], index)
    for j in (2, 1, 0):
        out = jnp.where(l < 32 * (j + 1), pick(x[:, 128 * j:128 * (j + 1)], index), out)
    return out


def expand(x, base):
    l = lanes((8, 128))
    q = l // 4
    own = x[2, pl.ds(base, 8), :]
    parts = [pick(own, q + 32 * j) for j in range(4)]
    east = pick(x[3, pl.ds(base, 8), :], q)
    west = pick(x[1, pl.ds(base, 8), :], q + 96)
    return jnp.concatenate(parts + [jnp.where(l < 64, east, west)], axis=1)


def kernel(
    b_in, e_in, s_in, sol, res,
    g, pk, re_, rw_, a0, ag, c, t1, got1, t2, got2, l6, far, half, halves,
    *rest,
):
    fine0, fine1, fine2, fine3, fine4, fine5 = rest[:9], rest[9:22], rest[22:32], rest[32:45], rest[45:58], rest[58:72]
    in_sem, a_send, a_recv, cs_send, cs_recv, fs_send, fs_recv, c1_send, c1_recv, c2_send, c2_recv = rest[72:]

    l0 = Level(1, PAD, N0, g.at[0], g.at[1], g.at[2], *fine0[:5], None, *fine0[5:])
    l1 = Level(2, PAD, N0 // 2, *fine1)
    l2 = Level(1, PAD2, 64, c.at[0], c.at[1], c.at[2], *fine2)
    l3 = Level(2, PAD, 32, *fine3)
    l4 = Level(4, PAD, 16, *fine4)
    l5 = Level(8, PAD, 8, *fine5)
    lat, lon = lax.axis_index("lat"), lax.axis_index("lon")

    def device(dlon, dlat):
        return {"lon": lax.rem(lon + dlon + NLON, NLON), "lat": lax.rem(lat + dlat + NLAT, NLAT)}

    block = (lon // BLOCK) * BLOCK
    inner = lax.rem(lon, BLOCK)

    def mate1(d):
        return {"lon": block + lax.rem(inner + d, BLOCK), "lat": lat}

    def mate2(d):
        return device(BLOCK * (d // 4), d % 4)

    top = PAD + H
    loads = [
        pltpu.make_async_copy(x.at[:, pl.ds(128 * j, 128)], g.at[i, j, pl.ds(top, ROWS)], in_sem.at[i, j])
        for i, x in enumerate((b_in, e_in, s_in))
        for j in range(4)
    ]
    barrier = pltpu.get_barrier_semaphore()
    greeted = [device(*d) for d in HALO + SPREAD[:11]]
    greeted += [mate1(d) for d in range(1, BLOCK)] + [mate2(d) for d in range(4, 16)]
    for k, other in enumerate(greeted):
        pl.semaphore_signal(barrier, inc=1, device_id=other, device_id_type=MESH)
        if k == len(HALO) - 1:
            for copy in loads:
                copy.start()

    def clear(ref, l):
        zero = jnp.zeros((l.pad, WIDE), F32)
        st(ref, 0, zero)
        st(ref, l.pad + l.n, zero)

    for l in (l0, l1):
        for ref in (l.wf, l.v, l.v2, l.q):
            clear(ref, l)
    for l in (l2, l3, l4, l5):
        for ref in (l.wf, l.v, l.v2, l.q, l.so):
            clear(ref, l)
    for ref in (l2.ae, l2.aw, l2.as_, l2.an):
        clear(ref, l2)
    for ref in (l5.e, l5.r):
        clear(ref, l5)

    for copy in loads:
        copy.wait()

    l8 = lanes((8, 128))
    for k in range(ROWS // 8):
        rows = slice(top + 8 * k, top + 8 * k + 8)
        first = [g[i, 0, rows] for i in range(3)]
        last = [g[i, 3, rows] for i in range(3)]
        x = jnp.where(l8 < 16, first[0], jnp.where(l8 < 32, roll_l(first[1], 16), roll_l(first[2], 32)))
        y = jnp.where(l8 >= 112, last[0], jnp.where(l8 >= 96, roll_l(last[1], -16), roll_l(last[2], -32)))
        pk[8 * k:8 * k + 8] = jnp.where(l8 < 64, x, y)

    own_rows = pl.ds(pl.multiple_of(PAD2 + lat * 16, 16), 16)

    for a in range(0, 16, 8):
        x = ld(g.at[1], top + 4 * a, 8, range(4), 4)
        for j in (1, 2, 3):
            x = x + ld(g.at[1], top + 4 * a + j, 8, range(4), 4)
        y = ld(g.at[2], top + 4 * a + 3, 8, range(4), 4)
        y = y + roll_l(y, -1)
        y = y + roll_l(y, -2)
        rows = pl.ds(pl.multiple_of(PAD2 + lat * 16 + a, 8), 8)
        c[1, 2, rows, :] = compact(x, 3)
        c[2, 2, rows, :] = compact(y, 0)

    pl.semaphore_wait(barrier, len(greeted))

    def send(src, dst, s_sem, r_sem, k, to):
        copy = pltpu.make_async_remote_copy(
            src_ref=src, dst_ref=dst, send_sem=s_sem.at[k], recv_sem=r_sem.at[k], device_id=to, device_id_type=MESH
        )
        copy.start()
        return copy

    def spread_lat(index, s_sem, r_sem):
        part = c.at[index, 2, own_rows]
        return [send(part, part, s_sem, r_sem, k, device(0, d)) for k, d in enumerate(SPREAD_LAT)]

    def spread_lon(index, s_sem, r_sem):
        rows = pl.ds(PAD2, 64)
        return [
            send(c.at[index, 2, rows], c.at[index, 2 - d, rows], s_sem, r_sem, 3 + k, device(d, 0))
            for k, d in enumerate(SPREAD_LON)
        ]

    conds = spread_lat(pl.ds(1, 2), cs_send, cs_recv)
    halos = []
    for k, (dlon, dlat) in enumerate(HALO):
        first_row, count = {0: (0, ROWS), 1: (ROWS - H, H), -1: (0, H)}[dlat]
        to = {0: H, 1: 0, -1: H + ROWS}[dlat]
        if dlon == 0:
            first_row, to = (ROWS - 8, H - 8) if dlat == 1 else (0, H + ROWS)
            src = g.at[:, pl.ds(0, 4), pl.ds(top + first_row, 8)]
            dst = g.at[:, pl.ds(0, 4), pl.ds(PAD + to, 8)]
        else:
            src = pk.at[pl.ds(first_row, count)]
            dst = (rw_ if dlon == 1 else re_).at[pl.ds(to, count)]
        halos.append(send(src, dst, a_send, a_recv, k, device(dlon, dlat)))

    far_halos = [
        send(g.at[:, pl.ds(0, 4), pl.ds(top + first, 8)], far.at[i], a_send, a_recv, 8 + i, device(0, dlat))
        for i, (dlat, first) in enumerate(((1, ROWS - 16), (-1, 8)))
    ]


    for copy in conds:
        copy.wait_recv()
    conds_lon = spread_lon(pl.ds(1, 2), cs_send, cs_recv)

    for copy in halos:
        copy.wait_recv()

    has_north = jnp.where(lat > 0, 1.0, 0.0).astype(F32)
    used = (l8 < 16) | (l8 >= 112)
    for k in range(N0 // 8):
        x = jnp.where(l8 < 64, re_[8 * k:8 * k + 8], rw_[8 * k:8 * k + 8])
        for i, other in ((0, 0.0), (1, 1.0), (2, 1.0)):
            y = x if i == 0 else jnp.where(l8 < 64, roll_l(x, -16 * i), roll_l(x, 16 * i))
            g[i, 4, PAD + 8 * k:PAD + 8 * k + 8, :] = jnp.where(used, y, other)
    g[2, :, PAD + 8:PAD + H] = g[2, :, PAD + 8:PAD + H] * has_north

    def bounds(halo, own):
        return jnp.where(lat > 0, 0, halo), jnp.where(lat < NLAT - 1, 2 * halo + own, halo + own)

    coeffs(l0, 16, bounds(H, ROWS), True, 8, 80)
    sweep(l0, l0.wf, l0.v, True, 8, 80, 16)
    coarsen(l0, l1)
    remainder(l0, 16, 8, 80)
    coeffs(l1, 16, bounds(H // 2, ROWS // 2))
    restrict(l0, l1)
    sweep(l1, l1.wf, l1.v, True, 0, 48, 16)
    remainder(l1, 16)
    for a in range(0, 16, 8):
        x = ld(l1.r, PAD + 8 + 2 * a, 8, range(4), 2) + ld(l1.r, PAD + 9 + 2 * a, 8, range(4), 2)
        rows = pl.ds(pl.multiple_of(PAD2 + lat * 16 + a, 8), 8)
        c[0, 2, rows, :] = compact(x + roll_l(x, -2), 0)
    x = c[0, 2, pl.ds(pl.multiple_of(PAD2 + lat * 16, 8), 8), :]
    y = roll_l(c[0, 2, pl.ds(pl.multiple_of(PAD2 + lat * 16 + 8, 8), 8), :], 64)
    half[0] = jnp.where(l8 >= 64, x, y)
    half[1] = jnp.where(l8 < 64, x, y)
    fields = []
    for k, d in enumerate(SPREAD):
        if abs(d[0]) == 2:
            side = 0 if d[0] == 2 else 1
            fields.append(send(half.at[side], halves.at[side, lat], fs_send, fs_recv, k, device(*d)))
        else:
            part = c.at[0, 2, own_rows]
            fields.append(send(part, c.at[0, 2 - d[0], own_rows], fs_send, fs_recv, k, device(*d)))

    for i, first in enumerate((PAD, PAD + N0 - 8)):
        far_halos[i].wait_recv()
        for k in range(3):
            for j in range(4):
                g[k, j, first:first + 8] = far[i, k, j]
    g[2, :, PAD:PAD + 8] = g[2, :, PAD:PAD + 8] * has_north
    for r0 in (0, N0 - 16):
        coeffs(l0, 16, bounds(H, ROWS), True, r0, 16)
    for r0 in (0, N0 - 16):
        sweep(l0, l0.wf, l0.v, True, r0, 16, 16)
        coarsen(l0, l1, r0 // 2, 8)
    for r0 in (0, N0 - 16):
        remainder(l0, 16, r0, 16)
        coeffs(l1, 8, bounds(H // 2, ROWS // 2), False, r0 // 2, 8)
    for r0 in (0, N0 - 16):
        restrict(l0, l1, r0 // 2, 8)
    for r0 in (0, N0 // 2 - 8):
        sweep(l1, l1.wf, l1.v, True, r0, 8, 8)

    for copy in conds_lon:
        copy.wait_recv()
    coeffs(l2, 16)
    coarsen(l2, l3)
    coeffs(l3, 16)
    coarsen(l3, l4)
    coeffs(l4, 16)
    coarsen(l4, l5)
    coeffs(l5, 8)


    def twice(l, v, source, r0, count, ch, blocks=ALL):
        sweep(l, v, l.v2, source, r0, count, ch, blocks)
        sweep(l, l.v2, v, source, r0, count, ch, blocks)

    def rise_coarse(name, source):
        u = [getattr(l, name) for l in (l0, l1, l2, l3, l4, l5)]
        twice(l5, u[5], source, 0, 8, 8, MID)
        prolong(l5, l4, u[5], u[4], 0, 8, source, MID)
        twice(l4, u[4], source, 0, 16, 16, MID)
        prolong(l4, l3, u[4], u[3], 0, 16, source, MID)
        twice(l3, u[3], source, 0, 32, 16, MID)
        near = lat * 8 - 4
        prolong(l3, l2, u[3], u[2], near, 16, source, MID)
        near = pl.multiple_of(lat * 16 - 8, 8)
        twice(l2, u[2], source, near, 32, 16, MID)

    def rise_fine(name, source):
        u = [getattr(l, name) for l in (l0, l1, l2)]
        for i in range(3):
            e = expand(u[2], PAD2 + lat * 16 - 4 + 8 * i)
            spread_rows(u[1], PAD + 16 * i, e, source)
        twice(l1, u[1], source, 0, 48, 16)
        prolong(l1, l0, u[1], u[0], 0, 48, source)
        twice(l0, u[0], source, 8, 80, 16)

    def applied(v, out, sums, n):
        def body(r, carry):
            x, av = operator(l0, v, top + r, 16)
            x, av = x[:, :COLS], av[:, :COLS]
            out[pl.ds(r, 16)] = av
            more = sums(pl.ds(r, 16), ld(l0.f, top + r, 16, range(4)), x, av)
            return tuple(y + (z[:8] + z[8:]) for y, z in zip(carry, more))

        carry = (jnp.zeros((8, COLS), F32),) * n
        for r in range(0, ROWS, 16):
            carry = body(r, carry)
        return carry

    x = pair(l5.e, PAD, 8, 0) + pair(l5.e, PAD, 8, 1)
    e6 = roll_l(x, -8)
    x = pair(l5.so, PAD, 8, 1)
    s6 = x + roll_l(x, -8)
    row6, lane6 = rows_of((8, WIDE)), lanes((8, WIDE))
    west6 = roll_l(e6, 16)
    north6 = jnp.where(row6 == 0, 0.0, pltpu.roll(s6, 1, 0))
    w6 = jnp.where(row6 < 4, OMEGA / (((e6 + west6) + s6) + north6), 0.0)
    for i, x in enumerate((e6, west6, s6, north6, w6, w6 * e6, w6 * west6, w6 * s6, w6 * north6)):
        st(l6, 8 * i, x)

    st(l5.q, PAD, jnp.ones((8, WIDE), F32))
    rise_coarse("q", False)
    for copy in halos + far_halos + conds:
        copy.wait_send()
    rise_fine("q", False)
    for copy in fields + conds_lon:
        copy.wait_send()
    sums_q = applied(l0.q, ag, lambda rows, b, v, av: (b * v, v * av), 2)

    for copy in fields:
        copy.wait_recv()

    for i in range(4):
        for side, slot in ((0, 0), (1, 4)):
            x = halves[side, i]
            c[0, slot, PAD2 + 16 * i:PAD2 + 16 * i + 8, :] = x
            c[0, slot, PAD2 + 16 * i + 8:PAD2 + 16 * i + 16, :] = roll_l(x, 64)

    def first(r):
        st(l2.wf, PAD2 + r, ld(l2.w, PAD2 + r, 16) * ld(l2.f, PAD2 + r, 16))

    loop(0, 64, 16, first)
    sweep(l2, l2.wf, l2.v, True, 0, 64, 16)
    remainder(l2, 16)
    for l, coarse in ((l2, l3), (l3, l4), (l4, l5)):
        restrict(l, coarse)
        sweep(coarse, coarse.wf, coarse.v, True, 0, coarse.n, min(16, coarse.n))
        remainder(coarse, min(16, coarse.n))

    x = pair(l5.r, PAD, 8, 0) + pair(l5.r, PAD, 8, 1)
    f6 = x + roll_l(x, -8)
    e6, west6, s6, north6, w6, ae6, aw6, as6, an6 = [ld(l6, 8 * i, 8) for i in range(9)]
    wf6 = w6 * f6
    field = wf6
    for _ in range(COARSE_SWEEPS - 1):
        x = ae6 * roll_l(field, -16) + aw6 * roll_l(field, 16)
        y = as6 * pltpu.roll(field, 7, 0) + an6 * pltpu.roll(field, 1, 0)
        field = (((1.0 - OMEGA) * field + wf6) + y) + x
    lon6 = e6 * (field - roll_l(field, -16)) + west6 * (field - roll_l(field, 16))
    lat6 = s6 * (field - pltpu.roll(field, 7, 0)) + north6 * (field - pltpu.roll(field, 1, 0))
    left = f6 - (lon6 + lat6)
    mine = ((lane6 & 15) == 0) & (lane6 >= 256) & (lane6 < 384)
    left = jnp.where(mine & (row6 == lat), left, 0.0)[:, 256:384]
    last = jnp.where(mine & (row6 == 3) & (lat == 3), s6, 0.0)[:, 256:384]

    e = jnp.where((lane6 & 8) == 0, field, roll_l(field, 8))
    for odd in (0, 1):
        st(l5.r, odd, e, ALL, 2)
    st(l5.v, PAD, ld(l5.v, PAD, 8) + ld(l5.r, 0, 8))
    rise_coarse("v", True)
    rise_fine("v", True)
    sums_v = applied(l0.v, a0, lambda rows, b, v, av: (b * v, v * av, v * ag[rows]), 3)

    def wait_all(got, sem):
        pltpu.make_async_copy(got, got, sem.at[0]).wait()

    def fold(x):
        return (x[:, 0:128] + x[:, 128:256]) + (x[:, 256:384] + x[:, 384:512])

    seven = [left, last, fold(sums_v[0]), fold(sums_q[0]), fold(sums_v[1]), fold(sums_v[2]), fold(sums_q[1])]
    row = rows_of((8, 128))
    total = jnp.zeros((8, 128), F32)
    for i, x in enumerate(seven):
        total = jnp.where(row == i, jnp.sum(x, axis=0, keepdims=True), total)
    t1[...] = total
    for d in FAR1:
        send(t1, got1.at[d - 1], c1_send, c1_recv, 0, mate1(d))
    wait_all(got1, c1_recv)

    def gathered(total, got):
        parts = [total] + [got[d] for d in range(15)]
        while len(parts) > 1:
            parts = [x + y for x, y in zip(parts[::2], parts[1::2])]
        return parts[0]

    total = gathered(total, got1)
    t2[...] = total
    for d in FAR2:
        send(t2, got2.at[d - 1], c2_send, c2_recv, 0, mate2(d))
    wait_all(got1, c1_send)
    wait_all(got2, c2_recv)
    total = gathered(total, got2)
    for by in (64, 32, 16, 8, 4, 2, 1):
        total = total + pltpu.roll(total, by, 1)
    n_left, n_last, bv, bq, vav, vaq, qaq = [total[i:i + 1] for i in range(7)]
    const = n_left / n_last
    step = (bv + const * bq) / ((vav + (2.0 * const) * vaq) + (const * const) * qaq)
    both = jnp.concatenate([step * const] * 4, axis=1)
    step = jnp.concatenate([step] * 4, axis=1)

    for r in range(0, ROWS, 16):
        rows = pl.ds(r, 16)
        sol[rows] = step * ld(l0.v, top + r, 16, range(4)) + both * ld(l0.q, top + r, 16, range(4))
        res[rows] = ld(l0.f, top + r, 16, range(4)) - (step * a0[rows] + both * ag[rows])
    wait_all(got2, c2_send)


def store(sol, res, sol_out, res_out, sem):
    copies = [pltpu.make_async_copy(x, y, sem.at[i]) for i, (x, y) in enumerate(((sol, sol_out), (res, res_out)))]
    for copy in copies:
        copy.start()
    for copy in copies:
        copy.wait()


def body(guidance, cond_lon, cond_lat):
    def vm(*shape):
        return pltpu.VMEM(shape, F32)

    def wide(n, count):
        return [vm(5, n, 128)] * count

    dma = pltpu.SemaphoreType.DMA
    scratch = [vm(3, 5, N0 + 2 * PAD, 128), vm(ROWS, 128), vm(N0, 128), vm(N0, 128), vm(ROWS, COLS), vm(ROWS, COLS)]
    scratch += [vm(3, 5, 64 + 2 * PAD2, 128), vm(8, 128), vm(15, 8, 128), vm(8, 128), vm(15, 8, 128), vm(5, 72, 128), vm(2, 3, 4, 8, 128), vm(2, 8, 128), vm(2, 4, 8, 128)]
    scratch += wide(N0 + 2 * PAD, 9) + wide(N0 // 2 + 2 * PAD, 13) + wide(64 + 2 * PAD2, 10)
    scratch += wide(32 + 2 * PAD, 13) + wide(16 + 2 * PAD, 13) + wide(8 + 2 * PAD, 14)
    scratch += [dma((3, 4)), dma((10,)), dma((10,)), dma((7,)), dma((7,)), dma((19,)), dma((19,))] + [dma((1,))] * 4
    sol, res = pl.pallas_call(
        kernel,
        out_shape=(pltpu.VMEM((ROWS, COLS), F32),) * 2,
        in_specs=[pl.BlockSpec(memory_space=pltpu.HBM)] * 3,
        out_specs=(pl.BlockSpec(memory_space=pltpu.VMEM),) * 2,
        scratch_shapes=scratch,
        compiler_params=pltpu.CompilerParams(
            collective_id=0, has_side_effects=True, vmem_limit_bytes=60 * 1024 * 1024
        ),
        cost_estimate=pl.CostEstimate(flops=10_000_000, bytes_accessed=655360, transcendentals=0),
    )(guidance, cond_lon, cond_lat)
    return pl.pallas_call(
        store,
        out_shape=(jax.ShapeDtypeStruct((ROWS, COLS), F32),) * 2,
        in_specs=[pl.BlockSpec(memory_space=pl.ANY)] * 2,
        out_specs=(pl.BlockSpec(memory_space=pl.ANY),) * 2,
        scratch_shapes=[dma((2,))],
        cost_estimate=pl.CostEstimate(flops=0, bytes_accessed=524288, transcendentals=0),
    )(sol, res)


def solution(mesh):
    spec = P("lat", "lon")
    return jax.shard_map(body, mesh=mesh, in_specs=(spec,) * 3, out_specs=(spec,) * 2, check_vma=False)
```

```python
import jax
import jax.numpy as jnp
from jax import lax
from jax.experimental import pallas as pl
from jax.experimental.pallas import tpu as pltpu
from jax.sharding import PartitionSpec as P

OMEGA = 0.8
COARSE_SWEEPS = 8
NLAT, NLON, BLOCK = 4, 64, 16
ROWS, COLS = 64, 512
H = 16
PAD = 8
PAD2 = 16
N0 = ROWS + 2 * H
WIDE = COLS + 128
ALL = range(5)
MID = range(1, 4)
MESH = pl.DeviceIdType.MESH
F32 = jnp.float32

HALO = ((1, 1), (1, -1), (-1, 1), (-1, -1), (1, 0), (-1, 0), (0, 1), (0, -1))
SPREAD_LAT = (1, 2, 3)
SPREAD_LON = (2, -2, 1, -1)
SPREAD = ((2, 2), (-2, 2), (1, 2), (-1, 2), (2, 1), (2, -1), (-2, 1), (-2, -1), (0, 2), (2, 0), (-2, 0))
SPREAD += ((1, 1), (1, -1), (-1, 1), (-1, -1), (0, 1), (0, -1), (1, 0), (-1, 0))
FAR1 = (8, 7, 9, 6, 10, 5, 11, 4, 12, 3, 13, 2, 14, 1, 15)
FAR2 = (10, 9, 11, 6, 14, 2, 8, 5, 7, 13, 15, 1, 3, 4, 12)


def lanes(shape):
    return lax.broadcasted_iota(jnp.int32, shape, len(shape) - 1)


def rows_of(shape):
    return lax.broadcasted_iota(jnp.int32, shape, 0)


def roll_l(x, by):
    return pltpu.roll(x, by % x.shape[1], 1)


def ld(ref, start, n, blocks=ALL, stride=None):
    rows = pl.ds(start, n) if stride is None else pl.ds(start, n, stride=stride)
    return jnp.concatenate([ref[j, rows, :] for j in blocks], axis=1)


def st(ref, start, x, blocks=ALL, stride=None):
    n = x.shape[0]
    rows = pl.ds(start, n) if stride is None else pl.ds(start, n, stride=stride)
    for i, j in enumerate(blocks):
        ref[j, rows, :] = x[:, 128 * i:128 * (i + 1)]


def loop(r0, count, ch, body):
    for k in range(count // ch):
        body(r0 + k * ch)


class Level:
    def __init__(self, s, pad, n, f, e, so, west, ae, aw, as_, an, w, wf, v, v2, q, r=None):
        self.s, self.pad, self.n = s, pad, n
        self.f, self.e, self.so, self.west = f, e, so, west
        self.ae, self.aw, self.as_, self.an, self.w, self.wf = ae, aw, as_, an, w, wf
        self.v, self.v2, self.q, self.r = v, v2, q, v2 if r is None else r


def coeffs(l, ch, keep=None, source=False, r0=0, count=None):
    def body(r):
        p = l.pad + r
        e, so, no = ld(l.e, p, ch), ld(l.so, p, ch), ld(l.so, p - 1, ch)
        we = roll_l(e, l.s)
        wk = OMEGA / (((e + we) + so) + no)
        if keep is not None:
            row = rows_of(wk.shape) + r
            wk = jnp.where((row >= keep[0]) & (row < keep[1]), wk, 0.0)
        st(l.west, p, we)
        st(l.ae, p, wk * e)
        st(l.aw, p, wk * we)
        st(l.as_, p, wk * so)
        st(l.an, p, wk * no)
        if source:
            st(l.wf, p, wk * ld(l.f, p, ch))
        else:
            st(l.w, p, wk)

    loop(r0, l.n if count is None else count, ch, body)


def sweep(l, src, dst, source, r0, count, ch, blocks=ALL):
    def body(r):
        p = l.pad + r
        v = ld(src, p, ch, blocks)
        x = ld(l.ae, p, ch, blocks) * roll_l(v, -l.s) + ld(l.aw, p, ch, blocks) * roll_l(v, l.s)
        y = ld(l.as_, p, ch, blocks) * ld(src, p + 1, ch, blocks) + ld(l.an, p, ch, blocks) * ld(src, p - 1, ch, blocks)
        z = (1.0 - OMEGA) * v
        if source:
            z = z + ld(l.wf, p, ch, blocks)
        st(dst, p, (y + z) + x, blocks)

    loop(r0, count, ch, body)


def operator(l, v, p, ch):
    x = ld(v, p, ch)
    lon = ld(l.e, p, ch) * (x - roll_l(x, -l.s)) + ld(l.west, p, ch) * (x - roll_l(x, l.s))
    lat = ld(l.so, p, ch) * (x - ld(v, p + 1, ch)) + ld(l.so, p - 1, ch) * (x - ld(v, p - 1, ch))
    return x, lat + lon


def remainder(l, ch, r0=0, count=None):
    def body(r):
        p = l.pad + r
        st(l.r, p, ld(l.f, p, ch) - operator(l, l.v, p, ch)[1])

    loop(r0, l.n if count is None else count, ch, body)


def pair(ref, start, n, odd, blocks=ALL):
    return ld(ref, start + odd, n, blocks, 2)


def restrict(l, c, a0=0, count=None):
    count = c.n if count is None else count
    ch = min(16, count)

    def body(a):
        x = pair(l.r, l.pad + 2 * a, ch, 0) + pair(l.r, l.pad + 2 * a, ch, 1)
        x = x + roll_l(x, -l.s)
        st(c.f, c.pad + a, x)
        st(c.wf, c.pad + a, x * ld(c.w, c.pad + a, ch))

    for a in range(a0, a0 + count, ch):
        body(a)


def coarsen(l, c, a0=0, count=None):
    count = c.n if count is None else count
    ch = min(16, count)
    for a in range(a0, a0 + count, ch):
        x = pair(l.e, l.pad + 2 * a, ch, 0) + pair(l.e, l.pad + 2 * a, ch, 1)
        st(c.e, c.pad + a, roll_l(x, -l.s))
        y = pair(l.so, l.pad + 2 * a, ch, 1)
        st(c.so, c.pad + a, y + roll_l(y, -l.s))


def spread_rows(v, start, e, add, blocks=ALL):
    for odd in (0, 1):
        x = e
        if add:
            x = x + ld(v, start + odd, e.shape[0], blocks, 2)
        st(v, start + odd, x, blocks, 2)


def prolong(c, l, src, dst, a0, n, add, blocks=ALL):
    for a in range(0, n, 8):
        e = ld(src, c.pad + a0 + a, 8, blocks)
        e = jnp.where((lanes(e.shape) & l.s) == 0, e, roll_l(e, l.s))
        spread_rows(dst, l.pad + 2 * (a0 + a), e, add, blocks)


def pick(x, index):
    return jnp.take_along_axis(x, index, axis=1, mode="promise_in_bounds")


def compact(x, offset):
    l = lanes((8, 128))
    index = (l % 32) * 4 + offset
    out = pick(x[:, 384:512], index)
    for j in (2, 1, 0):
        out = jnp.where(l < 32 * (j + 1), pick(x[:, 128 * j:128 * (j + 1)], index), out)
    return out


def expand(x, base):
    l = lanes((8, 128))
    q = l // 4
    own = x[2, pl.ds(base, 8), :]
    parts = [pick(own, q + 32 * j) for j in range(4)]
    east = pick(x[3, pl.ds(base, 8), :], q)
    west = pick(x[1, pl.ds(base, 8), :], q + 96)
    return jnp.concatenate(parts + [jnp.where(l < 64, east, west)], axis=1)


def kernel(
    b_in, e_in, s_in, sol, res,
    g, pk, re_, rw_, a0, ag, c, t1, got1, t2, got2, l6, far, half, halves,
    *rest,
):
    fine0, fine1, fine2, fine3, fine4, fine5 = rest[:9], rest[9:22], rest[22:32], rest[32:45], rest[45:58], rest[58:72]
    in_sem, a_send, a_recv, cs_send, cs_recv, fs_send, fs_recv, c1_send, c1_recv, c2_send, c2_recv = rest[72:]

    l0 = Level(1, PAD, N0, g.at[0], g.at[1], g.at[2], *fine0[:5], None, *fine0[5:])
    l1 = Level(2, PAD, N0 // 2, *fine1)
    l2 = Level(1, PAD2, 64, c.at[0], c.at[1], c.at[2], *fine2)
    l3 = Level(2, PAD, 32, *fine3)
    l4 = Level(4, PAD, 16, *fine4)
    l5 = Level(8, PAD, 8, *fine5)
    lat, lon = lax.axis_index("lat"), lax.axis_index("lon")

    def device(dlon, dlat):
        return {"lon": lax.rem(lon + dlon + NLON, NLON), "lat": lax.rem(lat + dlat + NLAT, NLAT)}

    block = (lon // BLOCK) * BLOCK
    inner = lax.rem(lon, BLOCK)

    def mate1(d):
        return {"lon": block + lax.rem(inner + d, BLOCK), "lat": lat}

    def mate2(d):
        return device(BLOCK * (d // 4), d % 4)

    top = PAD + H
    loads = [
        pltpu.make_async_copy(x.at[:, pl.ds(128 * j, 128)], g.at[i, j, pl.ds(top, ROWS)], in_sem.at[i, j])
        for i, x in enumerate((b_in, e_in, s_in))
        for j in range(4)
    ]
    barrier = pltpu.get_barrier_semaphore()
    greeted = [device(*d) for d in HALO + SPREAD[:11]]
    greeted += [mate1(d) for d in range(1, BLOCK)] + [mate2(d) for d in range(4, 16)]
    for k, other in enumerate(greeted):
        pl.semaphore_signal(barrier, inc=1, device_id=other, device_id_type=MESH)
        if k == len(HALO) - 1:
            for copy in loads:
                copy.start()

    def clear(ref, l):
        zero = jnp.zeros((l.pad, WIDE), F32)
        st(ref, 0, zero)
        st(ref, l.pad + l.n, zero)

    for l in (l0, l1):
        for ref in (l.wf, l.v, l.v2, l.q):
            clear(ref, l)
    for l in (l2, l3, l4, l5):
        for ref in (l.wf, l.v, l.v2, l.q, l.so):
            clear(ref, l)
    for ref in (l2.ae, l2.aw, l2.as_, l2.an):
        clear(ref, l2)
    for ref in (l5.e, l5.r):
        clear(ref, l5)

    for copy in loads:
        copy.wait()

    l8 = lanes((8, 128))
    for k in range(ROWS // 8):
        rows = slice(top + 8 * k, top + 8 * k + 8)
        first = [g[i, 0, rows] for i in range(3)]
        last = [g[i, 3, rows] for i in range(3)]
        x = jnp.where(l8 < 16, first[0], jnp.where(l8 < 32, roll_l(first[1], 16), roll_l(first[2], 32)))
        y = jnp.where(l8 >= 112, last[0], jnp.where(l8 >= 96, roll_l(last[1], -16), roll_l(last[2], -32)))
        pk[8 * k:8 * k + 8] = jnp.where(l8 < 64, x, y)

    own_rows = pl.ds(pl.multiple_of(PAD2 + lat * 16, 16), 16)

    for a in range(0, 16, 8):
        x = ld(g.at[1], top + 4 * a, 8, range(4), 4)
        for j in (1, 2, 3):
            x = x + ld(g.at[1], top + 4 * a + j, 8, range(4), 4)
        y = ld(g.at[2], top + 4 * a + 3, 8, range(4), 4)
        y = y + roll_l(y, -1)
        y = y + roll_l(y, -2)
        rows = pl.ds(pl.multiple_of(PAD2 + lat * 16 + a, 8), 8)
        c[1, 2, rows, :] = compact(x, 3)
        c[2, 2, rows, :] = compact(y, 0)

    pl.semaphore_wait(barrier, len(greeted))

    def send(src, dst, s_sem, r_sem, k, to):
        copy = pltpu.make_async_remote_copy(
            src_ref=src, dst_ref=dst, send_sem=s_sem.at[k], recv_sem=r_sem.at[k], device_id=to, device_id_type=MESH
        )
        copy.start()
        return copy

    def spread_lat(index, s_sem, r_sem):
        part = c.at[index, 2, own_rows]
        return [send(part, part, s_sem, r_sem, k, device(0, d)) for k, d in enumerate(SPREAD_LAT)]

    def spread_lon(index, s_sem, r_sem):
        rows = pl.ds(PAD2, 64)
        return [
            send(c.at[index, 2, rows], c.at[index, 2 - d, rows], s_sem, r_sem, 3 + k, device(d, 0))
            for k, d in enumerate(SPREAD_LON)
        ]

    conds = spread_lat(pl.ds(1, 2), cs_send, cs_recv)
    halos = []
    for k, (dlon, dlat) in enumerate(HALO):
        first_row, count = {0: (0, ROWS), 1: (ROWS - H, H), -1: (0, H)}[dlat]
        to = {0: H, 1: 0, -1: H + ROWS}[dlat]
        if dlon == 0:
            first_row, to = (ROWS - 8, H - 8) if dlat == 1 else (0, H + ROWS)
            src = g.at[:, pl.ds(0, 4), pl.ds(top + first_row, 8)]
            dst = g.at[:, pl.ds(0, 4), pl.ds(PAD + to, 8)]
        else:
            src = pk.at[pl.ds(first_row, count)]
            dst = (rw_ if dlon == 1 else re_).at[pl.ds(to, count)]
        halos.append(send(src, dst, a_send, a_recv, k, device(dlon, dlat)))

    far_halos = [
        send(g.at[:, pl.ds(0, 4), pl.ds(top + first, 8)], far.at[i], a_send, a_recv, 8 + i, device(0, dlat))
        for i, (dlat, first) in enumerate(((1, ROWS - 16), (-1, 8)))
    ]


    for copy in conds:
        copy.wait_recv()
    conds_lon = spread_lon(pl.ds(1, 2), cs_send, cs_recv)

    for copy in halos:
        copy.wait_recv()

    has_north = jnp.where(lat > 0, 1.0, 0.0).astype(F32)
    used = (l8 < 16) | (l8 >= 112)
    for k in range(N0 // 8):
        x = jnp.where(l8 < 64, re_[8 * k:8 * k + 8], rw_[8 * k:8 * k + 8])
        for i, other in ((0, 0.0), (1, 1.0), (2, 1.0)):
            y = x if i == 0 else jnp.where(l8 < 64, roll_l(x, -16 * i), roll_l(x, 16 * i))
            g[i, 4, PAD + 8 * k:PAD + 8 * k + 8, :] = jnp.where(used, y, other)
    g[2, :, PAD + 8:PAD + H] = g[2, :, PAD + 8:PAD + H] * has_north

    def bounds(halo, own):
        return jnp.where(lat > 0, 0, halo), jnp.where(lat < NLAT - 1, 2 * halo + own, halo + own)

    coeffs(l0, 16, bounds(H, ROWS), True, 8, 80)
    sweep(l0, l0.wf, l0.v, True, 8, 80, 16)
    coarsen(l0, l1)
    remainder(l0, 16, 8, 80)
    coeffs(l1, 16, bounds(H // 2, ROWS // 2))
    restrict(l0, l1)
    sweep(l1, l1.wf, l1.v, True, 0, 48, 16)
    remainder(l1, 16)
    for a in range(0, 16, 8):
        x = ld(l1.r, PAD + 8 + 2 * a, 8, range(4), 2) + ld(l1.r, PAD + 9 + 2 * a, 8, range(4), 2)
        rows = pl.ds(pl.multiple_of(PAD2 + lat * 16 + a, 8), 8)
        c[0, 2, rows, :] = compact(x + roll_l(x, -2), 0)
    x = c[0, 2, pl.ds(pl.multiple_of(PAD2 + lat * 16, 8), 8), :]
    y = roll_l(c[0, 2, pl.ds(pl.multiple_of(PAD2 + lat * 16 + 8, 8), 8), :], 64)
    half[0] = jnp.where(l8 >= 64, x, y)
    half[1] = jnp.where(l8 < 64, x, y)
    fields = []
    for k, d in enumerate(SPREAD):
        if abs(d[0]) == 2:
            side = 0 if d[0] == 2 else 1
            fields.append(send(half.at[side], halves.at[side, lat], fs_send, fs_recv, k, device(*d)))
        else:
            part = c.at[0, 2, own_rows]
            fields.append(send(part, c.at[0, 2 - d[0], own_rows], fs_send, fs_recv, k, device(*d)))

    for i, first in enumerate((PAD, PAD + N0 - 8)):
        far_halos[i].wait_recv()
        for k in range(3):
            for j in range(4):
                g[k, j, first:first + 8] = far[i, k, j]
    g[2, :, PAD:PAD + 8] = g[2, :, PAD:PAD + 8] * has_north
    for r0 in (0, N0 - 16):
        coeffs(l0, 16, bounds(H, ROWS), True, r0, 16)
    for r0 in (0, N0 - 16):
        sweep(l0, l0.wf, l0.v, True, r0, 16, 16)
        coarsen(l0, l1, r0 // 2, 8)
    for r0 in (0, N0 - 16):
        remainder(l0, 16, r0, 16)
        coeffs(l1, 8, bounds(H // 2, ROWS // 2), False, r0 // 2, 8)
    for r0 in (0, N0 - 16):
        restrict(l0, l1, r0 // 2, 8)
    for r0 in (0, N0 // 2 - 8):
        sweep(l1, l1.wf, l1.v, True, r0, 8, 8)

    for copy in conds_lon:
        copy.wait_recv()
    coeffs(l2, 16)
    coarsen(l2, l3)
    coeffs(l3, 16)
    coarsen(l3, l4)
    coeffs(l4, 16)
    coarsen(l4, l5)
    coeffs(l5, 8)


    def twice(l, v, source, r0, count, ch, blocks=ALL):
        sweep(l, v, l.v2, source, r0, count, ch, blocks)
        sweep(l, l.v2, v, source, r0, count, ch, blocks)

    def rise_coarse(name, source):
        u = [getattr(l, name) for l in (l0, l1, l2, l3, l4, l5)]
        twice(l5, u[5], source, 0, 8, 8, MID)
        prolong(l5, l4, u[5], u[4], 0, 8, source, MID)
        twice(l4, u[4], source, 0, 16, 16, MID)
        prolong(l4, l3, u[4], u[3], 0, 16, source, MID)
        twice(l3, u[3], source, 0, 32, 16, MID)
        near = lat * 8 - 4
        prolong(l3, l2, u[3], u[2], near, 16, source, MID)
        near = pl.multiple_of(lat * 16 - 8, 8)
        twice(l2, u[2], source, near, 32, 16, MID)

    def rise_fine(name, source):
        u = [getattr(l, name) for l in (l0, l1, l2)]
        for i in range(3):
            e = expand(u[2], PAD2 + lat * 16 - 4 + 8 * i)
            spread_rows(u[1], PAD + 16 * i, e, source)
        twice(l1, u[1], source, 0, 48, 16)
        prolong(l1, l0, u[1], u[0], 0, 48, source)
        twice(l0, u[0], source, 8, 80, 16)

    def applied(v, out, sums, n):
        def body(r, carry):
            x, av = operator(l0, v, top + r, 16)
            x, av = x[:, :COLS], av[:, :COLS]
            out[pl.ds(r, 16)] = av
            more = sums(pl.ds(r, 16), ld(l0.f, top + r, 16, range(4)), x, av)
            return tuple(y + (z[:8] + z[8:]) for y, z in zip(carry, more))

        carry = (jnp.zeros((8, COLS), F32),) * n
        for r in range(0, ROWS, 16):
            carry = body(r, carry)
        return carry

    x = pair(l5.e, PAD, 8, 0) + pair(l5.e, PAD, 8, 1)
    e6 = roll_l(x, -8)
    x = pair(l5.so, PAD, 8, 1)
    s6 = x + roll_l(x, -8)
    row6, lane6 = rows_of((8, WIDE)), lanes((8, WIDE))
    west6 = roll_l(e6, 16)
    north6 = jnp.where(row6 == 0, 0.0, pltpu.roll(s6, 1, 0))
    w6 = jnp.where(row6 < 4, OMEGA / (((e6 + west6) + s6) + north6), 0.0)
    for i, x in enumerate((e6, west6, s6, north6, w6, w6 * e6, w6 * west6, w6 * s6, w6 * north6)):
        st(l6, 8 * i, x)

    st(l5.q, PAD, jnp.ones((8, WIDE), F32))
    rise_coarse("q", False)
    for copy in halos + far_halos + conds:
        copy.wait_send()
    rise_fine("q", False)
    for copy in fields + conds_lon:
        copy.wait_send()
    sums_q = applied(l0.q, ag, lambda rows, b, v, av: (b * v, v * av), 2)

    for copy in fields:
        copy.wait_recv()

    for i in range(4):
        for side, slot in ((0, 0), (1, 4)):
            x = halves[side, i]
            c[0, slot, PAD2 + 16 * i:PAD2 + 16 * i + 8, :] = x
            c[0, slot, PAD2 + 16 * i + 8:PAD2 + 16 * i + 16, :] = roll_l(x, 64)

    def first(r):
        st(l2.wf, PAD2 + r, ld(l2.w, PAD2 + r, 16) * ld(l2.f, PAD2 + r, 16))

    loop(0, 64, 16, first)
    sweep(l2, l2.wf, l2.v, True, 0, 64, 16)
    remainder(l2, 16)
    for l, coarse in ((l2, l3), (l3, l4), (l4, l5)):
        restrict(l, coarse)
        sweep(coarse, coarse.wf, coarse.v, True, 0, coarse.n, min(16, coarse.n))
        remainder(coarse, min(16, coarse.n))

    x = pair(l5.r, PAD, 8, 0) + pair(l5.r, PAD, 8, 1)
    f6 = x + roll_l(x, -8)
    e6, west6, s6, north6, w6, ae6, aw6, as6, an6 = [ld(l6, 8 * i, 8) for i in range(9)]
    wf6 = w6 * f6
    field = wf6
    for _ in range(COARSE_SWEEPS - 1):
        x = ae6 * roll_l(field, -16) + aw6 * roll_l(field, 16)
        y = as6 * pltpu.roll(field, 7, 0) + an6 * pltpu.roll(field, 1, 0)
        field = (((1.0 - OMEGA) * field + wf6) + y) + x
    lon6 = e6 * (field - roll_l(field, -16)) + west6 * (field - roll_l(field, 16))
    lat6 = s6 * (field - pltpu.roll(field, 7, 0)) + north6 * (field - pltpu.roll(field, 1, 0))
    left = f6 - (lon6 + lat6)
    mine = ((lane6 & 15) == 0) & (lane6 >= 256) & (lane6 < 384)
    left = jnp.where(mine & (row6 == lat), left, 0.0)[:, 256:384]
    last = jnp.where(mine & (row6 == 3) & (lat == 3), s6, 0.0)[:, 256:384]

    e = jnp.where((lane6 & 8) == 0, field, roll_l(field, 8))
    for odd in (0, 1):
        st(l5.r, odd, e, ALL, 2)
    st(l5.v, PAD, ld(l5.v, PAD, 8) + ld(l5.r, 0, 8))
    rise_coarse("v", True)
    rise_fine("v", True)
    sums_v = applied(l0.v, a0, lambda rows, b, v, av: (b * v, v * av, v * ag[rows]), 3)

    def wait_all(got, sem):
        pltpu.make_async_copy(got, got, sem.at[0]).wait()

    def fold(x):
        return (x[:, 0:128] + x[:, 128:256]) + (x[:, 256:384] + x[:, 384:512])

    seven = [left, last, fold(sums_v[0]), fold(sums_q[0]), fold(sums_v[1]), fold(sums_v[2]), fold(sums_q[1])]
    row = rows_of((8, 128))
    total = jnp.zeros((8, 128), F32)
    for i, x in enumerate(seven):
        total = jnp.where(row == i, jnp.sum(x, axis=0, keepdims=True), total)
    t1[...] = total
    for d in FAR1:
        send(t1, got1.at[d - 1], c1_send, c1_recv, 0, mate1(d))
    wait_all(got1, c1_recv)

    def gathered(total, got):
        parts = [total] + [got[d] for d in range(15)]
        while len(parts) > 1:
            parts = [x + y for x, y in zip(parts[::2], parts[1::2])]
        return parts[0]

    total = gathered(total, got1)
    t2[...] = total
    for d in FAR2:
        send(t2, got2.at[d - 1], c2_send, c2_recv, 0, mate2(d))
    wait_all(got1, c1_send)
    wait_all(got2, c2_recv)
    total = gathered(total, got2)
    for by in (64, 32, 16, 8, 4, 2, 1):
        total = total + pltpu.roll(total, by, 1)
    n_left, n_last, bv, bq, vav, vaq, qaq = [total[i:i + 1] for i in range(7)]
    const = n_left / n_last
    step = (bv + const * bq) / ((vav + (2.0 * const) * vaq) + (const * const) * qaq)
    both = jnp.concatenate([step * const] * 4, axis=1)
    step = jnp.concatenate([step] * 4, axis=1)

    for r in range(0, ROWS, 16):
        rows = pl.ds(r, 16)
        sol[rows] = step * ld(l0.v, top + r, 16, range(4)) + both * ld(l0.q, top + r, 16, range(4))
        res[rows] = ld(l0.f, top + r, 16, range(4)) - (step * a0[rows] + both * ag[rows])
    wait_all(got2, c2_send)


def body(guidance, cond_lon, cond_lat):
    def vm(*shape):
        return pltpu.VMEM(shape, F32)

    def wide(n, count):
        return [vm(5, n, 128)] * count

    dma = pltpu.SemaphoreType.DMA
    scratch = [vm(3, 5, N0 + 2 * PAD, 128), vm(ROWS, 128), vm(N0, 128), vm(N0, 128), vm(ROWS, COLS), vm(ROWS, COLS)]
    scratch += [vm(3, 5, 64 + 2 * PAD2, 128), vm(8, 128), vm(15, 8, 128), vm(8, 128), vm(15, 8, 128), vm(5, 72, 128), vm(2, 3, 4, 8, 128), vm(2, 8, 128), vm(2, 4, 8, 128)]
    scratch += wide(N0 + 2 * PAD, 9) + wide(N0 // 2 + 2 * PAD, 13) + wide(64 + 2 * PAD2, 10)
    scratch += wide(32 + 2 * PAD, 13) + wide(16 + 2 * PAD, 13) + wide(8 + 2 * PAD, 14)
    scratch += [dma((3, 4)), dma((10,)), dma((10,)), dma((7,)), dma((7,)), dma((19,)), dma((19,))] + [dma((1,))] * 4
    return pl.pallas_call(
        kernel,
        out_shape=(pltpu.VMEM((ROWS, COLS), F32),) * 2,
        in_specs=[pl.BlockSpec(memory_space=pltpu.HBM)] * 3,
        out_specs=(pl.BlockSpec(memory_space=pltpu.VMEM),) * 2,
        scratch_shapes=scratch,
        compiler_params=pltpu.CompilerParams(
            collective_id=0, has_side_effects=True, vmem_limit_bytes=60 * 1024 * 1024
        ),
        cost_estimate=pl.CostEstimate(flops=10_000_000, bytes_accessed=655360, transcendentals=0),
    )(guidance, cond_lon, cond_lat)


def solution(mesh):
    spec = P("lat", "lon")
    return jax.shard_map(body, mesh=mesh, in_specs=(spec,) * 3, out_specs=(spec,) * 2, check_vma=False)
```

```python
import jax
import jax.numpy as jnp
from jax import lax
from jax.experimental import pallas as pl
from jax.experimental.pallas import tpu as pltpu
from jax.sharding import PartitionSpec as P

OMEGA = 0.8
COARSE_SWEEPS = 8
NLAT, NLON, BLOCK = 4, 64, 16
ROWS, COLS = 64, 512
H = 16
PAD = 8
PAD2 = 16
N0 = ROWS + 2 * H
WIDE = COLS + 128
ALL = range(5)
MID = range(1, 4)
MESH = pl.DeviceIdType.MESH
F32 = jnp.float32

HALO = ((1, 1), (1, -1), (-1, 1), (-1, -1), (1, 0), (-1, 0), (0, 1), (0, -1))
SPREAD_LAT = (1, 2, 3)
SPREAD_LON = (2, -2, 1, -1)
SPREAD = ((2, 2), (-2, 2), (1, 2), (-1, 2), (2, 1), (2, -1), (-2, 1), (-2, -1), (0, 2), (2, 0), (-2, 0))
SPREAD += ((1, 1), (1, -1), (-1, 1), (-1, -1), (0, 1), (0, -1), (1, 0), (-1, 0))
FAR1 = (8, 7, 9, 6, 10, 5, 11, 4, 12, 3, 13, 2, 14, 1, 15)
FAR2 = (10, 9, 11, 6, 14, 2, 8, 5, 7, 13, 15, 1, 3, 4, 12)


def lanes(shape):
    return lax.broadcasted_iota(jnp.int32, shape, len(shape) - 1)


def rows_of(shape):
    return lax.broadcasted_iota(jnp.int32, shape, 0)


def roll_l(x, by):
    return pltpu.roll(x, by % x.shape[1], 1)


def ld(ref, start, n, blocks=ALL, stride=None):
    rows = pl.ds(start, n) if stride is None else pl.ds(start, n, stride=stride)
    return jnp.concatenate([ref[j, rows, :] for j in blocks], axis=1)


def st(ref, start, x, blocks=ALL, stride=None):
    n = x.shape[0]
    rows = pl.ds(start, n) if stride is None else pl.ds(start, n, stride=stride)
    for i, j in enumerate(blocks):
        ref[j, rows, :] = x[:, 128 * i:128 * (i + 1)]


def loop(r0, count, ch, body):
    for k in range(count // ch):
        body(r0 + k * ch)


class Level:
    def __init__(self, s, pad, n, f, e, so, west, ae, aw, as_, an, w, wf, v, v2, q, r=None):
        self.s, self.pad, self.n = s, pad, n
        self.f, self.e, self.so, self.west = f, e, so, west
        self.ae, self.aw, self.as_, self.an, self.w, self.wf = ae, aw, as_, an, w, wf
        self.v, self.v2, self.q, self.r = v, v2, q, v2 if r is None else r


def coeffs(l, ch, keep=None, source=False, r0=0, count=None):
    def body(r):
        p = l.pad + r
        e, so, no = ld(l.e, p, ch), ld(l.so, p, ch), ld(l.so, p - 1, ch)
        we = roll_l(e, l.s)
        wk = OMEGA / (((e + we) + so) + no)
        if keep is not None:
            row = rows_of(wk.shape) + r
            wk = jnp.where((row >= keep[0]) & (row < keep[1]), wk, 0.0)
        st(l.west, p, we)
        st(l.ae, p, wk * e)
        st(l.aw, p, wk * we)
        st(l.as_, p, wk * so)
        st(l.an, p, wk * no)
        if source:
            st(l.wf, p, wk * ld(l.f, p, ch))
        else:
            st(l.w, p, wk)

    loop(r0, l.n if count is None else count, ch, body)


def sweep(l, src, dst, source, r0, count, ch, blocks=ALL):
    def body(r):
        p = l.pad + r
        v = ld(src, p, ch, blocks)
        x = ld(l.ae, p, ch, blocks) * roll_l(v, -l.s) + ld(l.aw, p, ch, blocks) * roll_l(v, l.s)
        y = ld(l.as_, p, ch, blocks) * ld(src, p + 1, ch, blocks) + ld(l.an, p, ch, blocks) * ld(src, p - 1, ch, blocks)
        z = (1.0 - OMEGA) * v
        if source:
            z = z + ld(l.wf, p, ch, blocks)
        st(dst, p, (y + z) + x, blocks)

    loop(r0, count, ch, body)


def operator(l, v, p, ch):
    x = ld(v, p, ch)
    lon = ld(l.e, p, ch) * (x - roll_l(x, -l.s)) + ld(l.west, p, ch) * (x - roll_l(x, l.s))
    lat = ld(l.so, p, ch) * (x - ld(v, p + 1, ch)) + ld(l.so, p - 1, ch) * (x - ld(v, p - 1, ch))
    return x, lat + lon


def remainder(l, ch, r0=0, count=None):
    def body(r):
        p = l.pad + r
        st(l.r, p, ld(l.f, p, ch) - operator(l, l.v, p, ch)[1])

    loop(r0, l.n if count is None else count, ch, body)


def pair(ref, start, n, odd, blocks=ALL):
    return ld(ref, start + odd, n, blocks, 2)


def restrict(l, c, a0=0, count=None):
    count = c.n if count is None else count
    ch = min(16, count)

    def body(a):
        x = pair(l.r, l.pad + 2 * a, ch, 0) + pair(l.r, l.pad + 2 * a, ch, 1)
        x = x + roll_l(x, -l.s)
        st(c.f, c.pad + a, x)
        st(c.wf, c.pad + a, x * ld(c.w, c.pad + a, ch))

    for a in range(a0, a0 + count, ch):
        body(a)


def coarsen(l, c, a0=0, count=None):
    count = c.n if count is None else count
    ch = min(16, count)
    for a in range(a0, a0 + count, ch):
        x = pair(l.e, l.pad + 2 * a, ch, 0) + pair(l.e, l.pad + 2 * a, ch, 1)
        st(c.e, c.pad + a, roll_l(x, -l.s))
        y = pair(l.so, l.pad + 2 * a, ch, 1)
        st(c.so, c.pad + a, y + roll_l(y, -l.s))


def spread_rows(v, start, e, add, blocks=ALL):
    for odd in (0, 1):
        x = e
        if add:
            x = x + ld(v, start + odd, e.shape[0], blocks, 2)
        st(v, start + odd, x, blocks, 2)


def prolong(c, l, src, dst, a0, n, add, blocks=ALL):
    for a in range(0, n, 8):
        e = ld(src, c.pad + a0 + a, 8, blocks)
        e = jnp.where((lanes(e.shape) & l.s) == 0, e, roll_l(e, l.s))
        spread_rows(dst, l.pad + 2 * (a0 + a), e, add, blocks)


def pick(x, index):
    return jnp.take_along_axis(x, index, axis=1, mode="promise_in_bounds")


def compact(x, offset):
    l = lanes((8, 128))
    index = (l % 32) * 4 + offset
    out = pick(x[:, 384:512], index)
    for j in (2, 1, 0):
        out = jnp.where(l < 32 * (j + 1), pick(x[:, 128 * j:128 * (j + 1)], index), out)
    return out


def expand(x, base):
    l = lanes((8, 128))
    q = l // 4
    own = x[2, pl.ds(base, 8), :]
    parts = [pick(own, q + 32 * j) for j in range(4)]
    east = pick(x[3, pl.ds(base, 8), :], q)
    west = pick(x[1, pl.ds(base, 8), :], q + 96)
    return jnp.concatenate(parts + [jnp.where(l < 64, east, west)], axis=1)


def kernel(
    b_in, e_in, s_in, sol, res,
    g, pk, re_, rw_, a0, ag, c, t1, got1, t2, got2, l6, far, half, halves,
    *rest,
):
    fine0, fine1, fine2, fine3, fine4, fine5 = rest[:9], rest[9:22], rest[22:32], rest[32:45], rest[45:58], rest[58:72]
    in_sem, a_send, a_recv, cs_send, cs_recv, fs_send, fs_recv, c1_send, c1_recv, c2_send, c2_recv = rest[72:]

    l0 = Level(1, PAD, N0, g.at[0], g.at[1], g.at[2], *fine0[:5], None, *fine0[5:])
    l1 = Level(2, PAD, N0 // 2, *fine1)
    l2 = Level(1, PAD2, 64, c.at[0], c.at[1], c.at[2], *fine2)
    l3 = Level(2, PAD, 32, *fine3)
    l4 = Level(4, PAD, 16, *fine4)
    l5 = Level(8, PAD, 8, *fine5)
    lat, lon = lax.axis_index("lat"), lax.axis_index("lon")

    def device(dlon, dlat):
        return {"lon": lax.rem(lon + dlon + NLON, NLON), "lat": lax.rem(lat + dlat + NLAT, NLAT)}

    block = (lon // BLOCK) * BLOCK
    inner = lax.rem(lon, BLOCK)

    def mate1(d):
        return {"lon": block + lax.rem(inner + d, BLOCK), "lat": lat}

    def mate2(d):
        return device(BLOCK * (d // 4), d % 4)

    top = PAD + H
    loads = [
        pltpu.make_async_copy(x.at[:, pl.ds(128 * j, 128)], g.at[i, j, pl.ds(top, ROWS)], in_sem.at[i, j])
        for i, x in enumerate((b_in, e_in, s_in))
        for j in range(4)
    ]
    barrier = pltpu.get_barrier_semaphore()
    greeted = [mate1(d) for d in FAR1] + [mate2(d) for d in FAR2 if d > 3]
    greeted += [device(*d) for d in SPREAD[:11] + HALO]
    for other in greeted:
        pl.semaphore_signal(barrier, inc=1, device_id=other, device_id_type=MESH)
    for copy in loads:
        copy.start()

    def clear(ref, l):
        zero = jnp.zeros((l.pad, WIDE), F32)
        st(ref, 0, zero)
        st(ref, l.pad + l.n, zero)

    for l in (l0, l1):
        for ref in (l.wf, l.v, l.v2, l.q):
            clear(ref, l)
    for l in (l2, l3, l4, l5):
        for ref in (l.wf, l.v, l.v2, l.q, l.so):
            clear(ref, l)
    for ref in (l2.ae, l2.aw, l2.as_, l2.an):
        clear(ref, l2)
    for ref in (l5.e, l5.r):
        clear(ref, l5)

    for copy in loads:
        copy.wait()

    l8 = lanes((8, 128))
    for k in range(ROWS // 8):
        rows = slice(top + 8 * k, top + 8 * k + 8)
        first = [g[i, 0, rows] for i in range(3)]
        last = [g[i, 3, rows] for i in range(3)]
        x = jnp.where(l8 < 16, first[0], jnp.where(l8 < 32, roll_l(first[1], 16), roll_l(first[2], 32)))
        y = jnp.where(l8 >= 112, last[0], jnp.where(l8 >= 96, roll_l(last[1], -16), roll_l(last[2], -32)))
        pk[8 * k:8 * k + 8] = jnp.where(l8 < 64, x, y)

    own_rows = pl.ds(pl.multiple_of(PAD2 + lat * 16, 16), 16)

    for a in range(0, 16, 8):
        x = ld(g.at[1], top + 4 * a, 8, range(4), 4)
        for j in (1, 2, 3):
            x = x + ld(g.at[1], top + 4 * a + j, 8, range(4), 4)
        y = ld(g.at[2], top + 4 * a + 3, 8, range(4), 4)
        y = y + roll_l(y, -1)
        y = y + roll_l(y, -2)
        rows = pl.ds(pl.multiple_of(PAD2 + lat * 16 + a, 8), 8)
        c[1, 2, rows, :] = compact(x, 3)
        c[2, 2, rows, :] = compact(y, 0)

    pl.semaphore_wait(barrier, len(greeted))

    def send(src, dst, s_sem, r_sem, k, to):
        copy = pltpu.make_async_remote_copy(
            src_ref=src, dst_ref=dst, send_sem=s_sem.at[k], recv_sem=r_sem.at[k], device_id=to, device_id_type=MESH
        )
        copy.start()
        return copy

    def spread_lat(index, s_sem, r_sem):
        part = c.at[index, 2, own_rows]
        return [send(part, part, s_sem, r_sem, k, device(0, d)) for k, d in enumerate(SPREAD_LAT)]

    def spread_lon(index, s_sem, r_sem):
        rows = pl.ds(PAD2, 64)
        return [
            send(c.at[index, 2, rows], c.at[index, 2 - d, rows], s_sem, r_sem, 3 + k, device(d, 0))
            for k, d in enumerate(SPREAD_LON)
        ]

    conds = spread_lat(pl.ds(1, 2), cs_send, cs_recv)
    halos = []
    for k, (dlon, dlat) in enumerate(HALO):
        first_row, count = {0: (0, ROWS), 1: (ROWS - H, H), -1: (0, H)}[dlat]
        to = {0: H, 1: 0, -1: H + ROWS}[dlat]
        if dlon == 0:
            first_row, to = (ROWS - 8, H - 8) if dlat == 1 else (0, H + ROWS)
            src = g.at[:, pl.ds(0, 4), pl.ds(top + first_row, 8)]
            dst = g.at[:, pl.ds(0, 4), pl.ds(PAD + to, 8)]
        else:
            src = pk.at[pl.ds(first_row, count)]
            dst = (rw_ if dlon == 1 else re_).at[pl.ds(to, count)]
        halos.append(send(src, dst, a_send, a_recv, k, device(dlon, dlat)))

    far_halos = [
        send(g.at[:, pl.ds(0, 4), pl.ds(top + first, 8)], far.at[i], a_send, a_recv, 8 + i, device(0, dlat))
        for i, (dlat, first) in enumerate(((1, ROWS - 16), (-1, 8)))
    ]


    for copy in conds:
        copy.wait_recv()
    conds_lon = spread_lon(pl.ds(1, 2), cs_send, cs_recv)

    for copy in halos:
        copy.wait_recv()

    has_north = jnp.where(lat > 0, 1.0, 0.0).astype(F32)
    used = (l8 < 16) | (l8 >= 112)
    for k in range(N0 // 8):
        x = jnp.where(l8 < 64, re_[8 * k:8 * k + 8], rw_[8 * k:8 * k + 8])
        for i, other in ((0, 0.0), (1, 1.0), (2, 1.0)):
            y = x if i == 0 else jnp.where(l8 < 64, roll_l(x, -16 * i), roll_l(x, 16 * i))
            g[i, 4, PAD + 8 * k:PAD + 8 * k + 8, :] = jnp.where(used, y, other)
    g[2, :, PAD + 8:PAD + H] = g[2, :, PAD + 8:PAD + H] * has_north

    def bounds(halo, own):
        return jnp.where(lat > 0, 0, halo), jnp.where(lat < NLAT - 1, 2 * halo + own, halo + own)

    coeffs(l0, 16, bounds(H, ROWS), True, 8, 80)
    sweep(l0, l0.wf, l0.v, True, 8, 80, 16)
    coarsen(l0, l1)
    remainder(l0, 16, 8, 80)
    coeffs(l1, 16, bounds(H // 2, ROWS // 2))
    restrict(l0, l1)
    sweep(l1, l1.wf, l1.v, True, 0, 48, 16)
    remainder(l1, 16)
    for a in range(0, 16, 8):
        x = ld(l1.r, PAD + 8 + 2 * a, 8, range(4), 2) + ld(l1.r, PAD + 9 + 2 * a, 8, range(4), 2)
        rows = pl.ds(pl.multiple_of(PAD2 + lat * 16 + a, 8), 8)
        c[0, 2, rows, :] = compact(x + roll_l(x, -2), 0)
    x = c[0, 2, pl.ds(pl.multiple_of(PAD2 + lat * 16, 8), 8), :]
    y = roll_l(c[0, 2, pl.ds(pl.multiple_of(PAD2 + lat * 16 + 8, 8), 8), :], 64)
    half[0] = jnp.where(l8 >= 64, x, y)
    half[1] = jnp.where(l8 < 64, x, y)
    fields = []
    for k, d in enumerate(SPREAD):
        if abs(d[0]) == 2:
            side = 0 if d[0] == 2 else 1
            fields.append(send(half.at[side], halves.at[side, lat], fs_send, fs_recv, k, device(*d)))
        else:
            part = c.at[0, 2, own_rows]
            fields.append(send(part, c.at[0, 2 - d[0], own_rows], fs_send, fs_recv, k, device(*d)))

    for i, first in enumerate((PAD, PAD + N0 - 8)):
        far_halos[i].wait_recv()
        for k in range(3):
            for j in range(4):
                g[k, j, first:first + 8] = far[i, k, j]
    g[2, :, PAD:PAD + 8] = g[2, :, PAD:PAD + 8] * has_north
    for r0 in (0, N0 - 16):
        coeffs(l0, 16, bounds(H, ROWS), True, r0, 16)
    for r0 in (0, N0 - 16):
        sweep(l0, l0.wf, l0.v, True, r0, 16, 16)
        coarsen(l0, l1, r0 // 2, 8)
    for r0 in (0, N0 - 16):
        remainder(l0, 16, r0, 16)
        coeffs(l1, 8, bounds(H // 2, ROWS // 2), False, r0 // 2, 8)
    for r0 in (0, N0 - 16):
        restrict(l0, l1, r0 // 2, 8)
    for r0 in (0, N0 // 2 - 8):
        sweep(l1, l1.wf, l1.v, True, r0, 8, 8)

    for copy in conds_lon:
        copy.wait_recv()
    coeffs(l2, 16)
    coarsen(l2, l3)
    coeffs(l3, 16)
    coarsen(l3, l4)
    coeffs(l4, 16)
    coarsen(l4, l5)
    coeffs(l5, 8)


    def twice(l, v, source, r0, count, ch, blocks=ALL):
        sweep(l, v, l.v2, source, r0, count, ch, blocks)
        sweep(l, l.v2, v, source, r0, count, ch, blocks)

    def rise_coarse(name, source):
        u = [getattr(l, name) for l in (l0, l1, l2, l3, l4, l5)]
        twice(l5, u[5], source, 0, 8, 8, MID)
        prolong(l5, l4, u[5], u[4], 0, 8, source, MID)
        twice(l4, u[4], source, 0, 16, 16, MID)
        prolong(l4, l3, u[4], u[3], 0, 16, source, MID)
        twice(l3, u[3], source, 0, 32, 16, MID)
        near = lat * 8 - 4
        prolong(l3, l2, u[3], u[2], near, 16, source, MID)
        near = pl.multiple_of(lat * 16 - 8, 8)
        twice(l2, u[2], source, near, 32, 16, MID)

    def rise_fine(name, source):
        u = [getattr(l, name) for l in (l0, l1, l2)]
        for i in range(3):
            e = expand(u[2], PAD2 + lat * 16 - 4 + 8 * i)
            spread_rows(u[1], PAD + 16 * i, e, source)
        twice(l1, u[1], source, 0, 48, 16)
        prolong(l1, l0, u[1], u[0], 0, 48, source)
        twice(l0, u[0], source, 8, 80, 16)

    def applied(v, out, sums, n):
        def body(r, carry):
            x, av = operator(l0, v, top + r, 16)
            x, av = x[:, :COLS], av[:, :COLS]
            out[pl.ds(r, 16)] = av
            more = sums(pl.ds(r, 16), ld(l0.f, top + r, 16, range(4)), x, av)
            return tuple(y + (z[:8] + z[8:]) for y, z in zip(carry, more))

        carry = (jnp.zeros((8, COLS), F32),) * n
        for r in range(0, ROWS, 16):
            carry = body(r, carry)
        return carry

    x = pair(l5.e, PAD, 8, 0) + pair(l5.e, PAD, 8, 1)
    e6 = roll_l(x, -8)
    x = pair(l5.so, PAD, 8, 1)
    s6 = x + roll_l(x, -8)
    row6, lane6 = rows_of((8, WIDE)), lanes((8, WIDE))
    west6 = roll_l(e6, 16)
    north6 = jnp.where(row6 == 0, 0.0, pltpu.roll(s6, 1, 0))
    w6 = jnp.where(row6 < 4, OMEGA / (((e6 + west6) + s6) + north6), 0.0)
    for i, x in enumerate((e6, west6, s6, north6, w6, w6 * e6, w6 * west6, w6 * s6, w6 * north6)):
        st(l6, 8 * i, x)

    st(l5.q, PAD, jnp.ones((8, WIDE), F32))
    rise_coarse("q", False)
    for copy in halos + far_halos + conds:
        copy.wait_send()
    rise_fine("q", False)
    for copy in fields + conds_lon:
        copy.wait_send()
    sums_q = applied(l0.q, ag, lambda rows, b, v, av: (b * v, v * av), 2)

    for copy in fields:
        copy.wait_recv()

    for i in range(4):
        for side, slot in ((0, 0), (1, 4)):
            x = halves[side, i]
            c[0, slot, PAD2 + 16 * i:PAD2 + 16 * i + 8, :] = x
            c[0, slot, PAD2 + 16 * i + 8:PAD2 + 16 * i + 16, :] = roll_l(x, 64)

    def first(r):
        st(l2.wf, PAD2 + r, ld(l2.w, PAD2 + r, 16) * ld(l2.f, PAD2 + r, 16))

    loop(0, 64, 16, first)
    sweep(l2, l2.wf, l2.v, True, 0, 64, 16)
    remainder(l2, 16)
    for l, coarse in ((l2, l3), (l3, l4), (l4, l5)):
        restrict(l, coarse)
        sweep(coarse, coarse.wf, coarse.v, True, 0, coarse.n, min(16, coarse.n))
        remainder(coarse, min(16, coarse.n))

    x = pair(l5.r, PAD, 8, 0) + pair(l5.r, PAD, 8, 1)
    f6 = x + roll_l(x, -8)
    e6, west6, s6, north6, w6, ae6, aw6, as6, an6 = [ld(l6, 8 * i, 8) for i in range(9)]
    wf6 = w6 * f6
    field = wf6
    for _ in range(COARSE_SWEEPS - 1):
        x = ae6 * roll_l(field, -16) + aw6 * roll_l(field, 16)
        y = as6 * pltpu.roll(field, 7, 0) + an6 * pltpu.roll(field, 1, 0)
        field = (((1.0 - OMEGA) * field + wf6) + y) + x
    lon6 = e6 * (field - roll_l(field, -16)) + west6 * (field - roll_l(field, 16))
    lat6 = s6 * (field - pltpu.roll(field, 7, 0)) + north6 * (field - pltpu.roll(field, 1, 0))
    left = f6 - (lon6 + lat6)
    mine = ((lane6 & 15) == 0) & (lane6 >= 256) & (lane6 < 384)
    left = jnp.where(mine & (row6 == lat), left, 0.0)[:, 256:384]
    last = jnp.where(mine & (row6 == 3) & (lat == 3), s6, 0.0)[:, 256:384]

    e = jnp.where((lane6 & 8) == 0, field, roll_l(field, 8))
    for odd in (0, 1):
        st(l5.r, odd, e, ALL, 2)
    st(l5.v, PAD, ld(l5.v, PAD, 8) + ld(l5.r, 0, 8))
    rise_coarse("v", True)
    rise_fine("v", True)
    sums_v = applied(l0.v, a0, lambda rows, b, v, av: (b * v, v * av, v * ag[rows]), 3)

    def wait_all(got, sem):
        pltpu.make_async_copy(got, got, sem.at[0]).wait()

    def fold(x):
        return (x[:, 0:128] + x[:, 128:256]) + (x[:, 256:384] + x[:, 384:512])

    seven = [left, last, fold(sums_v[0]), fold(sums_q[0]), fold(sums_v[1]), fold(sums_v[2]), fold(sums_q[1])]
    row = rows_of((8, 128))
    total = jnp.zeros((8, 128), F32)
    for i, x in enumerate(seven):
        total = jnp.where(row == i, jnp.sum(x, axis=0, keepdims=True), total)
    t1[...] = total
    for d in FAR1:
        send(t1, got1.at[d - 1], c1_send, c1_recv, 0, mate1(d))
    wait_all(got1, c1_recv)

    def gathered(total, got):
        parts = [total] + [got[d] for d in range(15)]
        while len(parts) > 1:
            parts = [x + y for x, y in zip(parts[::2], parts[1::2])]
        return parts[0]

    total = gathered(total, got1)
    t2[...] = total
    for d in FAR2:
        send(t2, got2.at[d - 1], c2_send, c2_recv, 0, mate2(d))
    wait_all(got1, c1_send)
    wait_all(got2, c2_recv)
    total = gathered(total, got2)
    for by in (64, 32, 16, 8, 4, 2, 1):
        total = total + pltpu.roll(total, by, 1)
    n_left, n_last, bv, bq, vav, vaq, qaq = [total[i:i + 1] for i in range(7)]
    const = n_left / n_last
    step = (bv + const * bq) / ((vav + (2.0 * const) * vaq) + (const * const) * qaq)
    both = jnp.concatenate([step * const] * 4, axis=1)
    step = jnp.concatenate([step] * 4, axis=1)

    for r in range(0, ROWS, 16):
        rows = pl.ds(r, 16)
        sol[rows] = step * ld(l0.v, top + r, 16, range(4)) + both * ld(l0.q, top + r, 16, range(4))
        res[rows] = ld(l0.f, top + r, 16, range(4)) - (step * a0[rows] + both * ag[rows])
    wait_all(got2, c2_send)


def body(guidance, cond_lon, cond_lat):
    def vm(*shape):
        return pltpu.VMEM(shape, F32)

    def wide(n, count):
        return [vm(5, n, 128)] * count

    dma = pltpu.SemaphoreType.DMA
    scratch = [vm(3, 5, N0 + 2 * PAD, 128), vm(ROWS, 128), vm(N0, 128), vm(N0, 128), vm(ROWS, COLS), vm(ROWS, COLS)]
    scratch += [vm(3, 5, 64 + 2 * PAD2, 128), vm(8, 128), vm(15, 8, 128), vm(8, 128), vm(15, 8, 128), vm(5, 72, 128), vm(2, 3, 4, 8, 128), vm(2, 8, 128), vm(2, 4, 8, 128)]
    scratch += wide(N0 + 2 * PAD, 9) + wide(N0 // 2 + 2 * PAD, 13) + wide(64 + 2 * PAD2, 10)
    scratch += wide(32 + 2 * PAD, 13) + wide(16 + 2 * PAD, 13) + wide(8 + 2 * PAD, 14)
    scratch += [dma((3, 4)), dma((10,)), dma((10,)), dma((7,)), dma((7,)), dma((19,)), dma((19,))] + [dma((1,))] * 4
    return pl.pallas_call(
        kernel,
        out_shape=(pltpu.VMEM((ROWS, COLS), F32),) * 2,
        in_specs=[pl.BlockSpec(memory_space=pltpu.HBM)] * 3,
        out_specs=(pl.BlockSpec(memory_space=pltpu.VMEM),) * 2,
        scratch_shapes=scratch,
        compiler_params=pltpu.CompilerParams(
            collective_id=0, has_side_effects=True, vmem_limit_bytes=60 * 1024 * 1024
        ),
        cost_estimate=pl.CostEstimate(flops=10_000_000, bytes_accessed=655360, transcendentals=0),
    )(guidance, cond_lon, cond_lat)


def solution(mesh):
    spec = P("lat", "lon")
    return jax.shard_map(body, mesh=mesh, in_specs=(spec,) * 3, out_specs=(spec,) * 2, check_vma=False)
```
